32 devices in a mesh: dp: 8 (over z, x), seq: 4 (over y, core).
Axes of the slice: x: 2, y: 2, z: 4, core: 2. Of those that a mesh axis runs over, the one named last changes fastest.
Arguments:
- tokens: bfloat16 [512, 64, 512], P('seq', 'dp')
- segments: int32 [512, 64], P(None, 'dp'), may hold values from 0 to 4, as said below
- projections: bfloat16 [512, 3, 512], replicated, may hold values from -0.25 to 0.25
- projbias: bfloat16 [2, 512], replicated, may hold values from -1.25 to 1.25
- outweight: bfloat16 [512, 512], replicated, may hold values from -1.5 to 1.5
- outbias: bfloat16 [512], replicated, may hold values from -1.75 to 1.75
- normgain: bfloat16 [512], replicated, may hold values from 0.25 to 1.75
- normshift: bfloat16 [512], replicated, may hold values from -1.75 to 1.75
- expander: bfloat16 [2048, 512], replicated, may hold values from -0.25 to 0.25
- expandbias: bfloat16 [2048], replicated, may hold values from -3 to 3
- shrinker: bfloat16 [2048, 512], replicated, may hold values from -0.125 to 0.125
- shrinkbias: bfloat16 [512], replicated, may hold values from -1.75 to 1.75
- finalgain: bfloat16 [512], replicated, may hold values from 0.25 to 1.75
- finalshift: bfloat16 [512], replicated, may hold values from -1.75 to 1.75
- cotangent: bfloat16 [512, 64, 512], P('seq', 'dp'), may hold values from -6 to 6
Outputs:
- result: bfloat16 [512, 64, 512], P('seq', 'dp')
- tokens_grad: bfloat16 [512, 64, 512], P('seq', 'dp')
- projections_grad: float32 [512, 3, 512], replicated
- projbias_grad: float32 [2, 512], replicated
- outweight_grad: float32 [512, 512], replicated
- outbias_grad: float32 [512], replicated
- normgain_grad: float32 [512], replicated
- normshift_grad: float32 [512], replicated
- expander_grad: float32 [2048, 512], replicated
- expandbias_grad: float32 [2048], replicated
- shrinker_grad: float32 [2048, 512], replicated
- shrinkbias_grad: float32 [512], replicated
- finalgain_grad: float32 [512], replicated
- finalshift_grad: float32 [512], replicated
- rms_values: float32 [3], replicated
The draws below stay inside these ranges and needn't reach their ends.
Inputs may be any that keep to these rules, and one draw needn't show every extreme that they name: `segments`: each row holds four documents with ids 1, 2, 3, 4 in this order, then a run of padding (id 0) at its end, possibly empty and shorter than 64 positions. With q = 112, document j + 1 begins at a position from (j - 1) * q + 1 to j * q - 1, for j = 1, 2, 3.
All inputs are finite; a program needn't handle non-finite values.
Results may differ from the reference program's by a relative error of at most 0.013.
Values may be sent and summed in bfloat16 or wider, within the bound.
A program may use at most 128 MiB of HBM per device.

```python
import jax
import jax.numpy as jnp
from jax import lax

D = 512
HEADS = 8
HEAD_DIM = 64
FF = 2048
LEN = 512
ROWS_DEV = 2
ROWS = 64
N_SEQ = 4


def draw_tokens(key, part):
    key = jax.random.fold_in(key, 5)
    rise = jnp.arange(ROWS, dtype=jnp.float32) / max(ROWS - 1, 1) - 0.5
    base = jax.random.normal(key, (LEN, ROWS, D), jnp.float32)
    scale = jnp.exp(0.5493061 * rise)
    return (base * scale[None, :, None]).astype(jnp.bfloat16)


def draw_segments(key, part):
    key = jax.random.fold_in(key, 9)
    first, second = jax.random.split(key)
    padding = jax.random.randint(first, (ROWS,), 0, LEN // 8)
    quarter = (LEN - LEN // 8) // 4
    offsets = jax.random.randint(second, (3, ROWS), 1, quarter)
    bounds = offsets + quarter * jnp.arange(3, dtype=jnp.int32)[:, None]
    position = jnp.arange(LEN, dtype=jnp.int32)[:, None]
    passed = jnp.zeros((LEN, ROWS), jnp.int32)
    for index in range(3):
        passed = passed + (position >= bounds[index][None, :]).astype(jnp.int32)
    return jnp.where(position < LEN - padding[None, :], 1 + passed, 0).astype(jnp.int32)


def levels(own_key, shape, cuts, least, top_value):
    loudness, own = 1.0, jax.random.fold_in(own_key, 6)
    for dim, shards_of in cuts:
        draws = jnp.exp(jax.random.uniform(jax.random.fold_in(own, dim), (shards_of,), jnp.float32, least / len(cuts), top_value / len(cuts)))
        loudness = loudness * jnp.repeat(draws, shape[dim] // shards_of).reshape([-1 if axis == dim else 1 for axis in range(len(shape))])
    return loudness


def gaussian(key, shape, deviation, bound, cuts=(), kind=jnp.bfloat16):
    drawn = jax.random.normal(key, shape, jnp.float32) * deviation
    if len(cuts) > 0:
        drawn = levels(key, shape, cuts, -0.22, 0.18) * drawn
    return jnp.clip(drawn, min=-bound, max=bound).astype(kind)


def setup_inputs(seed: int = 0) -> dict:
    arg_keys = jax.random.split(jax.random.key(seed), 16)
    tokens = draw_tokens(jax.random.fold_in(arg_keys[15], 71), 0)
    segments = draw_segments(jax.random.fold_in(arg_keys[15], 71), 0)
    projections = gaussian(arg_keys[2], (D, 3, D), D ** -0.5, 0.25)
    projbias = gaussian(arg_keys[3], (2, D), 0.2, 1.25)
    outweight = gaussian(arg_keys[4], (D, D), (max(D // 32, 2)) ** -0.5, 1.5)
    outbias = gaussian(arg_keys[5], (D,), 0.3, 1.75)
    normgain = jnp.clip(1.0 + 0.15 * jax.random.normal(arg_keys[6], (D,), jnp.float32), 0.25, 1.75).astype(jnp.bfloat16)
    normshift = gaussian(arg_keys[7], (D,), 0.3, 1.75)
    expander = gaussian(arg_keys[8], (FF, D), D ** -0.5, 0.25)
    expandbias = gaussian(arg_keys[9], (FF,), 0.5, 3.0)
    shrinker = gaussian(arg_keys[10], (FF, D), FF ** -0.5, 0.125)
    shrinkbias = gaussian(arg_keys[11], (D,), 0.3, 1.75)
    finalgain = jnp.clip(1.0 + 0.15 * jax.random.normal(arg_keys[12], (D,), jnp.float32), 0.25, 1.75).astype(jnp.bfloat16)
    finalshift = gaussian(arg_keys[13], (D,), 0.3, 1.75)
    cotangent = gaussian(arg_keys[14], (LEN, ROWS, D), 1.0, 6.0, ((0, 4), (1, 8)))
    return dict(tokens=tokens, segments=segments, projections=projections, projbias=projbias, outweight=outweight, outbias=outbias, normgain=normgain, normshift=normshift, expander=expander, expandbias=expandbias, shrinker=shrinker, shrinkbias=shrinkbias, finalgain=finalgain, finalshift=finalshift, cotangent=cotangent)


@jax.custom_vjp
def low(v):
    return lax.optimization_barrier(v.astype(jnp.bfloat16)).astype(jnp.float32)

@jax.custom_vjp
def low_back(v):
    return v

def low_keep(v):
    return (low(v), None)

def low_pass(kept, grad):
    return (grad,)

def back_keep(v):
    return (v, None)

def back_low(kept, grad):
    return (low(grad),)
low.defvjp(low_keep, low_pass)
low_back.defvjp(back_keep, back_low)
HIGH = lax.Precision.HIGHEST
EPSILON = 1e-12

def normalize(value, gain, shift):
    center = value - lax.optimization_barrier(jnp.mean(value, axis=-1, keepdims=True))
    spread = lax.optimization_barrier(jnp.mean(center * center, axis=-1, keepdims=True))
    return center * lax.rsqrt(spread + EPSILON) * gain + shift

def attend_row(packed):
    query, keys, values, labels = packed
    scores = jnp.einsum('phe,khe->hpk', query, keys, precision=HIGH) * HEAD_DIM ** (-0.5)
    scores = low_back(scores)
    same = labels[:, None] == labels[None, :]
    masked = jnp.where(same[None], scores, -1e+30)
    top = lax.optimization_barrier(jnp.max(masked, axis=-1, keepdims=True))
    raised = jnp.exp(masked - top)
    probs = raised / lax.optimization_barrier(jnp.sum(raised, axis=-1, keepdims=True))
    return jnp.einsum('hpk,khe->phe', low(probs), values, precision=HIGH)

def forward(block, params, labels):
    projections, projbias, outweight, outbias, normgain, normshift, expander, expandbias, shrinker, shrinkbias, finalgain, finalshift = params
    span = block.shape[1]
    bias = jnp.stack([projbias[0], jnp.zeros_like(projbias[0]), projbias[1]])
    mixed = jnp.einsum('prd,dkc->prkc', block, projections, precision=HIGH) + bias
    mixed = low_back(low(mixed))
    split = jnp.moveaxis(mixed.reshape(LEN, span, 3, HEADS, HEAD_DIM), 1, 0)
    context = lax.map(jax.checkpoint(attend_row), (split[:, :, 0], split[:, :, 1], split[:, :, 2], jnp.moveaxis(labels, 1, 0)))
    context = low_back(low(context.reshape(span, LEN, D)))
    attended = low_back(jnp.einsum('rpc,cd->prd', context, outweight, precision=HIGH) + outbias)
    hidden = normalize(block + attended, normgain, normshift)
    upper = low_back(jnp.einsum('prd,fd->prf', low(hidden), expander, precision=HIGH) + expandbias)
    active = low(jax.nn.gelu(upper, approximate=False))
    shrunk = low_back(jnp.einsum('prf,fd->prd', active, shrinker, precision=HIGH) + shrinkbias)
    result = normalize(hidden + shrunk, finalgain, finalshift)
    return (result, (attended, shrunk))

def reference(tokens, segments, projections, projbias, outweight, outbias, normgain, normshift, expander, expandbias, shrinker, shrinkbias, finalgain, finalshift, cotangent):
    params = tuple((item.astype(jnp.float32) for item in (projections, projbias, outweight, outbias, normgain, normshift, expander, expandbias, shrinker, shrinkbias, finalgain, finalshift)))
    span = ROWS_DEV * N_SEQ
    groups = ROWS // span

    def group_step(carry, index):
        totals, sums, count = carry
        start = index * span
        block = lax.dynamic_slice_in_dim(tokens, start, span, 1).astype(jnp.float32)
        labels = lax.dynamic_slice_in_dim(segments, start, span, 1)
        upstream = lax.dynamic_slice_in_dim(cotangent, start, span, 1).astype(jnp.float32)

        def run_block(block_in, weights):
            return forward(block_in, weights, labels)
        result, pullback, branches = jax.vjp(run_block, block, params, has_aux=True)
        block_grad, param_grads = pullback(upstream)
        valid = (labels != 0).astype(jnp.float32)[:, :, None]
        pieces = jnp.stack([jnp.sum(valid * block * block), jnp.sum(valid * branches[0] * branches[0]), jnp.sum(valid * branches[1] * branches[1])])
        totals = jax.tree.map(jnp.add, totals, param_grads)
        return ((totals, sums + pieces, count + jnp.sum(valid)), (result.astype(jnp.bfloat16), block_grad.astype(jnp.bfloat16)))
    zeros = tuple((jnp.zeros_like(item) for item in params))
    start_carry = (zeros, jnp.zeros((3,), jnp.float32), jnp.zeros((), jnp.float32))
    (totals, sums, count), (results, grads) = lax.scan(group_step, start_carry, jnp.arange(groups, dtype=jnp.int32))
    result = jnp.moveaxis(results, 0, 1).reshape(LEN, ROWS, D)
    tokens_grad = jnp.moveaxis(grads, 0, 1).reshape(LEN, ROWS, D)
    rms_values = jnp.sqrt(sums / (count * D))
    return (result, tokens_grad, totals[0], totals[1], totals[2], totals[3], totals[4], totals[5], totals[6], totals[7], totals[8], totals[9], totals[10], totals[11], rms_values)
```

```python
import jax
import jax.numpy as jnp
from jax import lax
from jax.experimental import pallas as pl
from jax.experimental.pallas import tpu as pltpu
from jax.sharding import PartitionSpec as P

HEAD_DIM = 64
EPSILON = 1e-12
LANES = 128
F32 = jnp.float32
BF16 = jnp.bfloat16
SCALE = HEAD_DIM ** (-0.5)

(V_QUERY, V_VALUE, V_OUT, V_GAIN1, V_SHIFT1, V_SHRINK, V_GAIN2, V_SHIFT2, V_EXPAND) = range(9)
(S_INPUT, S_ATTENDED, S_SHRUNK, S_COUNT) = range(4)


def nn(a, b):
    return lax.dot_general(a, b, (((1,), (0,)), ((), ())), preferred_element_type=F32)


def nt(a, b):
    return lax.dot_general(a, b, (((1,), (1,)), ((), ())), preferred_element_type=F32)


def tn(a, b):
    return lax.dot_general(a, b, (((0,), (0,)), ((), ())), preferred_element_type=F32)


def gelu_parts(u):
    z = jnp.abs(u)
    d = 1.0 + (0.3275911 * 0.5**0.5) * z
    t = pl.reciprocal(d, approx=True)
    t = t * (2.0 - d * t)
    e = jnp.exp(-0.5 * u * u)
    poly = 0.5 * 1.061405429
    poly = poly * t - 0.5 * 1.453152027
    poly = poly * t + 0.5 * 1.421413741
    poly = poly * t - 0.5 * 0.284496736
    poly = poly * t + 0.5 * 0.254829592
    tail = poly * t * e
    phi = jnp.where(u >= 0.0, 1.0 - tail, tail)
    return u * phi, phi + (0.3989422804014327 * u) * e


def levels_of(n_seq, n_dp):
    low = 2 if n_seq % 2 == 0 else 1
    near = 1
    while 4 * near * near <= n_dp and n_dp % (2 * near) == 0:
        near *= 2
    return {
        "core": ("seq", 1, low),
        "side": ("seq", low, n_seq // low),
        "near": ("dp", 1, near),
        "far": ("dp", near, n_dp // near),
    }


def slots_of(levels, order, rows):
    total = 0
    for name in order:
        size = levels[name][2]
        if size == 1:
            continue
        if rows % (16 * size) == 0:
            rows //= size
            total += (size - 1) * rows
        else:
            total += size * rows
    return total


def local(
    tokens,
    segments,
    projections,
    projbias,
    outweight,
    outbias,
    normgain,
    normshift,
    expander,
    expandbias,
    shrinker,
    shrinkbias,
    finalgain,
    finalshift,
    cotangent,
):
    n_seq, n_dp = lax.axis_size("seq"), lax.axis_size("dp")
    span, group, width = tokens.shape
    length = segments.shape[0]
    rows = group // n_seq
    hidden_units = expander.shape[0]
    blocks = hidden_units // width
    heads = width // HEAD_DIM
    pairs = width // LANES
    own_tokens = rows * length
    levels = levels_of(n_seq, n_dp)
    orders = (("core", "side", "near", "far"), ("core", "near", "side", "far"))
    chunks = [(2 * width * c, 2 * width) for c in range(blocks)]
    chunks.append((2 * width * blocks, width))
    chunks.append((2 * width * blocks + width, 3 * width))
    grad_rows = 2 * width * blocks + 4 * width
    slot_bases, slot_rows = [], 0
    for index, (_, count) in enumerate(chunks):
        slot_bases.append(slot_rows)
        slot_rows += slots_of(levels, orders[index % 2], count)
    vec_rows = V_EXPAND + blocks
    sum_rows = -(-(vec_rows + 4) // 8) * 8
    sums_at = vec_rows
    ring = sum(size - 1 for _, _, size in levels.values())
    n_remote = 4 * rows * (n_seq - 1) + len(chunks) * 2 * ring + ring
    n_local = 8 + 4 * rows + len(chunks)

    vectors = jnp.concatenate(
        [
            projbias,
            jnp.stack([outbias, normgain, normshift, shrinkbias, finalgain, finalshift]),
            expandbias.reshape(blocks, width),
        ]
    ).astype(F32)

    def kernel(
        tok_hbm,
        cot_hbm,
        labels,
        proj_hbm,
        out_hbm,
        exp_hbm,
        shr_hbm,
        vec,
        result_hbm,
        tgrad_hbm,
        grads_hbm,
        sums_out,
        x,
        cot,
        proj,
        outw,
        expw,
        shrw,
        mixed,
        probs,
        context,
        inverse,
        vhat1,
        rstd1,
        low1,
        active,
        slope,
        second,
        shrunk_low,
        attended_low,
        context_grad,
        result,
        valid,
        qfeat,
        kfeat,
        grads,
        slots,
        sums,
        sum_slots,
        send_sem,
        recv_sem,
        local_sem,
    ):
        me = lax.axis_index("seq")
        started, counters = [], {"remote": 0, "local": 0}

        def remote(src, dst, where):
            i = counters["remote"]
            counters["remote"] += 1
            copy = pltpu.make_async_remote_copy(
                src_ref=src,
                dst_ref=dst,
                send_sem=send_sem.at[i],
                recv_sem=recv_sem.at[i],
                device_id=where,
                device_id_type=pl.DeviceIdType.MESH,
            )
            copy.start()
            started.append(copy)
            return copy

        def near_copy(src, dst):
            i = counters["local"]
            counters["local"] += 1
            copy = pltpu.make_async_copy(src, dst, local_sem.at[i])
            copy.start()
            return copy

        def place(name):
            axis, stride, size = levels[name]
            index = lax.axis_index(axis)
            mine = lax.rem(lax.div(index, stride), size)
            return axis, index, stride, size, mine

        barrier = pltpu.get_barrier_semaphore()
        greeted = 0
        for j in range(1, n_seq):
            pl.semaphore_signal(
                barrier,
                inc=1,
                device_id={"seq": lax.rem(me + j, n_seq)},
                device_id_type=pl.DeviceIdType.MESH,
            )
            greeted += 1
        for name in ("near", "far"):
            axis, index, stride, size, mine = place(name)
            for j in range(1, size):
                k = lax.rem(mine + j, size)
                pl.semaphore_signal(
                    barrier,
                    inc=1,
                    device_id={axis: index + (k - mine) * stride},
                    device_id_type=pl.DeviceIdType.MESH,
                )
                greeted += 1

        def bring(src, dst, r):
            here = pl.ds(pl.multiple_of(r * length + me * span, 16), span)
            copies = [near_copy(src.at[me * rows + r], dst.at[here])]
            far = []
            for j in range(1, n_seq):
                k = lax.rem(me + j, n_seq)
                far.append(remote(src.at[k * rows + r], dst.at[here], {"seq": k}))
            return copies, far

        def deliver(src, dst, r):
            copies, far = [], []
            for j in range(n_seq):
                k = lax.rem(me + j, n_seq)
                piece = src.at[pl.ds(pl.multiple_of(r * length + k * span, 16), span)]
                if j == 0:
                    copies.append(near_copy(piece, dst.at[me * rows + r]))
                else:
                    far.append(remote(piece, dst.at[me * rows + r], {"seq": k}))
            return copies, far

        def arrive(pack):
            for copy in pack[0]:
                copy.wait()
            for copy in pack[1]:
                copy.wait_recv()

        def reduce_chunk(index):
            base, count = chunks[index]
            written = []
            at, slot, stack = base, slot_bases[index], []
            for name in orders[index % 2]:
                axis, own, stride, size, mine = place(name)
                if size == 1:
                    continue
                copies = []
                if count % (16 * size) == 0:
                    piece = count // size
                    for j in range(1, size):
                        k = lax.rem(mine + j, size)
                        copies.append(
                            remote(
                                grads.at[pl.ds(pl.multiple_of(at + k * piece, 16), piece)],
                                slots.at[pl.ds(slot + (j - 1) * piece, piece)],
                                {axis: own + (k - mine) * stride},
                            )
                        )
                    yield
                    here = pl.multiple_of(at + mine * piece, 16)
                    for copy in copies:
                        copy.wait_recv()
                    total = grads[pl.ds(here, piece)].astype(F32)
                    for j in range(size - 1):
                        total = total + slots[pl.ds(slot + j * piece, piece)].astype(F32)
                    grads[pl.ds(here, piece)] = total.astype(BF16)
                    stack.append((name, at, piece))
                    slot += (size - 1) * piece
                    at, count = here, piece
                else:
                    mine_slot = pl.ds(pl.multiple_of(slot + mine * count, 16), count)
                    slots[mine_slot] = grads[pl.ds(at, count)]
                    for j in range(1, size):
                        k = lax.rem(mine + j, size)
                        copies.append(
                            remote(
                                slots.at[mine_slot],
                                slots.at[mine_slot],
                                {axis: own + (k - mine) * stride},
                            )
                        )
                    yield
                    for copy in copies:
                        copy.wait_recv()
                    total = jnp.zeros((count, width), F32)
                    for j in range(size):
                        total = total + slots[pl.ds(slot + j * count, count)].astype(F32)
                    grads[pl.ds(at, count)] = total.astype(BF16)
                    slot += size * count
            block, copies = grads.at[pl.ds(at, count)], []
            written.append(near_copy(block, grads_hbm.at[pl.ds(at, count)]))
            for name, before, piece in reversed(stack):
                axis, own, stride, size, mine = place(name)
                target = grads_hbm.at[pl.ds(at, piece)]
                copies = []
                for j in range(1, size):
                    k = lax.rem(mine + j, size)
                    copies.append(remote(block, target, {axis: own + (k - mine) * stride}))
                yield
                for copy in copies:
                    copy.wait_recv()
                if written:
                    written.pop().wait()
                count = piece * size
                at, block = before, grads_hbm.at[pl.ds(before, count)]
            if written:
                written.pop().wait()

        def reduce_sums():
            current = sums
            for step, name in enumerate(("core", "side", "near", "far")):
                axis, own, stride, size, mine = place(name)
                if size == 1:
                    continue
                first = sum(levels[n][2] for n in ("core", "side", "near", "far")[:step])
                sum_slots[first + mine] = current[...]
                copies = []
                for j in range(1, size):
                    k = lax.rem(mine + j, size)
                    block = sum_slots.at[first + mine]
                    copies.append(remote(block, block, {axis: own + (k - mine) * stride}))
                yield
                for copy in copies:
                    copy.wait_recv()
                total = sum_slots[first]
                for j in range(1, size):
                    total = total + sum_slots[first + j]
                current[...] = total
            sums_out[...] = current[...]

        running = []

        def turn(limit=99):
            for reduction in list(running)[:limit]:
                if next(reduction, "end") == "end":
                    running.remove(reduction)

        def begin(reduction):
            next(reduction)
            running.append(reduction)

        def add(row, value):
            sums[row : row + 1, :] += jnp.sum(value, axis=0, keepdims=True)

        def vrow(i):
            return vec[i : i + 1, :]

        weights = [
            near_copy(proj_hbm, proj),
            near_copy(out_hbm, outw),
            near_copy(exp_hbm, expw),
            near_copy(shr_hbm, shrw),
        ]
        pl.semaphore_wait(barrier, greeted)
        incoming = [bring(tok_hbm, x, 0)]
        sums[...] = jnp.zeros_like(sums)
        for copy in weights:
            copy.wait()

        lane = lax.broadcasted_iota(jnp.int32, (length, LANES), 1)
        first_head = lane < HEAD_DIM
        lane_row = lax.broadcasted_iota(jnp.int32, (1, LANES), 1)
        masks = [
            jnp.where(lane_row // HEAD_DIM == part, 1.0, 0.0).astype(BF16) for part in (0, 1)
        ]
        scaled = [mask * BF16(SCALE) for mask in masks]

        def features(r):
            here = pl.ds(r * length, length)
            label = labels[pl.ds(me * rows + r, 1), :]
            ids = lax.broadcasted_iota(jnp.int32, (LANES, length), 0)
            hot = jnp.where(ids == label, 1.0, 0.0)
            hot = jnp.transpose(hot)
            qfeat[here] = hot.astype(BF16)
            kfeat[here] = ((hot - 1.0) * 1e30).astype(BF16)
            real = jnp.where(jnp.broadcast_to(label, (LANES, length)) != 0, 1.0, 0.0)
            real = jnp.transpose(real)
            valid[here] = real
            sums[sums_at + S_COUNT : sums_at + S_COUNT + 1, 0:LANES] += jnp.sum(
                real, axis=0, keepdims=True
            )

        def mix(r):
            here = pl.ds(r * length, length)
            block = x[here]
            mixed[0, here] = (nn(block, proj[0]) + vrow(V_QUERY)).astype(BF16)
            mixed[1, here] = nn(block, proj[1]).astype(BF16)
            mixed[2, here] = (nn(block, proj[2]) + vrow(V_VALUE)).astype(BF16)

        def attend(r):
            here = pl.ds(r * length, length)

            @pl.loop(0, pairs)
            def _(pair):
                lanes = pl.ds(pl.multiple_of(pair * LANES, LANES), LANES)
                query = mixed[0, here, lanes]
                keys = jnp.concatenate([mixed[1, here, lanes], kfeat[here]], axis=1)
                values = jnp.concatenate(
                    [mixed[2, here, lanes], jnp.ones((length, LANES), BF16)], axis=1
                )
                sides = []
                for part in (0, 1):
                    wide = jnp.concatenate([query * scaled[part], qfeat[here]], axis=1)
                    scores = nt(wide, keys)
                    raised = jnp.exp(scores - jnp.max(scores, axis=1, keepdims=True)).astype(BF16)
                    probs[r * heads + 2 * pair + part] = raised
                    sides.append(nn(raised, values))
                total = jnp.where(first_head, sides[0][:, LANES:], sides[1][:, LANES:])
                mean = jnp.where(first_head, sides[0][:, :LANES], sides[1][:, :LANES])
                inv = 1.0 / total
                context[here, lanes] = (mean * inv).astype(BF16)
                inverse[here, lanes] = inv

        def wide_valid(r):
            real = valid[pl.ds(r * length, length)]
            return jnp.concatenate([real] * (width // LANES), axis=1)

        def normalize(value):
            center = value - jnp.mean(value, axis=1, keepdims=True)
            spread = jnp.mean(center * center, axis=1, keepdims=True)
            scale = lax.rsqrt(spread + EPSILON)
            return center * scale, scale

        def normalize_back(up, gain, vhat, scale):
            a = up * gain
            return (
                a
                - jnp.mean(a, axis=1, keepdims=True)
                - vhat * jnp.mean(a * vhat, axis=1, keepdims=True)
            ) * scale

        def first_half(r):
            here = pl.ds(r * length, length)
            attended = nn(context[here], outw[...]) + vrow(V_OUT)
            inputs = x[here].astype(F32)
            real = wide_valid(r)
            add(sums_at + S_INPUT, real * inputs * inputs)
            add(sums_at + S_ATTENDED, real * attended * attended)
            vhat, scale = normalize(inputs + attended)
            vhat1[here] = vhat
            rstd1[here] = jnp.broadcast_to(scale, (length, LANES))
            low1[here] = (vhat * vrow(V_GAIN1) + vrow(V_SHIFT1)).astype(BF16)

        def expand(r):
            here = pl.ds(r * length, length)

            @pl.loop(0, blocks)
            def _(c):
                upper = nt(low1[here], expw[c]) + vec[pl.ds(V_EXPAND + c, 1), :]
                value, derivative = gelu_parts(upper)
                active[c, here] = value.astype(BF16)
                slope[c, here] = derivative.astype(BF16)

        def second_half(r):
            here = pl.ds(r * length, length)
            shrunk = nn(active[0, here], shrw[0])
            for c in range(1, blocks):
                shrunk = shrunk + nn(active[c, here], shrw[c])
            shrunk = shrunk + vrow(V_SHRINK)
            add(sums_at + S_SHRUNK, wide_valid(r) * shrunk * shrunk)
            hidden = vhat1[here] * vrow(V_GAIN1) + vrow(V_SHIFT1)
            vhat, scale = normalize(hidden + shrunk)
            result[here] = (vhat * vrow(V_GAIN2) + vrow(V_SHIFT2)).astype(BF16)
            up = cot[here].astype(F32)
            add(V_GAIN2, up * vhat)
            add(V_SHIFT2, up)
            grad = normalize_back(up, vrow(V_GAIN2), vhat, scale)
            second[here] = grad
            low = grad.astype(BF16)
            shrunk_low[here] = low
            add(V_SHRINK, low.astype(F32))

        ones = jnp.ones((8, own_tokens), BF16)

        def expand_back(c):
            for r in range(rows):
                here = pl.ds(r * length, length)
                grad = nt(shrunk_low[here], shrw[c])
                slope[c, here] = (grad * slope[c, here].astype(F32)).astype(BF16)
            base = 2 * width * c
            upper_grad = slope[c]
            grads[base : base + width] = tn(upper_grad, low1[...]).astype(BF16)
            grads[base + width : base + 2 * width] = tn(active[c], shrunk_low[...]).astype(BF16)
            sums[V_EXPAND + c : V_EXPAND + c + 1, :] = nn(ones, upper_grad)[0:1]

        def first_half_back(r):
            here = pl.ds(r * length, length)
            up = second[here]
            for c in range(blocks):
                up = up + nn(slope[c, here], expw[c])
            vhat = vhat1[here]
            add(V_GAIN1, up * vhat)
            add(V_SHIFT1, up)
            grad = normalize_back(up, vrow(V_GAIN1), vhat, rstd1[here][:, 0:1])
            second[here] = grad
            low = grad.astype(BF16)
            attended_low[here] = low
            add(V_OUT, low.astype(F32))
            context_grad[here] = nt(low, outw[...]).astype(BF16)

        def attend_back(r, pair):
            here = pl.ds(r * length, length)
            lanes = pl.ds(pair * LANES, LANES)
            query, keys, values = (mixed[j, here, lanes] for j in range(3))
            up = (context_grad[here, lanes].astype(F32) * inverse[here, lanes]).astype(BF16)
            inner = up.astype(F32) * context[here, lanes].astype(F32)
            sides = []
            for part in (0, 1):
                raised = probs[r * heads + 2 * pair + part]
                mine = first_head if part == 0 else jnp.logical_not(first_head)
                delta = jnp.sum(jnp.where(mine, inner, 0.0), axis=1, keepdims=True)
                dprobs = nt(up * masks[part], values)
                score = (raised.astype(F32) * (dprobs - delta)).astype(BF16)
                sides.append((nn(score, keys), tn(score, query), tn(raised, up)))
            for j, factor in enumerate((SCALE, SCALE, 1.0)):
                both = jnp.where(first_head, sides[0][j], sides[1][j])
                mixed[j, here, lanes] = (both * factor).astype(BF16)

        def tokens_back(r):
            here = pl.ds(r * length, length)
            grad = second[here]
            for j in range(3):
                grad = grad + nt(mixed[j, here], proj[j])
            low1[here] = grad.astype(BF16)

        outgoing = []
        for r in range(rows):
            features(r)
            arrive(incoming.pop(0))
            if r + 1 < rows:
                incoming.append(bring(tok_hbm, x, r + 1))
            else:
                cotangents = [bring(cot_hbm, cot, r2) for r2 in range(rows)]
            mix(r)
            attend(r)
        for r in range(rows):
            first_half(r)
            expand(r)
        for r in range(rows):
            arrive(cotangents[r])
            second_half(r)
            outgoing.append(deliver(result, result_hbm, r))
        for c in range(blocks):
            expand_back(c)
            begin(reduce_chunk(c))
            if c:
                turn(c)
        for r in range(rows):
            first_half_back(r)
            turn()
        base, _ = chunks[blocks]
        grads[base : base + width] = tn(context[...], attended_low[...]).astype(BF16)
        begin(reduce_chunk(blocks))
        for r in range(rows):
            for pair in range(pairs):
                attend_back(r, pair)
                turn()
        base, _ = chunks[blocks + 1]
        for j in range(3):
            grads[base + j * width : base + (j + 1) * width] = tn(x[...], mixed[j]).astype(BF16)
        begin(reduce_chunk(blocks + 1))
        turn(len(running) - 1)
        for row, j in ((V_QUERY, 0), (V_VALUE, 2)):
            sums[row : row + 1, :] = nn(ones, mixed[j])[0:1]
        begin(reduce_sums())
        for r in range(rows):
            tokens_back(r)
            outgoing.append(deliver(low1, tgrad_hbm, r))
            turn()
        while running:
            turn()
        for pack in outgoing:
            arrive(pack)
        for copy in started:
            copy.wait_send()

    hbm = pl.BlockSpec(memory_space=pl.ANY)
    vmem = pl.BlockSpec(memory_space=pltpu.VMEM)
    big = (own_tokens, width)
    result, tokens_grad, grads, sums = pl.pallas_call(
        kernel,
        out_shape=(
            jax.ShapeDtypeStruct((group, span, width), BF16),
            jax.ShapeDtypeStruct((group, span, width), BF16),
            jax.ShapeDtypeStruct((grad_rows, width), BF16),
            jax.ShapeDtypeStruct((sum_rows, width), F32),
        ),
        in_specs=[hbm, hbm, vmem, hbm, hbm, hbm, hbm, vmem],
        out_specs=(hbm, hbm, hbm, vmem),
        scratch_shapes=[
            pltpu.VMEM(big, BF16),
            pltpu.VMEM(big, BF16),
            pltpu.VMEM((3, width, width), BF16),
            pltpu.VMEM((width, width), BF16),
            pltpu.VMEM((blocks, width, width), BF16),
            pltpu.VMEM((blocks, width, width), BF16),
            pltpu.VMEM((3, *big), BF16),
            pltpu.VMEM((rows * heads, length, length), BF16),
            pltpu.VMEM(big, BF16),
            pltpu.VMEM(big, F32),
            pltpu.VMEM(big, F32),
            pltpu.VMEM((own_tokens, LANES), F32),
            pltpu.VMEM(big, BF16),
            pltpu.VMEM((blocks, *big), BF16),
            pltpu.VMEM((blocks, *big), BF16),
            pltpu.VMEM(big, F32),
            pltpu.VMEM(big, BF16),
            pltpu.VMEM(big, BF16),
            pltpu.VMEM(big, BF16),
            pltpu.VMEM(big, BF16),
            pltpu.VMEM((own_tokens, LANES), F32),
            pltpu.VMEM((own_tokens, LANES), BF16),
            pltpu.VMEM((own_tokens, LANES), BF16),
            pltpu.VMEM((grad_rows, width), BF16),
            pltpu.VMEM((slot_rows, width), BF16),
            pltpu.VMEM((sum_rows, width), F32),
            pltpu.VMEM((sum(size for _, _, size in levels.values()), sum_rows, width), F32),
            pltpu.SemaphoreType.DMA((n_remote,)),
            pltpu.SemaphoreType.DMA((n_remote,)),
            pltpu.SemaphoreType.DMA((n_local,)),
        ],
        compiler_params=pltpu.CompilerParams(
            collective_id=0, has_side_effects=True, vmem_limit_bytes=62 * 2**20
        ),
    )(
        jnp.transpose(tokens, (1, 0, 2)),
        jnp.transpose(cotangent, (1, 0, 2)),
        jnp.transpose(segments),
        jnp.transpose(projections, (1, 0, 2)),
        outweight,
        expander.reshape(blocks, width, width),
        shrinker.reshape(blocks, width, width),
        vectors,
    )
    hidden_grads = grads[: 2 * hidden_units].reshape(blocks, 2, width, width).astype(F32)
    rest = grads[2 * hidden_units :].astype(F32)
    totals = jnp.sum(sums[sums_at : sums_at + S_COUNT], axis=1)
    count = sums[sums_at + S_COUNT, 0]
    return (
        jnp.transpose(result, (1, 0, 2)),
        jnp.transpose(tokens_grad, (1, 0, 2)),
        jnp.transpose(rest[width:].reshape(3, width, width), (1, 0, 2)),
        sums[V_QUERY : V_VALUE + 1],
        rest[:width],
        sums[V_OUT],
        sums[V_GAIN1],
        sums[V_SHIFT1],
        hidden_grads[:, 0].reshape(hidden_units, width),
        sums[V_EXPAND : V_EXPAND + blocks].reshape(hidden_units),
        hidden_grads[:, 1].reshape(hidden_units, width),
        sums[V_SHRINK],
        sums[V_GAIN2],
        sums[V_SHIFT2],
        jnp.sqrt(totals / (count * width)),
    )


def solution(mesh):
    split = P("seq", "dp", None)
    placed = (split, P(None, "dp"), *([P()] * 12), split)
    return jax.shard_map(
        local,
        mesh=mesh,
        in_specs=placed,
        out_specs=(split, split, *([P()] * 13)),
        check_vma=False,
    )
```

```python
import jax
import jax.numpy as jnp
from jax import lax
from jax.experimental import pallas as pl
from jax.experimental.pallas import tpu as pltpu
from jax.sharding import PartitionSpec as P

HEAD_DIM = 64
EPSILON = 1e-12
LANES = 128
F32 = jnp.float32
BF16 = jnp.bfloat16
SCALE = HEAD_DIM ** (-0.5)

(V_QUERY, V_VALUE, V_OUT, V_GAIN1, V_SHIFT1, V_SHRINK, V_GAIN2, V_SHIFT2, V_EXPAND) = range(9)
(S_INPUT, S_ATTENDED, S_SHRUNK, S_COUNT) = range(4)


ORDERS = (
    ("core", "side", "near", "far"),
    ("core", "near", "side", "far"),
    ("core", "far", "near", "side"),
    ("core", "near", "far", "side"),
)
CLASSES = (2, 1, 3, 1, 1, 1, 1, 1, 0, 2, 1, 1)
UNIT, SHOW, FINISH = -1, -2, -3
PLAN = (
    UNIT, SHOW, UNIT, 0, 1, UNIT, 2, 3, UNIT, 1, 4, 5, 6, UNIT, 0, 2, 7, UNIT, 3, UNIT, UNIT,
    1, UNIT, FINISH, 2, 3, 4, 8, 1, UNIT, 2, 5, UNIT, 3, 4, 1, 6, 0, UNIT, 8, 2, UNIT, 3, 5, 7,
    4, UNIT, 1, 8, UNIT, 0, 2, 6, UNIT, 3, 5, UNIT, UNIT, 7, 0, 4, 1, UNIT, 9, UNIT, 8, 1, 10,
    6, 2, 4, 11, 12, UNIT, 5, 2, 7, 12, 3, 0, 12, 3, 10, 12, 9, 4, 8, 6, 4, 11, 7, 9, 5, 8, 10,
    6, 11, 5, 0, 7, 9, 10, 5, 0, 6, 11, 8, 9, 6, 10, 7, 11, 8, 9, 7, 10, 11, 10, 9, 10, 11, 9,
    11,
)


def nn(a, b):
    return lax.dot_general(a, b, (((1,), (0,)), ((), ())), preferred_element_type=F32)


def nt(a, b):
    return lax.dot_general(a, b, (((1,), (1,)), ((), ())), preferred_element_type=F32)


def tn(a, b):
    return lax.dot_general(a, b, (((0,), (0,)), ((), ())), preferred_element_type=F32)


def gelu_parts(u):
    z = jnp.abs(u)
    d = 1.0 + (0.3275911 * 0.5**0.5) * z
    t = pl.reciprocal(d, approx=True)
    t = t * (2.0 - d * t)
    e = jnp.exp(-0.5 * u * u)
    poly = 0.5 * 1.061405429
    poly = poly * t - 0.5 * 1.453152027
    poly = poly * t + 0.5 * 1.421413741
    poly = poly * t - 0.5 * 0.284496736
    poly = poly * t + 0.5 * 0.254829592
    tail = poly * t * e
    phi = jnp.where(u >= 0.0, 1.0 - tail, tail)
    return u * phi, phi + (0.3989422804014327 * u) * e


def levels_of(n_seq, n_dp):
    low = 2 if n_seq % 2 == 0 else 1
    near = 1
    while 4 * near * near <= n_dp and n_dp % (2 * near) == 0:
        near *= 2
    return {
        "core": ("seq", 1, low),
        "side": ("seq", low, n_seq // low),
        "near": ("dp", 1, near),
        "far": ("dp", near, n_dp // near),
    }


def slots_of(levels, order, rows):
    total = 0
    for name in order:
        size = levels[name][2]
        if size == 1:
            continue
        if rows % (16 * size) == 0:
            rows //= size
            total += (size - 1) * rows
        else:
            total += size * rows
    return total


def local(
    tokens,
    segments,
    projections,
    projbias,
    outweight,
    outbias,
    normgain,
    normshift,
    expander,
    expandbias,
    shrinker,
    shrinkbias,
    finalgain,
    finalshift,
    cotangent,
):
    n_seq, n_dp = lax.axis_size("seq"), lax.axis_size("dp")
    span, group, width = tokens.shape
    length = segments.shape[0]
    rows = group // n_seq
    hidden_units = expander.shape[0]
    blocks = hidden_units // width
    heads = width // HEAD_DIM
    pairs = width // LANES
    own_tokens = rows * length
    levels = levels_of(n_seq, n_dp)
    n_chunks = 2 * blocks + 4
    chunk_orders = [ORDERS[CLASSES[i % len(CLASSES)]] for i in range(n_chunks)]
    slot_bases, slot_rows = [], 0
    for order in chunk_orders:
        slot_bases.append(slot_rows)
        slot_rows += slots_of(levels, order, width)
    grad_rows = n_chunks * width
    vec_rows = V_EXPAND + blocks
    sum_rows = -(-(vec_rows + 4) // 8) * 8
    sums_at = vec_rows
    ring = sum(size - 1 for _, _, size in levels.values())
    n_remote = 4 * rows * (n_seq - 1) + n_chunks * 2 * ring + ring
    n_local = 8 + 4 * rows + n_chunks

    vectors = jnp.concatenate(
        [
            projbias.reshape(-1),
            outbias,
            normgain,
            normshift,
            shrinkbias,
            finalgain,
            finalshift,
            expandbias,
        ]
    )
    vectors = vectors.astype(F32).reshape(vec_rows, width)

    def kernel(
        tok_hbm,
        cot_hbm,
        labels,
        proj_hbm,
        out_hbm,
        exp_hbm,
        shr_hbm,
        vec,
        result_hbm,
        tgrad_hbm,
        exp_grad,
        shr_grad,
        out_grad,
        proj_grad,
        sums_out,
        raw,
        result_in,
        tgrad_in,
        x,
        cot,
        proj,
        outw,
        expw,
        shrw,
        mixed,
        probs,
        context,
        inverse,
        vhat1,
        rstd1,
        low1,
        active,
        slope,
        second,
        shrunk_low,
        result,
        valid,
        qfeat,
        kfeat,
        grads,
        slots,
        sums,
        sum_slots,
        send_sem,
        recv_sem,
        local_sem,
    ):
        me = lax.axis_index("seq")
        attended_low, context_grad = shrunk_low, cot
        started, counters = [], {"remote": 0, "local": 0}

        def remote(src, dst, where):
            i = counters["remote"]
            counters["remote"] += 1
            copy = pltpu.make_async_remote_copy(
                src_ref=src,
                dst_ref=dst,
                send_sem=send_sem.at[i],
                recv_sem=recv_sem.at[i],
                device_id=where,
                device_id_type=pl.DeviceIdType.MESH,
            )
            copy.start()
            started.append(copy)
            return copy

        def near_copy(src, dst):
            i = counters["local"]
            counters["local"] += 1
            copy = pltpu.make_async_copy(src, dst, local_sem.at[i])
            copy.start()
            return copy

        def place(name):
            axis, stride, size = levels[name]
            index = lax.axis_index(axis)
            mine = lax.rem(lax.div(index, stride), size)
            return axis, index, stride, size, mine

        arriving = [near_copy(tok_hbm, raw.at[0]), near_copy(cot_hbm, raw.at[1])]
        weights = [
            near_copy(proj_hbm, proj),
            near_copy(out_hbm, outw),
            near_copy(exp_hbm, expw),
            near_copy(shr_hbm, shrw),
        ]

        barrier = pltpu.get_barrier_semaphore()
        greeted = 0
        for j in range(1, n_seq):
            pl.semaphore_signal(
                barrier,
                inc=1,
                device_id={"seq": lax.rem(me + j, n_seq)},
                device_id_type=pl.DeviceIdType.MESH,
            )
            greeted += 1
        for name in ("near", "far"):
            axis, index, stride, size, mine = place(name)
            for j in range(1, size):
                k = lax.rem(mine + j, size)
                pl.semaphore_signal(
                    barrier,
                    inc=1,
                    device_id={axis: index + (k - mine) * stride},
                    device_id_type=pl.DeviceIdType.MESH,
                )
                greeted += 1

        def bring(base, dst, r):
            here = pl.ds(pl.multiple_of(r * length + me * span, 16), span)
            far = []
            for j in sorted(range(1, n_seq), key=lambda j: j % 2):
                k = lax.rem(me + j, n_seq)
                src = grads.at[pl.ds(pl.multiple_of(base + (k * rows + r) * span, 16), span)]
                far.append(remote(src, dst.at[here], {"seq": k}))
            own = pl.ds(pl.multiple_of(base + (me * rows + r) * span, 16), span)
            dst[here] = grads[own]
            return far

        def deliver(src, dst, r):
            far = []
            for j in sorted(range(1, n_seq), key=lambda j: j % 2):
                k = lax.rem(me + j, n_seq)
                piece = src.at[pl.ds(pl.multiple_of(r * length + k * span, 16), span)]
                far.append(remote(piece, dst.at[me * rows + r], {"seq": k}))
            own = pl.ds(pl.multiple_of(r * length + me * span, 16), span)
            dst[me * rows + r] = src[own]
            return far

        def arrive(copies):
            for copy in copies:
                copy.wait_recv()

        def spread(index, base):
            arriving[index].wait()
            turned = jnp.swapaxes(raw[index], 0, 1)
            grads[base : base + group * span] = turned.reshape(group * span, width)

        def collect(index, src, dst):
            raw[index] = jnp.swapaxes(src[...], 0, 1)
            return near_copy(raw.at[index], dst)

        goals = []
        for c in range(blocks):
            goals += [(exp_grad, c * width), (shr_grad, c * width)]
        goals.append((out_grad, 0))
        goals += [(proj_grad, j * width) for j in range(3)]

        def reduce_chunk(index):
            base, count = index * width, width
            written = []
            at, slot, stack = base, slot_bases[index], []
            goal, goal_row = goals[index]
            offset = goal_row - base
            for name in chunk_orders[index]:
                axis, own, stride, size, mine = place(name)
                if size == 1:
                    continue
                copies = []
                if count % (16 * size) == 0:
                    piece = count // size
                    for j in range(1, size):
                        k = lax.rem(mine + j, size)
                        copies.append(
                            remote(
                                grads.at[pl.ds(pl.multiple_of(at + k * piece, 16), piece)],
                                slots.at[pl.ds(slot + (j - 1) * piece, piece)],
                                {axis: own + (k - mine) * stride},
                            )
                        )
                    yield
                    here = pl.multiple_of(at + mine * piece, 16)
                    for copy in copies:
                        copy.wait_recv()
                    total = grads[pl.ds(here, piece)].astype(F32)
                    for j in range(size - 1):
                        total = total + slots[pl.ds(slot + j * piece, piece)].astype(F32)
                    grads[pl.ds(here, piece)] = total.astype(BF16)
                    stack.append((name, at, piece))
                    slot += (size - 1) * piece
                    at, count = here, piece
                else:
                    mine_slot = pl.ds(pl.multiple_of(slot + mine * count, 16), count)
                    slots[mine_slot] = grads[pl.ds(at, count)]
                    for j in range(1, size):
                        k = lax.rem(mine + j, size)
                        copies.append(
                            remote(
                                slots.at[mine_slot],
                                slots.at[mine_slot],
                                {axis: own + (k - mine) * stride},
                            )
                        )
                    yield
                    for copy in copies:
                        copy.wait_recv()
                    total = jnp.zeros((count, width), F32)
                    for j in range(size):
                        total = total + slots[pl.ds(slot + j * count, count)].astype(F32)
                    grads[pl.ds(at, count)] = total.astype(BF16)
                    slot += size * count
            block, copies = grads.at[pl.ds(at, count)], []
            written.append(near_copy(block, goal.at[pl.ds(pl.multiple_of(at + offset, 16), count)]))
            for name, before, piece in reversed(stack):
                axis, own, stride, size, mine = place(name)
                target = goal.at[pl.ds(pl.multiple_of(at + offset, 16), piece)]
                copies = []
                for j in range(1, size):
                    k = lax.rem(mine + j, size)
                    copies.append(remote(block, target, {axis: own + (k - mine) * stride}))
                yield
                for copy in copies:
                    copy.wait_recv()
                if written:
                    written.pop().wait()
                count = piece * size
                at, block = before, goal.at[pl.ds(pl.multiple_of(before + offset, 16), count)]
            if written:
                written.pop().wait()

        def reduce_sums():
            current = sums
            for step, name in enumerate(("core", "side", "near", "far")):
                axis, own, stride, size, mine = place(name)
                if size == 1:
                    continue
                first = sum(levels[n][2] for n in ("core", "side", "near", "far")[:step])
                sum_slots[first + mine] = current[...]
                copies = []
                for j in range(1, size):
                    k = lax.rem(mine + j, size)
                    block = sum_slots.at[first + mine]
                    copies.append(remote(block, block, {axis: own + (k - mine) * stride}))
                yield
                for copy in copies:
                    copy.wait_recv()
                total = sum_slots[first]
                for j in range(1, size):
                    total = total + sum_slots[first + j]
                current[...] = total
            sums_out[...] = current[...]

        running = {}

        def advance(index):
            if index in running and next(running[index], "end") == "end":
                del running[index]

        def begin(index):
            running[index] = reduce_chunk(index) if index < n_chunks else reduce_sums()
            next(running[index])

        def add(row, value):
            sums[row : row + 1, :] += jnp.sum(value, axis=0, keepdims=True)

        def vrow(i):
            return vec[i : i + 1, :]

        def features(r):
            here = pl.ds(r * length, length)
            label = labels[pl.ds(me * rows + r, 1), :]
            ids = lax.broadcasted_iota(jnp.int32, (LANES, length), 0)
            hot = jnp.where(ids == label, 1.0, 0.0)
            hot = jnp.transpose(hot)
            qfeat[here] = hot.astype(BF16)
            kfeat[here] = ((hot - 1.0) * 1e30).astype(BF16)
            real = jnp.where(jnp.broadcast_to(label, (LANES, length)) != 0, 1.0, 0.0)
            real = jnp.transpose(real)
            valid[here] = real
            sums[sums_at + S_COUNT : sums_at + S_COUNT + 1, 0:LANES] += jnp.sum(
                real, axis=0, keepdims=True
            )

        spread(0, 0)
        pl.semaphore_wait(barrier, greeted)
        incoming = [bring(0, x, r) for r in range(rows)]
        spread(1, group * span)
        cotangents = [bring(group * span, cot, r) for r in range(rows)]
        sent = list(started)
        sums[...] = jnp.zeros_like(sums)
        for r in range(rows):
            features(r)
        for copy in weights:
            copy.wait()

        lane = lax.broadcasted_iota(jnp.int32, (length, LANES), 1)
        first_head = lane < HEAD_DIM
        lane_row = lax.broadcasted_iota(jnp.int32, (1, LANES), 1)
        masks = [
            jnp.where(lane_row // HEAD_DIM == part, 1.0, 0.0).astype(BF16) for part in (0, 1)
        ]
        scaled = [mask * BF16(SCALE) for mask in masks]

        def mix(r):
            here = pl.ds(r * length, length)
            block = x[here]
            mixed[0, here] = (nn(block, proj[0]) + vrow(V_QUERY)).astype(BF16)
            mixed[1, here] = nn(block, proj[1]).astype(BF16)
            mixed[2, here] = (nn(block, proj[2]) + vrow(V_VALUE)).astype(BF16)

        def attend(r):
            here = pl.ds(r * length, length)

            @pl.loop(0, pairs)
            def _(pair):
                lanes = pl.ds(pl.multiple_of(pair * LANES, LANES), LANES)
                query = mixed[0, here, lanes]
                keys = jnp.concatenate([mixed[1, here, lanes], kfeat[here]], axis=1)
                values = jnp.concatenate(
                    [mixed[2, here, lanes], jnp.ones((length, LANES), BF16)], axis=1
                )
                sides = []
                for part in (0, 1):
                    wide = jnp.concatenate([query * scaled[part], qfeat[here]], axis=1)
                    scores = nt(wide, keys)
                    raised = jnp.exp(scores - jnp.max(scores, axis=1, keepdims=True)).astype(BF16)
                    probs[r * heads + 2 * pair + part] = raised
                    sides.append(nn(raised, values))
                total = jnp.where(first_head, sides[0][:, LANES:], sides[1][:, LANES:])
                mean = jnp.where(first_head, sides[0][:, :LANES], sides[1][:, :LANES])
                inv = 1.0 / total
                context[here, lanes] = (mean * inv).astype(BF16)
                inverse[here, lanes] = inv

        def wide_valid(r):
            real = valid[pl.ds(r * length, length)]
            return jnp.concatenate([real] * (width // LANES), axis=1)

        def normalize(value):
            center = value - jnp.mean(value, axis=1, keepdims=True)
            spread = jnp.mean(center * center, axis=1, keepdims=True)
            scale = lax.rsqrt(spread + EPSILON)
            return center * scale, scale

        def normalize_back(up, gain, vhat, scale):
            a = up * gain
            return (
                a
                - jnp.mean(a, axis=1, keepdims=True)
                - vhat * jnp.mean(a * vhat, axis=1, keepdims=True)
            ) * scale

        def first_half(r):
            here = pl.ds(r * length, length)
            attended = nn(context[here], outw[...]) + vrow(V_OUT)
            inputs = x[here].astype(F32)
            real = wide_valid(r)
            add(sums_at + S_INPUT, real * inputs * inputs)
            add(sums_at + S_ATTENDED, real * attended * attended)
            vhat, scale = normalize(inputs + attended)
            vhat1[here] = vhat
            rstd1[here] = jnp.broadcast_to(scale, (length, LANES))
            low1[here] = (vhat * vrow(V_GAIN1) + vrow(V_SHIFT1)).astype(BF16)

        def expand(r):
            here = pl.ds(r * length, length)

            @pl.loop(0, blocks)
            def _(c):
                upper = nt(low1[here], expw[c]) + vec[pl.ds(V_EXPAND + c, 1), :]
                value, derivative = gelu_parts(upper)
                active[c, here] = value.astype(BF16)
                slope[c, here] = derivative.astype(BF16)

        def second_half(r):
            here = pl.ds(r * length, length)
            shrunk = nn(active[0, here], shrw[0])
            for c in range(1, blocks):
                shrunk = shrunk + nn(active[c, here], shrw[c])
            shrunk = shrunk + vrow(V_SHRINK)
            add(sums_at + S_SHRUNK, wide_valid(r) * shrunk * shrunk)
            hidden = vhat1[here] * vrow(V_GAIN1) + vrow(V_SHIFT1)
            vhat, scale = normalize(hidden + shrunk)
            result[here] = (vhat * vrow(V_GAIN2) + vrow(V_SHIFT2)).astype(BF16)
            up = cot[here].astype(F32)
            add(V_GAIN2, up * vhat)
            add(V_SHIFT2, up)
            grad = normalize_back(up, vrow(V_GAIN2), vhat, scale)
            second[here] = grad
            low = grad.astype(BF16)
            shrunk_low[here] = low
            add(V_SHRINK, low.astype(F32))

        ones = jnp.ones((8, own_tokens), BF16)

        def expand_back(c):
            for r in range(rows):
                here = pl.ds(r * length, length)
                grad = nt(shrunk_low[here], shrw[c])
                slope[c, here] = (grad * slope[c, here].astype(F32)).astype(BF16)
            base = 2 * width * c
            upper_grad = slope[c]
            grads[base : base + width] = tn(upper_grad, low1[...]).astype(BF16)
            begin(2 * c)
            grads[base + width : base + 2 * width] = tn(active[c], shrunk_low[...]).astype(BF16)
            begin(2 * c + 1)
            sums[V_EXPAND + c : V_EXPAND + c + 1, :] = nn(ones, upper_grad)[0:1]

        def first_half_back(r):
            here = pl.ds(r * length, length)
            up = second[here]
            for c in range(blocks):
                up = up + nn(slope[c, here], expw[c])
            vhat = vhat1[here]
            add(V_GAIN1, up * vhat)
            add(V_SHIFT1, up)
            grad = normalize_back(up, vrow(V_GAIN1), vhat, rstd1[here][:, 0:1])
            second[here] = grad
            low = grad.astype(BF16)
            attended_low[here] = low
            add(V_OUT, low.astype(F32))
            context_grad[here] = nt(low, outw[...]).astype(BF16)

        def attend_back(r, pair):
            here = pl.ds(r * length, length)
            lanes = pl.ds(pair * LANES, LANES)
            query, keys, values = (mixed[j, here, lanes] for j in range(3))
            up = (context_grad[here, lanes].astype(F32) * inverse[here, lanes]).astype(BF16)
            inner = up.astype(F32) * context[here, lanes].astype(F32)
            sides = []
            for part in (0, 1):
                raised = probs[r * heads + 2 * pair + part]
                mine = first_head if part == 0 else jnp.logical_not(first_head)
                delta = jnp.sum(jnp.where(mine, inner, 0.0), axis=1, keepdims=True)
                dprobs = nt(up * masks[part], values)
                score = (raised.astype(F32) * (dprobs - delta)).astype(BF16)
                sides.append((nn(score, keys), tn(score, query), tn(raised, up)))
            for j, factor in enumerate((SCALE, SCALE, 1.0)):
                both = jnp.where(first_head, sides[0][j], sides[1][j])
                mixed[j, here, lanes] = (both * factor).astype(BF16)

        def tokens_back(r):
            here = pl.ds(r * length, length)
            grad = second[here]
            for j in range(3):
                grad = grad + nt(mixed[j, here], proj[j])
            low1[here] = grad.astype(BF16)

        def out_back():
            base = 2 * blocks * width
            grads[base : base + width] = tn(context[...], attended_low[...]).astype(BF16)
            begin(2 * blocks)

        def mix_back(j):
            base = (2 * blocks + 1 + j) * width
            grads[base : base + width] = tn(x[...], mixed[j]).astype(BF16)
            begin(2 * blocks + 1 + j)

        def sums_back():
            for row, j in ((V_QUERY, 0), (V_VALUE, 2)):
                sums[row : row + 1, :] = nn(ones, mixed[j])[0:1]
            begin(n_chunks)

        returned, written_out = [], []

        def give_back(r):
            tokens_back(r)
            returned.append(deliver(low1, tgrad_in, r))

        def finish_result():
            for copies in results:
                arrive(copies)
            written_out.append(collect(0, result_in, result_hbm))

        for r in range(rows):
            arrive(incoming[r])
            mix(r)
            attend(r)
            first_half(r)
            expand(r)
        results = []
        for r in range(rows):
            arrive(cotangents[r])
            second_half(r)
        for copy in sent:
            copy.wait_send()

        def show(r):
            results.append(deliver(result, result_in, r))

        units = []
        for c in range(blocks):
            units.append(lambda c=c: expand_back(c))
        units += [lambda r=r: first_half_back(r) for r in range(rows)]
        units.append(out_back)
        for r in range(rows):
            units += [lambda r=r, pair=pair: attend_back(r, pair) for pair in range(pairs)]
        units += [lambda j=j: mix_back(j) for j in range(3)]
        units.append(sums_back)
        units += [lambda r=r: give_back(r) for r in range(rows)]
        late = {SHOW: lambda: [show(r) for r in range(rows)], FINISH: finish_result}
        for index in PLAN:
            if index == UNIT:
                if units:
                    units.pop(0)()
            elif index in late:
                late.pop(index)()
            else:
                advance(index)
        for unit in units + list(late.values()):
            unit()
        while running:
            for index in list(running):
                advance(index)
        for copies in returned:
            arrive(copies)
        written_out.append(collect(1, tgrad_in, tgrad_hbm))
        for copy in started[len(sent) :]:
            copy.wait_send()
        for copy in written_out:
            copy.wait()

    hbm = pl.BlockSpec(memory_space=pl.ANY)
    vmem = pl.BlockSpec(memory_space=pltpu.VMEM)
    big = (own_tokens, width)
    result, tokens_grad, exp_grad, shr_grad, out_grad, proj_grad, sums = pl.pallas_call(
        kernel,
        out_shape=(
            jax.ShapeDtypeStruct((span, group, width), BF16),
            jax.ShapeDtypeStruct((span, group, width), BF16),
            jax.ShapeDtypeStruct((hidden_units, width), BF16),
            jax.ShapeDtypeStruct((hidden_units, width), BF16),
            jax.ShapeDtypeStruct((width, width), BF16),
            jax.ShapeDtypeStruct((3 * width, width), BF16),
            jax.ShapeDtypeStruct((sum_rows, width), F32),
        ),
        in_specs=[hbm, hbm, vmem, hbm, hbm, hbm, hbm, vmem],
        out_specs=(*([hbm] * 6), vmem),
        scratch_shapes=[
            pltpu.VMEM((2, span, group, width), BF16),
            pltpu.VMEM((group, span, width), BF16),
            pltpu.VMEM((group, span, width), BF16),
            pltpu.VMEM(big, BF16),
            pltpu.VMEM(big, BF16),
            pltpu.VMEM((3, width, width), BF16),
            pltpu.VMEM((width, width), BF16),
            pltpu.VMEM((blocks, width, width), BF16),
            pltpu.VMEM((blocks, width, width), BF16),
            pltpu.VMEM((3, *big), BF16),
            pltpu.VMEM((rows * heads, length, length), BF16),
            pltpu.VMEM(big, BF16),
            pltpu.VMEM(big, F32),
            pltpu.VMEM(big, F32),
            pltpu.VMEM((own_tokens, LANES), F32),
            pltpu.VMEM(big, BF16),
            pltpu.VMEM((blocks, *big), BF16),
            pltpu.VMEM((blocks, *big), BF16),
            pltpu.VMEM(big, F32),
            pltpu.VMEM(big, BF16),
            pltpu.VMEM(big, BF16),
            pltpu.VMEM((own_tokens, LANES), F32),
            pltpu.VMEM((own_tokens, LANES), BF16),
            pltpu.VMEM((own_tokens, LANES), BF16),
            pltpu.VMEM((grad_rows, width), BF16),
            pltpu.VMEM((slot_rows, width), BF16),
            pltpu.VMEM((sum_rows, width), F32),
            pltpu.VMEM((sum(size for _, _, size in levels.values()), sum_rows, width), F32),
            pltpu.SemaphoreType.DMA((n_remote,)),
            pltpu.SemaphoreType.DMA((n_remote,)),
            pltpu.SemaphoreType.DMA((n_local,)),
        ],
        compiler_params=pltpu.CompilerParams(
            collective_id=0, has_side_effects=True, vmem_limit_bytes=62 * 2**20
        ),
    )(
        tokens,
        cotangent,
        jnp.transpose(segments),
        jnp.transpose(projections, (1, 0, 2)),
        outweight,
        expander.reshape(blocks, width, width),
        shrinker.reshape(blocks, width, width),
        vectors,
    )
    totals = jnp.sum(sums[sums_at : sums_at + S_COUNT], axis=1)
    count = sums[sums_at + S_COUNT, 0]
    return (
        result,
        tokens_grad,
        jnp.transpose(proj_grad.reshape(3, width, width), (1, 0, 2)).astype(F32),
        sums[V_QUERY : V_VALUE + 1],
        out_grad.astype(F32),
        sums[V_OUT],
        sums[V_GAIN1],
        sums[V_SHIFT1],
        exp_grad.astype(F32),
        sums[V_EXPAND : V_EXPAND + blocks].reshape(hidden_units),
        shr_grad.astype(F32),
        sums[V_SHRINK],
        sums[V_GAIN2],
        sums[V_SHIFT2],
        jnp.sqrt(totals / (count * width)),
    )


def solution(mesh):
    split = P("seq", "dp", None)
    placed = (split, P(None, "dp"), *([P()] * 12), split)
    return jax.shard_map(
        local,
        mesh=mesh,
        in_specs=placed,
        out_specs=(split, split, *([P()] * 13)),
        check_vma=False,
    )
```

```python
import jax
import jax.numpy as jnp
from jax import lax
from jax.experimental import pallas as pl
from jax.experimental.pallas import tpu as pltpu
from jax.sharding import PartitionSpec as P

HEAD_DIM = 64
EPSILON = 1e-12
LANES = 128
F32 = jnp.float32
BF16 = jnp.bfloat16
SCALE = HEAD_DIM ** (-0.5)

(V_QUERY, V_VALUE, V_OUT, V_GAIN1, V_SHIFT1, V_SHRINK, V_GAIN2, V_SHIFT2, V_EXPAND) = range(9)
(S_INPUT, S_ATTENDED, S_SHRUNK, S_COUNT) = range(4)


ORDERS = (
    ("core", "side", "near", "far"),
    ("core", "near", "side", "far"),
    ("core", "far", "near", "side"),
    ("core", "near", "far", "side"),
)
CLASSES = (2, 1, 3, 1, 1, 1, 1, 1, 0, 2, 1, 1)
UNIT, SHOW = -1, -2
PLAN = (
    UNIT, SHOW, UNIT, 0, 1, UNIT, 2, 3, UNIT, 1, 4, 5, 6, UNIT, 0, 2, 7, UNIT, 3, UNIT, UNIT,
    1, UNIT, 2, 3, 4, 8, 1, UNIT, 2, 5, UNIT, 3, 4, 1, 6, 0, UNIT, 8, 2, UNIT, 3, 5, 7, 4,
    UNIT, 1, 8, UNIT, 0, 2, 6, UNIT, 3, 5, UNIT, UNIT, 7, 0, 4, 1, UNIT, 9, UNIT, 8, 1, 10, 6,
    2, 4, 11, 12, UNIT, 5, 2, 7, 12, 3, 0, 12, 3, 10, 12, 9, 4, 8, 6, 4, 11, 7, 9, 5, 8, 10, 6,
    11, 5, 0, 7, 9, 10, 5, 0, 6, 11, 8, 9, 6, 10, 7, 11, 8, 9, 7, 10, 11, 10, 9, 10, 11, 9, 11,
)


def nn(a, b):
    return lax.dot_general(a, b, (((1,), (0,)), ((), ())), preferred_element_type=F32)


def nt(a, b):
    return lax.dot_general(a, b, (((1,), (1,)), ((), ())), preferred_element_type=F32)


def tn(a, b):
    return lax.dot_general(a, b, (((0,), (0,)), ((), ())), preferred_element_type=F32)


def gelu_parts(u):
    z = jnp.abs(u)
    d = 1.0 + (0.3275911 * 0.5**0.5) * z
    t = pl.reciprocal(d, approx=True)
    t = t * (2.0 - d * t)
    e = jnp.exp(-0.5 * u * u)
    poly = 0.5 * 1.061405429
    poly = poly * t - 0.5 * 1.453152027
    poly = poly * t + 0.5 * 1.421413741
    poly = poly * t - 0.5 * 0.284496736
    poly = poly * t + 0.5 * 0.254829592
    tail = poly * t * e
    phi = jnp.where(u >= 0.0, 1.0 - tail, tail)
    return u * phi, phi + (0.3989422804014327 * u) * e


def levels_of(n_seq, n_dp):
    low = 2 if n_seq % 2 == 0 else 1
    near = 1
    while 4 * near * near <= n_dp and n_dp % (2 * near) == 0:
        near *= 2
    return {
        "core": ("seq", 1, low),
        "side": ("seq", low, n_seq // low),
        "near": ("dp", 1, near),
        "far": ("dp", near, n_dp // near),
    }


def slots_of(levels, order, rows):
    total = 0
    for name in order:
        size = levels[name][2]
        if size == 1:
            continue
        if rows % (16 * size) == 0:
            rows //= size
            total += (size - 1) * rows
        else:
            total += size * rows
    return total


def local(
    tokens,
    segments,
    projections,
    projbias,
    outweight,
    outbias,
    normgain,
    normshift,
    expander,
    expandbias,
    shrinker,
    shrinkbias,
    finalgain,
    finalshift,
    cotangent,
):
    n_seq, n_dp = lax.axis_size("seq"), lax.axis_size("dp")
    span, group, width = tokens.shape
    length = segments.shape[0]
    rows = group // n_seq
    hidden_units = expander.shape[0]
    blocks = hidden_units // width
    heads = width // HEAD_DIM
    pairs = width // LANES
    own_tokens = rows * length
    levels = levels_of(n_seq, n_dp)
    n_chunks = 2 * blocks + 4
    chunk_orders = [ORDERS[CLASSES[i % len(CLASSES)]] for i in range(n_chunks)]
    slot_bases, slot_rows = [], 0
    for order in chunk_orders:
        slot_bases.append(slot_rows)
        slot_rows += slots_of(levels, order, width)
    grad_rows = n_chunks * width
    vec_rows = V_EXPAND + blocks
    sum_rows = -(-(vec_rows + 4) // 8) * 8
    sums_at = vec_rows
    ring = sum(size - 1 for _, _, size in levels.values())
    n_remote = 4 * rows * (n_seq - 1) + n_chunks * 2 * ring + ring
    n_local = 8 + 4 * rows + n_chunks

    def kernel(
        tok_hbm,
        cot_hbm,
        labels,
        proj_hbm,
        out_hbm,
        exp_hbm,
        shr_hbm,
        bias,
        out_bias,
        gain1,
        shift1,
        exp_bias,
        shr_bias,
        gain2,
        shift2,
        result_in,
        tgrad_in,
        exp_grad,
        shr_grad,
        out_grad,
        proj_grad,
        sums_out,
        raw,
        vec,
        x,
        cot,
        proj,
        outw,
        expw,
        shrw,
        mixed,
        probs,
        context,
        inverse,
        vhat1,
        rstd1,
        low1,
        active,
        slope,
        second,
        shrunk_low,
        result,
        valid,
        qfeat,
        kfeat,
        grads,
        slots,
        sums,
        sum_slots,
        send_sem,
        recv_sem,
        local_sem,
    ):
        me = lax.axis_index("seq")
        attended_low, context_grad = shrunk_low, cot
        started, counters = [], {"remote": 0, "local": 0}

        def remote(src, dst, where):
            i = counters["remote"]
            counters["remote"] += 1
            copy = pltpu.make_async_remote_copy(
                src_ref=src,
                dst_ref=dst,
                send_sem=send_sem.at[i],
                recv_sem=recv_sem.at[i],
                device_id=where,
                device_id_type=pl.DeviceIdType.MESH,
            )
            copy.start()
            started.append(copy)
            return copy

        def near_copy(src, dst):
            i = counters["local"]
            counters["local"] += 1
            copy = pltpu.make_async_copy(src, dst, local_sem.at[i])
            copy.start()
            return copy

        def place(name):
            axis, stride, size = levels[name]
            index = lax.axis_index(axis)
            mine = lax.rem(lax.div(index, stride), size)
            return axis, index, stride, size, mine

        arriving = [near_copy(tok_hbm, raw.at[0]), near_copy(cot_hbm, raw.at[1])]
        weights = [
            near_copy(proj_hbm, proj),
            near_copy(out_hbm, outw),
            near_copy(exp_hbm, expw),
            near_copy(shr_hbm, shrw),
        ]

        barrier = pltpu.get_barrier_semaphore()
        greeted = 0
        for j in range(1, n_seq):
            pl.semaphore_signal(
                barrier,
                inc=1,
                device_id={"seq": lax.rem(me + j, n_seq)},
                device_id_type=pl.DeviceIdType.MESH,
            )
            greeted += 1
        for name in ("near", "far"):
            axis, index, stride, size, mine = place(name)
            for j in range(1, size):
                k = lax.rem(mine + j, size)
                pl.semaphore_signal(
                    barrier,
                    inc=1,
                    device_id={axis: index + (k - mine) * stride},
                    device_id_type=pl.DeviceIdType.MESH,
                )
                greeted += 1

        def bring(base, dst, r):
            here = pl.ds(pl.multiple_of(r * length + me * span, 16), span)
            far = []
            for j in sorted(range(1, n_seq), key=lambda j: j % 2):
                k = lax.rem(me + j, n_seq)
                src = grads.at[pl.ds(pl.multiple_of(base + (k * rows + r) * span, 16), span)]
                far.append(remote(src, dst.at[here], {"seq": k}))
            own = pl.ds(pl.multiple_of(base + (me * rows + r) * span, 16), span)
            dst[here] = grads[own]
            return far

        def deliver(src, dst, r):
            far = []
            for j in sorted(range(1, n_seq), key=lambda j: j % 2):
                k = lax.rem(me + j, n_seq)
                piece = src.at[pl.ds(pl.multiple_of(r * length + k * span, 16), span)]
                far.append(remote(piece, dst.at[me * rows + r], {"seq": k}))
            own = pl.ds(pl.multiple_of(r * length + me * span, 16), span)
            kept.append(near_copy(src.at[own], dst.at[me * rows + r]))
            return far

        kept = []

        def arrive(copies):
            for copy in copies:
                copy.wait_recv()

        def spread(index, base):
            arriving[index].wait()
            turned = jnp.swapaxes(raw[index], 0, 1)
            grads[base : base + group * span] = turned.reshape(group * span, width)

        goals = []
        for c in range(blocks):
            goals += [(exp_grad, c * width), (shr_grad, c * width)]
        goals.append((out_grad, 0))
        goals += [(proj_grad, j * width) for j in range(3)]

        def reduce_chunk(index):
            base, count = index * width, width
            written = []
            at, slot, stack = base, slot_bases[index], []
            goal, goal_row = goals[index]
            offset = goal_row - base
            for name in chunk_orders[index]:
                axis, own, stride, size, mine = place(name)
                if size == 1:
                    continue
                copies = []
                if count % (16 * size) == 0:
                    piece = count // size
                    for j in range(1, size):
                        k = lax.rem(mine + j, size)
                        copies.append(
                            remote(
                                grads.at[pl.ds(pl.multiple_of(at + k * piece, 16), piece)],
                                slots.at[pl.ds(slot + (j - 1) * piece, piece)],
                                {axis: own + (k - mine) * stride},
                            )
                        )
                    yield
                    here = pl.multiple_of(at + mine * piece, 16)
                    for copy in copies:
                        copy.wait_recv()
                    total = grads[pl.ds(here, piece)].astype(F32)
                    for j in range(size - 1):
                        total = total + slots[pl.ds(slot + j * piece, piece)].astype(F32)
                    grads[pl.ds(here, piece)] = total.astype(BF16)
                    stack.append((name, at, piece))
                    slot += (size - 1) * piece
                    at, count = here, piece
                else:
                    mine_slot = pl.ds(pl.multiple_of(slot + mine * count, 16), count)
                    slots[mine_slot] = grads[pl.ds(at, count)]
                    for j in range(1, size):
                        k = lax.rem(mine + j, size)
                        copies.append(
                            remote(
                                slots.at[mine_slot],
                                slots.at[mine_slot],
                                {axis: own + (k - mine) * stride},
                            )
                        )
                    yield
                    for copy in copies:
                        copy.wait_recv()
                    total = jnp.zeros((count, width), F32)
                    for j in range(size):
                        total = total + slots[pl.ds(slot + j * count, count)].astype(F32)
                    grads[pl.ds(at, count)] = total.astype(BF16)
                    slot += size * count
            block, copies = grads.at[pl.ds(at, count)], []
            written.append(near_copy(block, goal.at[pl.ds(pl.multiple_of(at + offset, 16), count)]))
            for name, before, piece in reversed(stack):
                axis, own, stride, size, mine = place(name)
                target = goal.at[pl.ds(pl.multiple_of(at + offset, 16), piece)]
                copies = []
                for j in range(1, size):
                    k = lax.rem(mine + j, size)
                    copies.append(remote(block, target, {axis: own + (k - mine) * stride}))
                yield
                for copy in copies:
                    copy.wait_recv()
                if written:
                    written.pop().wait()
                count = piece * size
                at, block = before, goal.at[pl.ds(pl.multiple_of(before + offset, 16), count)]
            if written:
                written.pop().wait()

        def reduce_sums():
            current = sums
            for step, name in enumerate(("core", "side", "near", "far")):
                axis, own, stride, size, mine = place(name)
                if size == 1:
                    continue
                first = sum(levels[n][2] for n in ("core", "side", "near", "far")[:step])
                sum_slots[first + mine] = current[...]
                copies = []
                for j in range(1, size):
                    k = lax.rem(mine + j, size)
                    block = sum_slots.at[first + mine]
                    copies.append(remote(block, block, {axis: own + (k - mine) * stride}))
                yield
                for copy in copies:
                    copy.wait_recv()
                total = sum_slots[first]
                for j in range(1, size):
                    total = total + sum_slots[first + j]
                current[...] = total
            sums_out[...] = current[...]

        running = {}

        def advance(index):
            if index in running and next(running[index], "end") == "end":
                del running[index]

        def begin(index):
            running[index] = reduce_chunk(index) if index < n_chunks else reduce_sums()
            next(running[index])

        def add(row, value):
            sums[row : row + 1, :] += jnp.sum(value, axis=0, keepdims=True)

        def vrow(i):
            return vec[i : i + 1, :]

        def features(r):
            here = pl.ds(r * length, length)
            label = labels[pl.ds(me * rows + r, 1), :]
            ids = lax.broadcasted_iota(jnp.int32, (LANES, length), 0)
            hot = jnp.where(ids == label, 1.0, 0.0)
            hot = jnp.transpose(hot)
            qfeat[here] = hot.astype(BF16)
            kfeat[here] = ((hot - 1.0) * 1e30).astype(BF16)
            real = jnp.where(jnp.broadcast_to(label, (LANES, length)) != 0, 1.0, 0.0)
            real = jnp.transpose(real)
            valid[here] = real
            sums[sums_at + S_COUNT : sums_at + S_COUNT + 1, 0:LANES] += jnp.sum(
                real, axis=0, keepdims=True
            )

        vec[0:2] = bias[...].astype(F32)
        for row, vector in enumerate((out_bias, gain1, shift1, shr_bias, gain2, shift2)):
            vec[2 + row : 3 + row] = vector[...].astype(F32).reshape(1, width)
        vec[V_EXPAND:vec_rows] = exp_bias[...].astype(F32).reshape(blocks, width)
        spread(0, 0)
        pl.semaphore_wait(barrier, greeted)
        incoming = [bring(0, x, r) for r in range(rows)]
        spread(1, group * span)
        cotangents = [bring(group * span, cot, r) for r in range(rows)]
        sent = list(started)
        sums[...] = jnp.zeros_like(sums)
        for r in range(rows):
            features(r)
        for copy in weights:
            copy.wait()

        lane = lax.broadcasted_iota(jnp.int32, (length, LANES), 1)
        first_head = lane < HEAD_DIM
        lane_row = lax.broadcasted_iota(jnp.int32, (1, LANES), 1)
        masks = [
            jnp.where(lane_row // HEAD_DIM == part, 1.0, 0.0).astype(BF16) for part in (0, 1)
        ]
        scaled = [mask * BF16(SCALE) for mask in masks]

        def mix(r):
            here = pl.ds(r * length, length)
            block = x[here]
            mixed[0, here] = (nn(block, proj[0]) + vrow(V_QUERY)).astype(BF16)
            mixed[1, here] = nn(block, proj[1]).astype(BF16)
            mixed[2, here] = (nn(block, proj[2]) + vrow(V_VALUE)).astype(BF16)

        def attend(r):
            here = pl.ds(r * length, length)

            @pl.loop(0, pairs)
            def _(pair):
                lanes = pl.ds(pl.multiple_of(pair * LANES, LANES), LANES)
                query = mixed[0, here, lanes]
                keys = jnp.concatenate([mixed[1, here, lanes], kfeat[here]], axis=1)
                values = jnp.concatenate(
                    [mixed[2, here, lanes], jnp.ones((length, LANES), BF16)], axis=1
                )
                sides = []
                for part in (0, 1):
                    wide = jnp.concatenate([query * scaled[part], qfeat[here]], axis=1)
                    scores = nt(wide, keys)
                    raised = jnp.exp(scores - jnp.max(scores, axis=1, keepdims=True)).astype(BF16)
                    probs[r * heads + 2 * pair + part] = raised
                    sides.append(nn(raised, values))
                total = jnp.where(first_head, sides[0][:, LANES:], sides[1][:, LANES:])
                mean = jnp.where(first_head, sides[0][:, :LANES], sides[1][:, :LANES])
                inv = 1.0 / total
                context[here, lanes] = (mean * inv).astype(BF16)
                inverse[here, lanes] = inv

        def wide_valid(r):
            real = valid[pl.ds(r * length, length)]
            return jnp.concatenate([real] * (width // LANES), axis=1)

        def normalize(value):
            center = value - jnp.mean(value, axis=1, keepdims=True)
            spread = jnp.mean(center * center, axis=1, keepdims=True)
            scale = lax.rsqrt(spread + EPSILON)
            return center * scale, scale

        def normalize_back(up, gain, vhat, scale):
            a = up * gain
            return (
                a
                - jnp.mean(a, axis=1, keepdims=True)
                - vhat * jnp.mean(a * vhat, axis=1, keepdims=True)
            ) * scale

        def first_half(r):
            here = pl.ds(r * length, length)
            attended = nn(context[here], outw[...]) + vrow(V_OUT)
            inputs = x[here].astype(F32)
            real = wide_valid(r)
            add(sums_at + S_INPUT, real * inputs * inputs)
            add(sums_at + S_ATTENDED, real * attended * attended)
            vhat, scale = normalize(inputs + attended)
            vhat1[here] = vhat
            rstd1[here] = jnp.broadcast_to(scale, (length, LANES))
            low1[here] = (vhat * vrow(V_GAIN1) + vrow(V_SHIFT1)).astype(BF16)

        def expand(r):
            here = pl.ds(r * length, length)

            @pl.loop(0, blocks)
            def _(c):
                upper = nt(low1[here], expw[c]) + vec[pl.ds(V_EXPAND + c, 1), :]
                value, derivative = gelu_parts(upper)
                active[c, here] = value.astype(BF16)
                slope[c, here] = derivative.astype(BF16)

        def second_half(r):
            here = pl.ds(r * length, length)
            shrunk = nn(active[0, here], shrw[0])
            for c in range(1, blocks):
                shrunk = shrunk + nn(active[c, here], shrw[c])
            shrunk = shrunk + vrow(V_SHRINK)
            add(sums_at + S_SHRUNK, wide_valid(r) * shrunk * shrunk)
            hidden = vhat1[here] * vrow(V_GAIN1) + vrow(V_SHIFT1)
            vhat, scale = normalize(hidden + shrunk)
            result[here] = (vhat * vrow(V_GAIN2) + vrow(V_SHIFT2)).astype(BF16)
            up = cot[here].astype(F32)
            add(V_GAIN2, up * vhat)
            add(V_SHIFT2, up)
            grad = normalize_back(up, vrow(V_GAIN2), vhat, scale)
            second[here] = grad
            low = grad.astype(BF16)
            shrunk_low[here] = low
            add(V_SHRINK, low.astype(F32))

        ones = jnp.ones((8, own_tokens), BF16)

        def expand_back(c):
            for r in range(rows):
                here = pl.ds(r * length, length)
                grad = nt(shrunk_low[here], shrw[c])
                slope[c, here] = (grad * slope[c, here].astype(F32)).astype(BF16)
            base = 2 * width * c
            upper_grad = slope[c]
            grads[base : base + width] = tn(upper_grad, low1[...]).astype(BF16)
            begin(2 * c)
            grads[base + width : base + 2 * width] = tn(active[c], shrunk_low[...]).astype(BF16)
            begin(2 * c + 1)
            sums[V_EXPAND + c : V_EXPAND + c + 1, :] = nn(ones, upper_grad)[0:1]

        def first_half_back(r):
            here = pl.ds(r * length, length)
            up = second[here]
            for c in range(blocks):
                up = up + nn(slope[c, here], expw[c])
            vhat = vhat1[here]
            add(V_GAIN1, up * vhat)
            add(V_SHIFT1, up)
            grad = normalize_back(up, vrow(V_GAIN1), vhat, rstd1[here][:, 0:1])
            second[here] = grad
            low = grad.astype(BF16)
            attended_low[here] = low
            add(V_OUT, low.astype(F32))
            context_grad[here] = nt(low, outw[...]).astype(BF16)

        def attend_back(r, pair):
            here = pl.ds(r * length, length)
            lanes = pl.ds(pair * LANES, LANES)
            query, keys, values = (mixed[j, here, lanes] for j in range(3))
            up = (context_grad[here, lanes].astype(F32) * inverse[here, lanes]).astype(BF16)
            inner = up.astype(F32) * context[here, lanes].astype(F32)
            sides = []
            for part in (0, 1):
                raised = probs[r * heads + 2 * pair + part]
                mine = first_head if part == 0 else jnp.logical_not(first_head)
                delta = jnp.sum(jnp.where(mine, inner, 0.0), axis=1, keepdims=True)
                dprobs = nt(up * masks[part], values)
                score = (raised.astype(F32) * (dprobs - delta)).astype(BF16)
                sides.append((nn(score, keys), tn(score, query), tn(raised, up)))
            for j, factor in enumerate((SCALE, SCALE, 1.0)):
                both = jnp.where(first_head, sides[0][j], sides[1][j])
                mixed[j, here, lanes] = (both * factor).astype(BF16)

        def tokens_back(r):
            here = pl.ds(r * length, length)
            grad = second[here]
            for j in range(3):
                grad = grad + nt(mixed[j, here], proj[j])
            low1[here] = grad.astype(BF16)

        def out_back():
            base = 2 * blocks * width
            grads[base : base + width] = tn(context[...], attended_low[...]).astype(BF16)
            begin(2 * blocks)

        def mix_back(j):
            base = (2 * blocks + 1 + j) * width
            grads[base : base + width] = tn(x[...], mixed[j]).astype(BF16)
            begin(2 * blocks + 1 + j)

        def sums_back():
            for row, j in ((V_QUERY, 0), (V_VALUE, 2)):
                sums[row : row + 1, :] = nn(ones, mixed[j])[0:1]
            begin(n_chunks)

        returned = []

        def give_back(r):
            tokens_back(r)
            returned.append(deliver(low1, tgrad_in, r))

        for r in range(rows):
            arrive(incoming[r])
            mix(r)
            attend(r)
            first_half(r)
            expand(r)
        results = []
        for r in range(rows):
            arrive(cotangents[r])
            second_half(r)
        for copy in sent:
            copy.wait_send()

        def show(r):
            results.append(deliver(result, result_in, r))

        units = []
        for c in range(blocks):
            units.append(lambda c=c: expand_back(c))
        units += [lambda r=r: first_half_back(r) for r in range(rows)]
        units.append(out_back)
        for r in range(rows):
            units += [lambda r=r, pair=pair: attend_back(r, pair) for pair in range(pairs)]
        units += [lambda j=j: mix_back(j) for j in range(3)]
        units.append(sums_back)
        units += [lambda r=r: give_back(r) for r in range(rows)]
        late = {SHOW: lambda: [show(r) for r in range(rows)]}
        for index in PLAN:
            if index == UNIT:
                if units:
                    units.pop(0)()
            elif index in late:
                late.pop(index)()
            else:
                advance(index)
        for unit in units + list(late.values()):
            unit()
        while running:
            for index in list(running):
                advance(index)
        for copies in results + returned:
            arrive(copies)
        for copy in started[len(sent) :]:
            copy.wait_send()
        for copy in kept:
            copy.wait()

    hbm = pl.BlockSpec(memory_space=pl.ANY)
    vmem = pl.BlockSpec(memory_space=pltpu.VMEM)
    big = (own_tokens, width)
    result, tokens_grad, exp_grad, shr_grad, out_grad, proj_grad, sums = pl.pallas_call(
        kernel,
        out_shape=(
            jax.ShapeDtypeStruct((group, span, width), BF16),
            jax.ShapeDtypeStruct((group, span, width), BF16),
            jax.ShapeDtypeStruct((hidden_units, width), BF16),
            jax.ShapeDtypeStruct((hidden_units, width), BF16),
            jax.ShapeDtypeStruct((width, width), BF16),
            jax.ShapeDtypeStruct((3 * width, width), BF16),
            jax.ShapeDtypeStruct((sum_rows, width), F32),
        ),
        in_specs=[hbm, hbm, vmem, hbm, hbm, hbm, hbm, *([vmem] * 8)],
        out_specs=(*([hbm] * 6), vmem),
        scratch_shapes=[
            pltpu.VMEM((2, span, group, width), BF16),
            pltpu.VMEM((sum_rows, width), F32),
            pltpu.VMEM(big, BF16),
            pltpu.VMEM(big, BF16),
            pltpu.VMEM((3, width, width), BF16),
            pltpu.VMEM((width, width), BF16),
            pltpu.VMEM((blocks, width, width), BF16),
            pltpu.VMEM((blocks, width, width), BF16),
            pltpu.VMEM((3, *big), BF16),
            pltpu.VMEM((rows * heads, length, length), BF16),
            pltpu.VMEM(big, BF16),
            pltpu.VMEM(big, F32),
            pltpu.VMEM(big, F32),
            pltpu.VMEM((own_tokens, LANES), F32),
            pltpu.VMEM(big, BF16),
            pltpu.VMEM((blocks, *big), BF16),
            pltpu.VMEM((blocks, *big), BF16),
            pltpu.VMEM(big, F32),
            pltpu.VMEM(big, BF16),
            pltpu.VMEM(big, BF16),
            pltpu.VMEM((own_tokens, LANES), F32),
            pltpu.VMEM((own_tokens, LANES), BF16),
            pltpu.VMEM((own_tokens, LANES), BF16),
            pltpu.VMEM((grad_rows, width), BF16),
            pltpu.VMEM((slot_rows, width), BF16),
            pltpu.VMEM((sum_rows, width), F32),
            pltpu.VMEM((sum(size for _, _, size in levels.values()), sum_rows, width), F32),
            pltpu.SemaphoreType.DMA((n_remote,)),
            pltpu.SemaphoreType.DMA((n_remote,)),
            pltpu.SemaphoreType.DMA((n_local,)),
        ],
        compiler_params=pltpu.CompilerParams(
            collective_id=0, has_side_effects=True, vmem_limit_bytes=62 * 2**20
        ),
    )(
        tokens,
        cotangent,
        jnp.transpose(segments),
        jnp.transpose(projections, (1, 0, 2)),
        outweight,
        expander.reshape(blocks, width, width),
        shrinker.reshape(blocks, width, width),
        projbias,
        outbias,
        normgain,
        normshift,
        expandbias,
        shrinkbias,
        finalgain,
        finalshift,
    )
    def finish(
        result_in,
        tgrad_in,
        exp_low,
        shr_low,
        out_low,
        proj_low,
        totals,
        result_out,
        tgrad_out,
        proj_out,
        bias_out,
        out_out,
        out_bias_out,
        gain1_out,
        shift1_out,
        exp_out,
        exp_bias_out,
        shr_out,
        shr_bias_out,
        gain2_out,
        shift2_out,
        rms_out,
        turned_in,
        turned,
        low,
        full,
        in_sem,
        out_sem,
    ):
        pieces = []
        for c in range(blocks):
            here = pl.ds(c * width, width)
            pieces.append((exp_low.at[here], exp_out.at[here]))
        for c in range(blocks):
            here = pl.ds(c * width, width)
            pieces.append((shr_low.at[here], shr_out.at[here]))
        for j in range(3):
            pieces.append((proj_low.at[pl.ds(j * width, width)], proj_out.at[j]))
        pieces.append((out_low, out_out))
        loads = []
        for i, (src, _) in enumerate(pieces):
            loads.append(pltpu.make_async_copy(src, low.at[i], in_sem.at[i]))
        for i, src in enumerate((result_in, tgrad_in)):
            loads.append(pltpu.make_async_copy(src, turned_in.at[i], in_sem.at[n_chunks + i]))
        for load in loads:
            load.start()
        bias_out[...] = totals[V_QUERY : V_VALUE + 1]
        for row, out in (
            (V_OUT, out_bias_out),
            (V_GAIN1, gain1_out),
            (V_SHIFT1, shift1_out),
            (V_SHRINK, shr_bias_out),
            (V_GAIN2, gain2_out),
            (V_SHIFT2, shift2_out),
        ):
            out[...] = totals[row]
        exp_bias_out[...] = totals[V_EXPAND : V_EXPAND + blocks].reshape(hidden_units)
        squares = jnp.sum(totals[sums_at : sums_at + 4], axis=1, keepdims=True)
        count = totals[sums_at + S_COUNT : sums_at + S_COUNT + 1, 0:1] * width
        roots = jnp.sqrt(squares / count)
        lane = lax.broadcasted_iota(jnp.int32, (4, LANES), 1)
        row = lax.broadcasted_iota(jnp.int32, (4, LANES), 0)
        line = jnp.sum(jnp.where(lane == row, roots, 0.0), axis=0)
        rms_out[...] = line[0:3]
        stores = []
        for i, (_, dst) in enumerate(pieces):
            loads[i].wait()
            full[i] = low[i].astype(F32)
            stores.append(pltpu.make_async_copy(full.at[i], dst, out_sem.at[i]))
            stores[-1].start()
        for i, dst in enumerate((result_out, tgrad_out)):
            loads[n_chunks + i].wait()
            turned[i] = jnp.swapaxes(turned_in[i], 0, 1)
            stores.append(pltpu.make_async_copy(turned.at[i], dst, out_sem.at[n_chunks + i]))
            stores[-1].start()
        for store in stores:
            store.wait()

    vector = jax.ShapeDtypeStruct((width,), F32)
    square = (n_chunks, width, width)
    outs = pl.pallas_call(
        finish,
        out_shape=(
            jax.ShapeDtypeStruct((span, group, width), BF16),
            jax.ShapeDtypeStruct((span, group, width), BF16),
            jax.ShapeDtypeStruct((3, width, width), F32),
            jax.ShapeDtypeStruct((2, width), F32),
            jax.ShapeDtypeStruct((width, width), F32),
            vector,
            vector,
            vector,
            jax.ShapeDtypeStruct((hidden_units, width), F32),
            jax.ShapeDtypeStruct((hidden_units,), F32),
            jax.ShapeDtypeStruct((hidden_units, width), F32),
            vector,
            vector,
            vector,
            jax.ShapeDtypeStruct((3,), F32),
        ),
        in_specs=[*([hbm] * 6), vmem],
        out_specs=(hbm, hbm, hbm, vmem, hbm, vmem, vmem, vmem, hbm, vmem, hbm, *([vmem] * 4)),
        scratch_shapes=[
            pltpu.VMEM((2, group, span, width), BF16),
            pltpu.VMEM((2, span, group, width), BF16),
            pltpu.VMEM(square, BF16),
            pltpu.VMEM(square, F32),
            pltpu.SemaphoreType.DMA((n_chunks + 2,)),
            pltpu.SemaphoreType.DMA((n_chunks + 2,)),
        ],
        compiler_params=pltpu.CompilerParams(vmem_limit_bytes=62 * 2**20),
    )(result, tokens_grad, exp_grad, shr_grad, out_grad, proj_grad, sums)
    outs = list(outs)
    outs[2] = jnp.transpose(outs[2], (1, 0, 2))
    return tuple(outs)


def solution(mesh):
    split = P("seq", "dp", None)
    placed = (split, P(None, "dp"), *([P()] * 12), split)
    return jax.shard_map(
        local,
        mesh=mesh,
        in_specs=placed,
        out_specs=(split, split, *([P()] * 13)),
        check_vma=False,
    )
```

```python
import jax
import jax.numpy as jnp
from jax import lax
from jax.experimental import pallas as pl
from jax.experimental.pallas import tpu as pltpu
from jax.sharding import PartitionSpec as P

HEAD_DIM = 64
EPSILON = 1e-12
LANES = 128
F32 = jnp.float32
BF16 = jnp.bfloat16
SCALE = HEAD_DIM ** (-0.5)

(V_QUERY, V_VALUE, V_OUT, V_GAIN1, V_SHIFT1, V_SHRINK, V_GAIN2, V_SHIFT2, V_EXPAND) = range(9)
(S_INPUT, S_ATTENDED, S_SHRUNK, S_COUNT) = range(4)


ORDERS = (
    ("core", "side", "near", "far"),
    ("core", "near", "side", "far"),
    ("core", "far", "near", "side"),
    ("core", "near", "far", "side"),
)
CLASSES = (1, 3, 2, 2, 1, 3, 1, 1, 0, 1, 1, 0)
UNIT, SHOW = -1, -2
PLAN = (
    UNIT, UNIT, UNIT, 0, 1, 3, 4, 5, 2, UNIT, 0, UNIT, 6, 7, 1, 0, 3, UNIT, 4, UNIT, UNIT,
    SHOW, 5, 2, UNIT, 8, 6, 4, 1, 7, 0, 3, 2, UNIT, 5, UNIT, 4, 0, UNIT, UNIT, UNIT, 4, UNIT,
    UNIT, 8, UNIT, 6, 1, UNIT, 9, 7, 10, 8, 5, 6, 11, 0, 1, 7, 5, 9, 8, 4, 3, 6, 2, 10, 11,
    UNIT, 1, 9, 0, 3, 7, 6, 2, 12, UNIT, 10, 5, 4, 11, 8, 7, 0, 9, 12, UNIT, 10, 1, 4, 11, 3,
    12, 9, 6, 2, 1, 10, 12, 11, 6, 5, 8, 5, 9, 7, 3, 10, 11, 7, 3, 8, 9, 2, 11, 8, 10, 9, 2,
    11, 10,
)


def nn(a, b):
    return lax.dot_general(a, b, (((1,), (0,)), ((), ())), preferred_element_type=F32)


def nt(a, b):
    return lax.dot_general(a, b, (((1,), (1,)), ((), ())), preferred_element_type=F32)


def tn(a, b):
    return lax.dot_general(a, b, (((0,), (0,)), ((), ())), preferred_element_type=F32)


def gelu_parts(u):
    phi = 0.5 + 0.5 * lax.erf(u * 0.5**0.5)
    density = jnp.exp2((u * (-0.5 * 1.4426950408889634)) * u)
    return u * phi, phi + (0.3989422804014327 * u) * density


def levels_of(n_seq, n_dp):
    low = 2 if n_seq % 2 == 0 else 1
    near = 1
    while 4 * near * near <= n_dp and n_dp % (2 * near) == 0:
        near *= 2
    return {
        "core": ("seq", 1, low),
        "side": ("seq", low, n_seq // low),
        "near": ("dp", 1, near),
        "far": ("dp", near, n_dp // near),
    }


def slots_of(levels, order, rows):
    total = 0
    for name in order:
        size = levels[name][2]
        if size == 1:
            continue
        if rows % (16 * size) == 0:
            rows //= size
            total += (size - 1) * rows
        else:
            total += size * rows
    return total


def local(
    tokens,
    segments,
    projections,
    projbias,
    outweight,
    outbias,
    normgain,
    normshift,
    expander,
    expandbias,
    shrinker,
    shrinkbias,
    finalgain,
    finalshift,
    cotangent,
):
    n_seq, n_dp = lax.axis_size("seq"), lax.axis_size("dp")
    span, group, width = tokens.shape
    length = segments.shape[0]
    rows = group // n_seq
    hidden_units = expander.shape[0]
    blocks = hidden_units // width
    heads = width // HEAD_DIM
    pairs = width // LANES
    own_tokens = rows * length
    levels = levels_of(n_seq, n_dp)
    n_chunks = 2 * blocks + 4
    chunk_orders = [ORDERS[CLASSES[i % len(CLASSES)]] for i in range(n_chunks)]
    slot_bases, slot_rows = [], 0
    for order in chunk_orders:
        slot_bases.append(slot_rows)
        slot_rows += slots_of(levels, order, width)
    grad_rows = n_chunks * width
    vec_rows = V_EXPAND + blocks
    sum_rows = -(-(vec_rows + 4) // 8) * 8
    sums_at = vec_rows
    ring = sum(size - 1 for _, _, size in levels.values())
    n_remote = 4 * rows * (n_seq - 1) + n_chunks * 2 * ring + ring
    n_local = 8 + 4 * rows + n_chunks

    def kernel(
        tok_hbm,
        cot_hbm,
        labels,
        proj_hbm,
        out_hbm,
        exp_hbm,
        shr_hbm,
        bias,
        out_bias,
        gain1,
        shift1,
        exp_bias,
        shr_bias,
        gain2,
        shift2,
        result_in,
        tgrad_in,
        exp_grad,
        shr_grad,
        out_grad,
        proj_grad,
        sums_out,
        raw,
        vec,
        x,
        cot,
        proj,
        outw,
        expw,
        shrw,
        mixed,
        probs,
        context,
        inverse,
        vhat1,
        rstd1,
        low1,
        active,
        slope,
        second,
        shrunk_low,
        qfeat,
        grads,
        slots,
        sums,
        sum_slots,
        send_sem,
        recv_sem,
        local_sem,
    ):
        me = lax.axis_index("seq")
        attended_low, context_grad = shrunk_low, cot
        shown_at = (n_chunks - 3) * width
        started, counters = [], {"remote": 0, "local": 0}

        def remote(src, dst, where):
            i = counters["remote"]
            counters["remote"] += 1
            copy = pltpu.make_async_remote_copy(
                src_ref=src,
                dst_ref=dst,
                send_sem=send_sem.at[i],
                recv_sem=recv_sem.at[i],
                device_id=where,
                device_id_type=pl.DeviceIdType.MESH,
            )
            copy.start()
            started.append(copy)
            return copy

        def near_copy(src, dst):
            i = counters["local"]
            counters["local"] += 1
            copy = pltpu.make_async_copy(src, dst, local_sem.at[i])
            copy.start()
            return copy

        def place(name):
            axis, stride, size = levels[name]
            index = lax.axis_index(axis)
            mine = lax.rem(lax.div(index, stride), size)
            return axis, index, stride, size, mine

        arriving = [near_copy(tok_hbm, raw)]
        weights = [
            near_copy(proj_hbm, proj),
            near_copy(out_hbm, outw),
            near_copy(exp_hbm, expw),
            near_copy(shr_hbm, shrw),
        ]

        barrier = pltpu.get_barrier_semaphore()
        greeted = 0
        for j in range(1, n_seq):
            pl.semaphore_signal(
                barrier,
                inc=1,
                device_id={"seq": lax.rem(me + j, n_seq)},
                device_id_type=pl.DeviceIdType.MESH,
            )
            greeted += 1
        for name in ("near", "far"):
            axis, index, stride, size, mine = place(name)
            for j in range(1, size):
                k = lax.rem(mine + j, size)
                pl.semaphore_signal(
                    barrier,
                    inc=1,
                    device_id={axis: index + (k - mine) * stride},
                    device_id_type=pl.DeviceIdType.MESH,
                )
                greeted += 1

        def bring(base, dst, r):
            here = pl.ds(pl.multiple_of(r * length + me * span, 16), span)
            far = []
            for j in sorted(range(1, n_seq), key=lambda j: j % 2):
                k = lax.rem(me + j, n_seq)
                src = grads.at[pl.ds(pl.multiple_of(base + (k * rows + r) * span, 16), span)]
                far.append(remote(src, dst.at[here], {"seq": k}))
            own = pl.ds(pl.multiple_of(base + (me * rows + r) * span, 16), span)
            dst[here] = grads[own]
            return far

        def deliver(src, dst, r):
            far = []
            for j in sorted(range(1, n_seq), key=lambda j: j % 2):
                k = lax.rem(me + j, n_seq)
                piece = src.at[pl.ds(pl.multiple_of(r * length + k * span, 16), span)]
                far.append(remote(piece, dst.at[me * rows + r], {"seq": k}))
            own = pl.ds(pl.multiple_of(r * length + me * span, 16), span)
            kept.append(near_copy(src.at[own], dst.at[me * rows + r]))
            return far

        kept = []

        def arrive(copies):
            for copy in copies:
                copy.wait_recv()

        def spread(index, base):
            arriving[index].wait()
            turned = jnp.swapaxes(raw[...], 0, 1)
            grads[base : base + group * span] = turned.reshape(group * span, width)

        goals = []
        for c in range(blocks):
            goals += [(exp_grad, c * width), (shr_grad, c * width)]
        goals.append((out_grad, 0))
        goals += [(proj_grad, j * width) for j in range(3)]

        def reduce_chunk(index):
            base, count = index * width, width
            written = []
            at, slot, stack = base, slot_bases[index], []
            goal, goal_row = goals[index]
            offset = goal_row - base
            for name in chunk_orders[index]:
                axis, own, stride, size, mine = place(name)
                if size == 1:
                    continue
                copies = []
                if count % (16 * size) == 0:
                    piece = count // size
                    for j in range(1, size):
                        k = lax.rem(mine + j, size)
                        copies.append(
                            remote(
                                grads.at[pl.ds(pl.multiple_of(at + k * piece, 16), piece)],
                                slots.at[pl.ds(slot + (j - 1) * piece, piece)],
                                {axis: own + (k - mine) * stride},
                            )
                        )
                    yield
                    here = pl.multiple_of(at + mine * piece, 16)
                    for copy in copies:
                        copy.wait_recv()
                    total = grads[pl.ds(here, piece)].astype(F32)
                    for j in range(size - 1):
                        total = total + slots[pl.ds(slot + j * piece, piece)].astype(F32)
                    grads[pl.ds(here, piece)] = total.astype(BF16)
                    stack.append((name, at, piece))
                    slot += (size - 1) * piece
                    at, count = here, piece
                else:
                    mine_slot = pl.ds(pl.multiple_of(slot + mine * count, 16), count)
                    slots[mine_slot] = grads[pl.ds(at, count)]
                    for j in range(1, size):
                        k = lax.rem(mine + j, size)
                        copies.append(
                            remote(
                                slots.at[mine_slot],
                                slots.at[mine_slot],
                                {axis: own + (k - mine) * stride},
                            )
                        )
                    yield
                    for copy in copies:
                        copy.wait_recv()
                    total = jnp.zeros((count, width), F32)
                    for j in range(size):
                        total = total + slots[pl.ds(slot + j * count, count)].astype(F32)
                    grads[pl.ds(at, count)] = total.astype(BF16)
                    slot += size * count
            block, copies = grads.at[pl.ds(at, count)], []
            written.append(near_copy(block, goal.at[pl.ds(pl.multiple_of(at + offset, 16), count)]))
            for name, before, piece in reversed(stack):
                axis, own, stride, size, mine = place(name)
                target = goal.at[pl.ds(pl.multiple_of(at + offset, 16), piece)]
                copies = []
                for j in range(1, size):
                    k = lax.rem(mine + j, size)
                    copies.append(remote(block, target, {axis: own + (k - mine) * stride}))
                yield
                for copy in copies:
                    copy.wait_recv()
                if written:
                    written.pop().wait()
                count = piece * size
                at, block = before, goal.at[pl.ds(pl.multiple_of(before + offset, 16), count)]
            if written:
                written.pop().wait()

        def reduce_sums():
            current = sums
            for step, name in enumerate(("core", "side", "near", "far")):
                axis, own, stride, size, mine = place(name)
                if size == 1:
                    continue
                first = sum(levels[n][2] for n in ("core", "side", "near", "far")[:step])
                sum_slots[first + mine] = current[...]
                copies = []
                for j in range(1, size):
                    k = lax.rem(mine + j, size)
                    block = sum_slots.at[first + mine]
                    copies.append(remote(block, block, {axis: own + (k - mine) * stride}))
                yield
                for copy in copies:
                    copy.wait_recv()
                total = sum_slots[first]
                for j in range(1, size):
                    total = total + sum_slots[first + j]
                current[...] = total
            sums_out[...] = current[...]

        running = {}

        def advance(index):
            if index in running and next(running[index], "end") == "end":
                del running[index]

        def begin(index):
            running[index] = reduce_chunk(index) if index < n_chunks else reduce_sums()
            next(running[index])

        def add(row, value):
            sums[row : row + 1, :] += jnp.sum(value, axis=0, keepdims=True)

        def vrow(i):
            return vec[i : i + 1, :]

        def features(r):
            here = pl.ds(r * length, length)
            label = labels[pl.ds(me * rows + r, 1), :]
            ids = lax.broadcasted_iota(jnp.int32, (LANES, length), 0)
            hot = jnp.where(ids == label, 1.0, 0.0)
            hot = jnp.transpose(hot)
            qfeat[here] = hot.astype(BF16)
            real = 1.0 - hot[:, 0:1]
            sums[sums_at + S_COUNT : sums_at + S_COUNT + 1, 0:LANES] += jnp.sum(
                jnp.broadcast_to(real, (length, LANES)), axis=0, keepdims=True
            )

        vec[0:2] = bias[...].astype(F32)
        for row, vector in enumerate((out_bias, gain1, shift1, shr_bias, gain2, shift2)):
            vec[2 + row : 3 + row] = vector[...].astype(F32).reshape(1, width)
        vec[V_EXPAND:vec_rows] = exp_bias[...].astype(F32).reshape(blocks, width)
        spread(0, 0)
        arriving.append(near_copy(cot_hbm, raw))
        pl.semaphore_wait(barrier, greeted)
        incoming = [bring(0, x, r) for r in range(rows)]
        spread(1, group * span)
        cotangents = [bring(group * span, cot, r) for r in range(rows)]
        sent = list(started)
        sums[...] = jnp.zeros_like(sums)
        for r in range(rows):
            features(r)
        for copy in weights:
            copy.wait()

        lane = lax.broadcasted_iota(jnp.int32, (length, LANES), 1)
        first_head = lane < HEAD_DIM
        lane_row = lax.broadcasted_iota(jnp.int32, (1, LANES), 1)
        masks = [
            jnp.where(lane_row // HEAD_DIM == part, 1.0, 0.0).astype(BF16) for part in (0, 1)
        ]
        scaled = [mask * BF16(SCALE) for mask in masks]

        def mix(r):
            here = pl.ds(r * length, length)
            block = x[here]
            mixed[0, here] = (nn(block, proj[0]) + vrow(V_QUERY)).astype(BF16)
            mixed[1, here] = nn(block, proj[1]).astype(BF16)
            mixed[2, here] = (nn(block, proj[2]) + vrow(V_VALUE)).astype(BF16)

        def attend(r):
            here = pl.ds(r * length, length)

            apart = ((qfeat[here].astype(F32) - 1.0) * 1e30).astype(BF16)
            for pair in range(pairs):
                lanes = pl.ds(pair * LANES, LANES)
                query = mixed[0, here, lanes]
                keys = jnp.concatenate([mixed[1, here, lanes], apart], axis=1)
                values = jnp.concatenate(
                    [mixed[2, here, lanes], jnp.ones((length, LANES), BF16)], axis=1
                )
                sides = []
                for part in (0, 1):
                    wide = jnp.concatenate([query * scaled[part], qfeat[here]], axis=1)
                    scores = nt(wide, keys)
                    raised = jnp.exp(scores - jnp.max(scores, axis=1, keepdims=True)).astype(BF16)
                    probs[r * heads + 2 * pair + part] = raised
                    sides.append(nn(raised, values))
                total = jnp.where(first_head, sides[0][:, LANES:], sides[1][:, LANES:])
                mean = jnp.where(first_head, sides[0][:, :LANES], sides[1][:, :LANES])
                inv = 1.0 / total
                context[here, lanes] = (mean * inv).astype(BF16)
                inverse[here, lanes] = inv

        def wide_valid(r):
            return 1.0 - qfeat[pl.ds(r * length, length)].astype(F32)[:, 0:1]

        def normalize(value):
            center = value - jnp.mean(value, axis=1, keepdims=True)
            spread = jnp.mean(center * center, axis=1, keepdims=True)
            scale = lax.rsqrt(spread + EPSILON)
            return center * scale, scale

        def normalize_back(up, gain, vhat, scale):
            a = up * gain
            return (
                a
                - jnp.mean(a, axis=1, keepdims=True)
                - vhat * jnp.mean(a * vhat, axis=1, keepdims=True)
            ) * scale

        def first_half(r):
            here = pl.ds(r * length, length)
            attended = nn(context[here], outw[...]) + vrow(V_OUT)
            inputs = x[here].astype(F32)
            real = wide_valid(r)
            add(sums_at + S_INPUT, real * inputs * inputs)
            add(sums_at + S_ATTENDED, real * attended * attended)
            vhat, scale = normalize(inputs + attended)
            vhat1[here] = vhat
            rstd1[here] = jnp.broadcast_to(scale, (length, LANES))
            low1[here] = (vhat * vrow(V_GAIN1) + vrow(V_SHIFT1)).astype(BF16)

        def expand(r):
            here = pl.ds(r * length, length)

            for c in range(blocks):
                upper = nt(low1[here], expw[c]) + vrow(V_EXPAND + c)
                value, derivative = gelu_parts(upper)
                active[c, here] = value.astype(BF16)
                slope[c, here] = derivative.astype(BF16)

        def second_half(r):
            here = pl.ds(r * length, length)
            shrunk = nn(active[0, here], shrw[0])
            for c in range(1, blocks):
                shrunk = shrunk + nn(active[c, here], shrw[c])
            shrunk = shrunk + vrow(V_SHRINK)
            add(sums_at + S_SHRUNK, wide_valid(r) * shrunk * shrunk)
            hidden = vhat1[here] * vrow(V_GAIN1) + vrow(V_SHIFT1)
            vhat, scale = normalize(hidden + shrunk)
            there = pl.ds(shown_at + r * length, length)
            grads[there] = (vhat * vrow(V_GAIN2) + vrow(V_SHIFT2)).astype(BF16)
            up = cot[here].astype(F32)
            add(V_GAIN2, up * vhat)
            add(V_SHIFT2, up)
            grad = normalize_back(up, vrow(V_GAIN2), vhat, scale)
            second[here] = grad
            low = grad.astype(BF16)
            shrunk_low[here] = low
            add(V_SHRINK, low.astype(F32))

        ones = jnp.ones((8, own_tokens), BF16)

        def expand_back(c):
            for r in range(rows):
                here = pl.ds(r * length, length)
                grad = nt(shrunk_low[here], shrw[c])
                slope[c, here] = (grad * slope[c, here].astype(F32)).astype(BF16)
            base = 2 * width * c
            upper_grad = slope[c]
            grads[base : base + width] = tn(upper_grad, low1[...]).astype(BF16)
            begin(2 * c)
            grads[base + width : base + 2 * width] = tn(active[c], shrunk_low[...]).astype(BF16)
            begin(2 * c + 1)
            sums[V_EXPAND + c : V_EXPAND + c + 1, :] = nn(ones, upper_grad)[0:1]

        def first_half_back(r):
            here = pl.ds(r * length, length)
            up = second[here]
            for c in range(blocks):
                up = up + nn(slope[c, here], expw[c])
            vhat = vhat1[here]
            add(V_GAIN1, up * vhat)
            add(V_SHIFT1, up)
            grad = normalize_back(up, vrow(V_GAIN1), vhat, rstd1[here][:, 0:1])
            second[here] = grad
            low = grad.astype(BF16)
            attended_low[here] = low
            add(V_OUT, low.astype(F32))
            context_grad[here] = nt(low, outw[...]).astype(BF16)

        def attend_back(r, pair):
            here = pl.ds(r * length, length)
            lanes = pl.ds(pair * LANES, LANES)
            query, keys, values = (mixed[j, here, lanes] for j in range(3))
            up = (context_grad[here, lanes].astype(F32) * inverse[here, lanes]).astype(BF16)
            inner = up.astype(F32) * context[here, lanes].astype(F32)
            sides = []
            for part in (0, 1):
                raised = probs[r * heads + 2 * pair + part]
                mine = first_head if part == 0 else jnp.logical_not(first_head)
                delta = jnp.sum(jnp.where(mine, inner, 0.0), axis=1, keepdims=True)
                dprobs = nt(up * masks[part], values)
                score = (raised.astype(F32) * (dprobs - delta)).astype(BF16)
                sides.append((nn(score, keys), tn(score, query), tn(raised, up)))
            for j, factor in enumerate((SCALE, SCALE, 1.0)):
                both = jnp.where(first_head, sides[0][j], sides[1][j])
                mixed[j, here, lanes] = (both * factor).astype(BF16)

        def tokens_back(r):
            here = pl.ds(r * length, length)
            grad = second[here]
            for j in range(3):
                grad = grad + nt(mixed[j, here], proj[j])
            low1[here] = grad.astype(BF16)

        def out_back():
            base = 2 * blocks * width
            grads[base : base + width] = tn(context[...], attended_low[...]).astype(BF16)
            begin(2 * blocks)

        def mix_back(j):
            if j == 0:
                for copies in results:
                    for copy in copies:
                        copy.wait_send()
                        shown.append(copy)
                while kept:
                    kept.pop().wait()
            base = (2 * blocks + 1 + j) * width
            grads[base : base + width] = tn(x[...], mixed[j]).astype(BF16)
            begin(2 * blocks + 1 + j)

        def sums_back():
            for row, j in ((V_QUERY, 0), (V_VALUE, 2)):
                sums[row : row + 1, :] = nn(ones, mixed[j])[0:1]
            begin(n_chunks)

        returned, shown = [], []

        def give_back(r):
            tokens_back(r)
            returned.append(deliver(low1, tgrad_in, r))

        for r in range(rows):
            arrive(incoming[r])
            mix(r)
            attend(r)
            first_half(r)
            expand(r)
        results = []
        for r in range(rows):
            arrive(cotangents[r])
            second_half(r)
        for copy in sent:
            copy.wait_send()

        def show(r):
            results.append(deliver(grads.at[pl.ds(shown_at, own_tokens)], result_in, r))

        units = []
        for c in range(blocks):
            units.append(lambda c=c: expand_back(c))
        units += [lambda r=r: first_half_back(r) for r in range(rows)]
        units.append(out_back)
        for r in range(rows):
            units += [lambda r=r, pair=pair: attend_back(r, pair) for pair in range(pairs)]
        units += [lambda j=j: mix_back(j) for j in range(3)]
        units.append(sums_back)
        units += [lambda r=r: give_back(r) for r in range(rows)]
        late = {SHOW: lambda: [show(r) for r in range(rows)]}
        for index in PLAN:
            if index == UNIT:
                if units:
                    units.pop(0)()
            elif index in late:
                late.pop(index)()
            else:
                advance(index)
        for unit in list(late.values()) + units:
            unit()
        while running:
            for index in list(running):
                advance(index)
        for copies in results + returned:
            arrive(copies)
        for copy in started[len(sent) :]:
            if all(copy is not other for other in shown):
                copy.wait_send()
        for copy in kept:
            copy.wait()

    hbm = pl.BlockSpec(memory_space=pl.ANY)
    vmem = pl.BlockSpec(memory_space=pltpu.VMEM)
    big = (own_tokens, width)
    result, tokens_grad, exp_grad, shr_grad, out_grad, proj_grad, sums = pl.pallas_call(
        kernel,
        out_shape=(
            jax.ShapeDtypeStruct((group, span, width), BF16),
            jax.ShapeDtypeStruct((group, span, width), BF16),
            jax.ShapeDtypeStruct((hidden_units, width), BF16),
            jax.ShapeDtypeStruct((hidden_units, width), BF16),
            jax.ShapeDtypeStruct((width, width), BF16),
            jax.ShapeDtypeStruct((3 * width, width), BF16),
            jax.ShapeDtypeStruct((sum_rows, width), F32),
        ),
        in_specs=[hbm, hbm, vmem, hbm, hbm, hbm, hbm, *([vmem] * 8)],
        out_specs=(*([hbm] * 6), vmem),
        scratch_shapes=[
            pltpu.VMEM((span, group, width), BF16),
            pltpu.VMEM((sum_rows, width), F32),
            pltpu.VMEM(big, BF16),
            pltpu.VMEM(big, BF16),
            pltpu.VMEM((3, width, width), BF16),
            pltpu.VMEM((width, width), BF16),
            pltpu.VMEM((blocks, width, width), BF16),
            pltpu.VMEM((blocks, width, width), BF16),
            pltpu.VMEM((3, *big), BF16),
            pltpu.VMEM((rows * heads, length, length), BF16),
            pltpu.VMEM(big, BF16),
            pltpu.VMEM(big, F32),
            pltpu.VMEM(big, F32),
            pltpu.VMEM((own_tokens, LANES), F32),
            pltpu.VMEM(big, BF16),
            pltpu.VMEM((blocks, *big), BF16),
            pltpu.VMEM((blocks, *big), BF16),
            pltpu.VMEM(big, F32),
            pltpu.VMEM(big, BF16),
            pltpu.VMEM((own_tokens, LANES), BF16),
            pltpu.VMEM((grad_rows, width), BF16),
            pltpu.VMEM((slot_rows, width), BF16),
            pltpu.VMEM((sum_rows, width), F32),
            pltpu.VMEM((sum(size for _, _, size in levels.values()), sum_rows, width), F32),
            pltpu.SemaphoreType.DMA((n_remote,)),
            pltpu.SemaphoreType.DMA((n_remote,)),
            pltpu.SemaphoreType.DMA((n_local,)),
        ],
        compiler_params=pltpu.CompilerParams(
            collective_id=0, has_side_effects=True, vmem_limit_bytes=63 * 2**20
        ),
    )(
        tokens,
        cotangent,
        jnp.transpose(segments),
        jnp.transpose(projections, (1, 0, 2)),
        outweight,
        expander.reshape(blocks, width, width),
        shrinker.reshape(blocks, width, width),
        projbias,
        outbias,
        normgain,
        normshift,
        expandbias,
        shrinkbias,
        finalgain,
        finalshift,
    )
    def finish(
        result_in,
        tgrad_in,
        exp_low,
        shr_low,
        out_low,
        proj_low,
        totals,
        result_out,
        tgrad_out,
        proj_out,
        bias_out,
        out_out,
        out_bias_out,
        gain1_out,
        shift1_out,
        exp_out,
        exp_bias_out,
        shr_out,
        shr_bias_out,
        gain2_out,
        shift2_out,
        rms_out,
        turned_in,
        turned,
        low,
        full,
        in_sem,
        out_sem,
    ):
        pieces = []
        for c in range(blocks):
            here = pl.ds(c * width, width)
            pieces.append((exp_low.at[here], exp_out.at[here]))
        for c in range(blocks):
            here = pl.ds(c * width, width)
            pieces.append((shr_low.at[here], shr_out.at[here]))
        for j in range(3):
            pieces.append((proj_low.at[pl.ds(j * width, width)], proj_out.at[j]))
        pieces.append((out_low, out_out))
        loads = []
        for i, (src, _) in enumerate(pieces):
            loads.append(pltpu.make_async_copy(src, low.at[i], in_sem.at[i]))
        for i, src in enumerate((result_in, tgrad_in)):
            loads.append(pltpu.make_async_copy(src, turned_in.at[i], in_sem.at[n_chunks + i]))
        for load in loads:
            load.start()
        bias_out[...] = totals[V_QUERY : V_VALUE + 1]
        for row, out in (
            (V_OUT, out_bias_out),
            (V_GAIN1, gain1_out),
            (V_SHIFT1, shift1_out),
            (V_SHRINK, shr_bias_out),
            (V_GAIN2, gain2_out),
            (V_SHIFT2, shift2_out),
        ):
            out[...] = totals[row]
        exp_bias_out[...] = totals[V_EXPAND : V_EXPAND + blocks].reshape(hidden_units)
        squares = jnp.sum(totals[sums_at : sums_at + 4], axis=1, keepdims=True)
        count = totals[sums_at + S_COUNT : sums_at + S_COUNT + 1, 0:1] * width
        roots = jnp.sqrt(squares / count)
        lane = lax.broadcasted_iota(jnp.int32, (4, LANES), 1)
        row = lax.broadcasted_iota(jnp.int32, (4, LANES), 0)
        line = jnp.sum(jnp.where(lane == row, roots, 0.0), axis=0)
        rms_out[...] = line[0:3]
        stores = []
        for i, (_, dst) in enumerate(pieces):
            loads[i].wait()
            full[i] = low[i].astype(F32)
            stores.append(pltpu.make_async_copy(full.at[i], dst, out_sem.at[i]))
            stores[-1].start()
        for i, dst in enumerate((result_out, tgrad_out)):
            loads[n_chunks + i].wait()
            turned[i] = jnp.swapaxes(turned_in[i], 0, 1)
            stores.append(pltpu.make_async_copy(turned.at[i], dst, out_sem.at[n_chunks + i]))
            stores[-1].start()
        for store in stores:
            store.wait()

    vector = jax.ShapeDtypeStruct((width,), F32)
    square = (n_chunks, width, width)
    outs = pl.pallas_call(
        finish,
        out_shape=(
            jax.ShapeDtypeStruct((span, group, width), BF16),
            jax.ShapeDtypeStruct((span, group, width), BF16),
            jax.ShapeDtypeStruct((3, width, width), F32),
            jax.ShapeDtypeStruct((2, width), F32),
            jax.ShapeDtypeStruct((width, width), F32),
            vector,
            vector,
            vector,
            jax.ShapeDtypeStruct((hidden_units, width), F32),
            jax.ShapeDtypeStruct((hidden_units,), F32),
            jax.ShapeDtypeStruct((hidden_units, width), F32),
            vector,
            vector,
            vector,
            jax.ShapeDtypeStruct((3,), F32),
        ),
        in_specs=[*([hbm] * 6), vmem],
        out_specs=(hbm, hbm, hbm, vmem, hbm, vmem, vmem, vmem, hbm, vmem, hbm, *([vmem] * 4)),
        scratch_shapes=[
            pltpu.VMEM((2, group, span, width), BF16),
            pltpu.VMEM((2, span, group, width), BF16),
            pltpu.VMEM(square, BF16),
            pltpu.VMEM(square, F32),
            pltpu.SemaphoreType.DMA((n_chunks + 2,)),
            pltpu.SemaphoreType.DMA((n_chunks + 2,)),
        ],
        compiler_params=pltpu.CompilerParams(vmem_limit_bytes=62 * 2**20),
    )(result, tokens_grad, exp_grad, shr_grad, out_grad, proj_grad, sums)
    outs = list(outs)
    outs[2] = jnp.transpose(outs[2], (1, 0, 2))
    return tuple(outs)


def solution(mesh):
    split = P("seq", "dp", None)
    placed = (split, P(None, "dp"), *([P()] * 12), split)
    return jax.shard_map(
        local,
        mesh=mesh,
        in_specs=placed,
        out_specs=(split, split, *([P()] * 13)),
        check_vma=False,
    )
```

```python
import jax
import jax.numpy as jnp
from jax import lax
from jax.experimental import pallas as pl
from jax.experimental.pallas import tpu as pltpu
from jax.sharding import PartitionSpec as P

HEAD_DIM = 64
EPSILON = 1e-12
LANES = 128
F32 = jnp.float32
BF16 = jnp.bfloat16
SCALE = HEAD_DIM ** (-0.5)

(V_QUERY, V_VALUE, V_OUT, V_GAIN1, V_SHIFT1, V_SHRINK, V_GAIN2, V_SHIFT2, V_EXPAND) = range(9)
(S_INPUT, S_ATTENDED, S_SHRUNK, S_COUNT) = range(4)


ORDERS = (
    ("core", "side", "near", "far"),
    ("core", "near", "side", "far"),
    ("core", "far", "near", "side"),
    ("core", "near", "far", "side"),
)
CLASSES = (1, 3, 0, 1, 2, 0, 1, 0, 1)
UNIT, SHOW = -1, -2
MERGED = (1, 1, 2, 2, 2, 1, 1, 1, 1)
PLAN = (
    UNIT, UNIT, UNIT, UNIT, UNIT, 0, 1, UNIT, SHOW, 2, UNIT, UNIT, UNIT, 3, 0, 4, 1, UNIT,
    UNIT, UNIT, UNIT, UNIT, 3, 5, UNIT, UNIT, UNIT, UNIT, UNIT, 2, 0, 4, UNIT, UNIT, 1, 3,
    UNIT, UNIT, 0, 6, 7, 1, 2, 8, 9, 4, 3, 5, 0, UNIT, 7, 1, 9, 6, 2, 8, 0, 4, 9, 5, 3, UNIT,
    7, 9, 1, 0, 6, 2, 8, 0, 4, 5, 1, 7, 6, 3, 2, 8, 1, 4, 5, 7, 6, 8, 3, 5, 7, 2, 3, 6, 8, 2,
    5, 6, 4, 7, 5, 8, 6, 4, 7, 8,
)


def nn(a, b):
    return lax.dot_general(a, b, (((1,), (0,)), ((), ())), preferred_element_type=F32)


def nt(a, b):
    return lax.dot_general(a, b, (((1,), (1,)), ((), ())), preferred_element_type=F32)


def tn(a, b):
    return lax.dot_general(a, b, (((0,), (0,)), ((), ())), preferred_element_type=F32)


def gelu_parts(u):
    phi = 0.5 + 0.5 * lax.erf(u * 0.5**0.5)
    density = jnp.exp2((u * (-0.5 * 1.4426950408889634)) * u)
    return u * phi, phi + (0.3989422804014327 * u) * density


def levels_of(n_seq, n_dp):
    low = 2 if n_seq % 2 == 0 else 1
    near = 1
    while 4 * near * near <= n_dp and n_dp % (2 * near) == 0:
        near *= 2
    return {
        "core": ("seq", 1, low),
        "side": ("seq", low, n_seq // low),
        "near": ("dp", 1, near),
        "far": ("dp", near, n_dp // near),
    }


def slots_of(levels, order, rows):
    total = 0
    for name in order:
        size = levels[name][2]
        if size == 1:
            continue
        if rows % (16 * size) == 0:
            rows //= size
            total += (size - 1) * rows
        else:
            total += size * rows
    return total


def local(
    tokens,
    segments,
    projections,
    projbias,
    outweight,
    outbias,
    normgain,
    normshift,
    expander,
    expandbias,
    shrinker,
    shrinkbias,
    finalgain,
    finalshift,
    cotangent,
):
    n_seq, n_dp = lax.axis_size("seq"), lax.axis_size("dp")
    span, group, width = tokens.shape
    length = segments.shape[0]
    rows = group // n_seq
    hidden_units = expander.shape[0]
    blocks = hidden_units // width
    heads = width // HEAD_DIM
    pairs = width // LANES
    own_tokens = rows * length
    levels = levels_of(n_seq, n_dp)
    n_blocks = 2 * blocks + 4
    chunks, taken = [], 0
    while taken < n_blocks:
        count = min(MERGED[len(chunks)] if len(chunks) < len(MERGED) else 1, n_blocks - taken)
        chunks.append((taken, count))
        taken += count
    n_chunks = len(chunks)
    chunk_orders = []
    for index, (_, count) in enumerate(chunks):
        choices = (ORDERS[CLASSES[index % len(CLASSES)]], ORDERS[0])
        chunk_orders.append(min(choices, key=lambda order: slots_of(levels, order, count * width)))
    slot_bases, slot_rows = [], 0
    for order, (_, count) in zip(chunk_orders, chunks):
        slot_bases.append(slot_rows)
        slot_rows += slots_of(levels, order, count * width)
    grad_rows = n_blocks * width
    vec_rows = V_EXPAND + blocks
    sum_rows = -(-(vec_rows + 4) // 8) * 8
    sums_at = vec_rows
    ring = sum(size - 1 for _, _, size in levels.values())
    n_remote = 4 * rows * (n_seq - 1) + n_chunks * 2 * ring + ring
    n_local = 8 + 4 * rows + n_chunks

    def kernel(
        tok_hbm,
        cot_hbm,
        labels,
        proj_hbm,
        out_hbm,
        exp_hbm,
        shr_hbm,
        bias,
        out_bias,
        gain1,
        shift1,
        exp_bias,
        shr_bias,
        gain2,
        shift2,
        result_in,
        tgrad_in,
        low_grads,
        sums_out,
        raw,
        vec,
        x,
        cot,
        proj,
        outw,
        expw,
        shrw,
        mixed,
        probs,
        context,
        inverse,
        vhat1,
        rstd1,
        low1,
        active,
        slope,
        second,
        shrunk_low,
        qfeat,
        grads,
        slots,
        sums,
        sum_slots,
        send_sem,
        recv_sem,
        local_sem,
    ):
        me = lax.axis_index("seq")
        attended_low, context_grad = shrunk_low, cot
        shown_at = (n_blocks - 3) * width
        started, counters = [], {"remote": 0, "local": 0}

        def remote(src, dst, where):
            i = counters["remote"]
            counters["remote"] += 1
            copy = pltpu.make_async_remote_copy(
                src_ref=src,
                dst_ref=dst,
                send_sem=send_sem.at[i],
                recv_sem=recv_sem.at[i],
                device_id=where,
                device_id_type=pl.DeviceIdType.MESH,
            )
            copy.start()
            started.append(copy)
            return copy

        def near_copy(src, dst):
            i = counters["local"]
            counters["local"] += 1
            copy = pltpu.make_async_copy(src, dst, local_sem.at[i])
            copy.start()
            return copy

        def place(name):
            axis, stride, size = levels[name]
            index = lax.axis_index(axis)
            mine = lax.rem(lax.div(index, stride), size)
            return axis, index, stride, size, mine

        arriving = [near_copy(tok_hbm, raw)]
        weights = [
            near_copy(proj_hbm, proj),
            near_copy(out_hbm, outw),
            near_copy(exp_hbm, expw),
            near_copy(shr_hbm, shrw),
        ]

        barrier = pltpu.get_barrier_semaphore()
        greeted = 0
        for j in range(1, n_seq):
            pl.semaphore_signal(
                barrier,
                inc=1,
                device_id={"seq": lax.rem(me + j, n_seq)},
                device_id_type=pl.DeviceIdType.MESH,
            )
            greeted += 1
        for name in ("near", "far"):
            axis, index, stride, size, mine = place(name)
            for j in range(1, size):
                k = lax.rem(mine + j, size)
                pl.semaphore_signal(
                    barrier,
                    inc=1,
                    device_id={axis: index + (k - mine) * stride},
                    device_id_type=pl.DeviceIdType.MESH,
                )
                greeted += 1

        def bring(base, dst, r):
            here = pl.ds(pl.multiple_of(r * length + me * span, 16), span)
            far = []
            for j in sorted(range(1, n_seq), key=lambda j: j % 2):
                k = lax.rem(me + j, n_seq)
                src = grads.at[pl.ds(pl.multiple_of(base + (k * rows + r) * span, 16), span)]
                far.append(remote(src, dst.at[here], {"seq": k}))
            own = pl.ds(pl.multiple_of(base + (me * rows + r) * span, 16), span)
            dst[here] = grads[own]
            return far

        def deliver(src, dst, r):
            far = []
            for j in sorted(range(1, n_seq), key=lambda j: j % 2):
                k = lax.rem(me + j, n_seq)
                piece = src.at[pl.ds(pl.multiple_of(r * length + k * span, 16), span)]
                far.append(remote(piece, dst.at[me * rows + r], {"seq": k}))
            own = pl.ds(pl.multiple_of(r * length + me * span, 16), span)
            kept.append(near_copy(src.at[own], dst.at[me * rows + r]))
            return far

        kept = []

        def arrive(copies):
            for copy in copies:
                copy.wait_recv()

        def spread(index, base):
            arriving[index].wait()
            turned = jnp.swapaxes(raw[...], 0, 1)
            grads[base : base + group * span] = turned.reshape(group * span, width)

        def reduce_chunk(index):
            base, count = chunks[index][0] * width, chunks[index][1] * width
            written = []
            at, slot, stack = base, slot_bases[index], []
            for name in chunk_orders[index]:
                axis, own, stride, size, mine = place(name)
                if size == 1:
                    continue
                copies = []
                if count % (16 * size) == 0:
                    piece = count // size
                    for j in range(1, size):
                        k = lax.rem(mine + j, size)
                        copies.append(
                            remote(
                                grads.at[pl.ds(pl.multiple_of(at + k * piece, 16), piece)],
                                slots.at[pl.ds(slot + (j - 1) * piece, piece)],
                                {axis: own + (k - mine) * stride},
                            )
                        )
                    yield
                    here = pl.multiple_of(at + mine * piece, 16)
                    for copy in copies:
                        copy.wait_recv()
                    total = grads[pl.ds(here, piece)].astype(F32)
                    for j in range(size - 1):
                        total = total + slots[pl.ds(slot + j * piece, piece)].astype(F32)
                    grads[pl.ds(here, piece)] = total.astype(BF16)
                    stack.append((name, at, piece))
                    slot += (size - 1) * piece
                    at, count = here, piece
                else:
                    mine_slot = pl.ds(pl.multiple_of(slot + mine * count, 16), count)
                    slots[mine_slot] = grads[pl.ds(at, count)]
                    for j in range(1, size):
                        k = lax.rem(mine + j, size)
                        copies.append(
                            remote(
                                slots.at[mine_slot],
                                slots.at[mine_slot],
                                {axis: own + (k - mine) * stride},
                            )
                        )
                    yield
                    for copy in copies:
                        copy.wait_recv()
                    total = jnp.zeros((count, width), F32)
                    for j in range(size):
                        total = total + slots[pl.ds(slot + j * count, count)].astype(F32)
                    grads[pl.ds(at, count)] = total.astype(BF16)
                    slot += size * count
            block, copies = grads.at[pl.ds(at, count)], []
            written.append(near_copy(block, low_grads.at[pl.ds(pl.multiple_of(at, 16), count)]))
            for name, before, piece in reversed(stack):
                axis, own, stride, size, mine = place(name)
                target = low_grads.at[pl.ds(pl.multiple_of(at, 16), piece)]
                copies = []
                for j in range(1, size):
                    k = lax.rem(mine + j, size)
                    copies.append(remote(block, target, {axis: own + (k - mine) * stride}))
                yield
                for copy in copies:
                    copy.wait_recv()
                if written:
                    written.pop().wait()
                count = piece * size
                at, block = before, low_grads.at[pl.ds(pl.multiple_of(before, 16), count)]
            if written:
                written.pop().wait()

        def reduce_sums():
            current = sums
            for step, name in enumerate(("core", "side", "near", "far")):
                axis, own, stride, size, mine = place(name)
                if size == 1:
                    continue
                first = sum(levels[n][2] for n in ("core", "side", "near", "far")[:step])
                sum_slots[first + mine] = current[...]
                copies = []
                for j in range(1, size):
                    k = lax.rem(mine + j, size)
                    block = sum_slots.at[first + mine]
                    copies.append(remote(block, block, {axis: own + (k - mine) * stride}))
                yield
                for copy in copies:
                    copy.wait_recv()
                total = sum_slots[first]
                for j in range(1, size):
                    total = total + sum_slots[first + j]
                current[...] = total
            sums_out[...] = current[...]

        running = {}

        def advance(index):
            if index in running and next(running[index], "end") == "end":
                del running[index]

        def begin(index):
            running[index] = reduce_chunk(index) if index < n_chunks else reduce_sums()
            next(running[index])

        def done(block):
            for index, (first, count) in enumerate(chunks):
                if first + count - 1 == block:
                    begin(index)

        def add(row, value):
            sums[row : row + 1, :] += jnp.sum(value, axis=0, keepdims=True)

        def vrow(i):
            return vec[i : i + 1, :]

        def features(r):
            here = pl.ds(r * length, length)
            label = labels[pl.ds(me * rows + r, 1), :]
            ids = lax.broadcasted_iota(jnp.int32, (LANES, length), 0)
            hot = jnp.where(ids == label, 1.0, 0.0)
            hot = jnp.transpose(hot)
            qfeat[here] = hot.astype(BF16)
            real = 1.0 - hot[:, 0:1]
            sums[sums_at + S_COUNT : sums_at + S_COUNT + 1, 0:LANES] += jnp.sum(
                jnp.broadcast_to(real, (length, LANES)), axis=0, keepdims=True
            )

        vec[0:2] = bias[...].astype(F32)
        for row, vector in enumerate((out_bias, gain1, shift1, shr_bias, gain2, shift2)):
            vec[2 + row : 3 + row] = vector[...].astype(F32).reshape(1, width)
        vec[V_EXPAND:vec_rows] = exp_bias[...].astype(F32).reshape(blocks, width)
        spread(0, 0)
        arriving.append(near_copy(cot_hbm, raw))
        pl.semaphore_wait(barrier, greeted)
        incoming = [bring(0, x, r) for r in range(rows)]
        spread(1, group * span)
        cotangents = [bring(group * span, cot, r) for r in range(rows)]
        sent = list(started)
        sums[...] = jnp.zeros_like(sums)
        for r in range(rows):
            features(r)
        for copy in weights:
            copy.wait()

        lane = lax.broadcasted_iota(jnp.int32, (length, LANES), 1)
        first_head = lane < HEAD_DIM
        lane_row = lax.broadcasted_iota(jnp.int32, (1, LANES), 1)
        masks = [
            jnp.where(lane_row // HEAD_DIM == part, 1.0, 0.0).astype(BF16) for part in (0, 1)
        ]
        scaled = [mask * BF16(SCALE) for mask in masks]

        def mix(r):
            here = pl.ds(r * length, length)
            block = x[here]
            mixed[0, here] = (nn(block, proj[0]) + vrow(V_QUERY)).astype(BF16)
            mixed[1, here] = nn(block, proj[1]).astype(BF16)
            mixed[2, here] = (nn(block, proj[2]) + vrow(V_VALUE)).astype(BF16)

        def attend(r):
            here = pl.ds(r * length, length)

            apart = ((qfeat[here].astype(F32) - 1.0) * 1e30).astype(BF16)
            for pair in range(pairs):
                lanes = pl.ds(pair * LANES, LANES)
                query = mixed[0, here, lanes]
                keys = jnp.concatenate([mixed[1, here, lanes], apart], axis=1)
                values = jnp.concatenate(
                    [mixed[2, here, lanes], jnp.ones((length, LANES), BF16)], axis=1
                )
                sides = []
                for part in (0, 1):
                    wide = jnp.concatenate([query * scaled[part], qfeat[here]], axis=1)
                    scores = nt(wide, keys)
                    raised = jnp.exp(scores - jnp.max(scores, axis=1, keepdims=True)).astype(BF16)
                    probs[r * heads + 2 * pair + part] = raised
                    sides.append(nn(raised, values))
                total = jnp.where(first_head, sides[0][:, LANES:], sides[1][:, LANES:])
                mean = jnp.where(first_head, sides[0][:, :LANES], sides[1][:, :LANES])
                inv = 1.0 / total
                context[here, lanes] = (mean * inv).astype(BF16)
                inverse[here, lanes] = inv.astype(BF16)

        def wide_valid(r):
            return 1.0 - qfeat[pl.ds(r * length, length)].astype(F32)[:, 0:1]

        def normalize(value):
            center = value - jnp.mean(value, axis=1, keepdims=True)
            spread = jnp.mean(center * center, axis=1, keepdims=True)
            scale = lax.rsqrt(spread + EPSILON)
            return center * scale, scale

        def normalize_back(up, gain, vhat, scale):
            a = up * gain
            return (
                a
                - jnp.mean(a, axis=1, keepdims=True)
                - vhat * jnp.mean(a * vhat, axis=1, keepdims=True)
            ) * scale

        def first_half(r):
            here = pl.ds(r * length, length)
            attended = nn(context[here], outw[...]) + vrow(V_OUT)
            inputs = x[here].astype(F32)
            real = wide_valid(r)
            add(sums_at + S_INPUT, real * inputs * inputs)
            add(sums_at + S_ATTENDED, real * attended * attended)
            vhat, scale = normalize(inputs + attended)
            vhat1[here] = vhat
            rstd1[here] = jnp.broadcast_to(scale, (length, LANES))
            low1[here] = (vhat * vrow(V_GAIN1) + vrow(V_SHIFT1)).astype(BF16)

        def expand(r):
            here = pl.ds(r * length, length)

            for c in range(blocks):
                upper = nt(low1[here], expw[c]) + vrow(V_EXPAND + c)
                value, derivative = gelu_parts(upper)
                active[c, here] = value.astype(BF16)
                slope[c, here] = derivative.astype(BF16)

        def second_half(r):
            here = pl.ds(r * length, length)
            shrunk = nn(active[0, here], shrw[0])
            for c in range(1, blocks):
                shrunk = shrunk + nn(active[c, here], shrw[c])
            shrunk = shrunk + vrow(V_SHRINK)
            add(sums_at + S_SHRUNK, wide_valid(r) * shrunk * shrunk)
            hidden = vhat1[here] * vrow(V_GAIN1) + vrow(V_SHIFT1)
            vhat, scale = normalize(hidden + shrunk)
            there = pl.ds(shown_at + r * length, length)
            grads[there] = (vhat * vrow(V_GAIN2) + vrow(V_SHIFT2)).astype(BF16)
            up = cot[here].astype(F32)
            add(V_GAIN2, up * vhat)
            add(V_SHIFT2, up)
            grad = normalize_back(up, vrow(V_GAIN2), vhat, scale)
            second[here] = grad
            low = grad.astype(BF16)
            shrunk_low[here] = low
            add(V_SHRINK, low.astype(F32))

        ones = jnp.ones((8, own_tokens), BF16)

        def upper_back(c, r):
            here = pl.ds(r * length, length)
            grad = nt(shrunk_low[here], shrw[c])
            slope[c, here] = (grad * slope[c, here].astype(F32)).astype(BF16)

        def expand_back(c):
            upper_back(c, rows - 1)
            base = 2 * width * c
            grads[base : base + width] = tn(slope[c], low1[...]).astype(BF16)
            done(2 * c)

        def shrink_back(c):
            base = 2 * width * c + width
            grads[base : base + width] = tn(active[c], shrunk_low[...]).astype(BF16)
            done(2 * c + 1)
            sums[V_EXPAND + c : V_EXPAND + c + 1, :] = nn(ones, slope[c])[0:1]

        def first_half_back(r):
            here = pl.ds(r * length, length)
            up = second[here]
            for c in range(blocks):
                up = up + nn(slope[c, here], expw[c])
            vhat = vhat1[here]
            add(V_GAIN1, up * vhat)
            add(V_SHIFT1, up)
            grad = normalize_back(up, vrow(V_GAIN1), vhat, rstd1[here][:, 0:1])
            second[here] = grad
            low = grad.astype(BF16)
            attended_low[here] = low
            add(V_OUT, low.astype(F32))
            context_grad[here] = nt(low, outw[...]).astype(BF16)

        def attend_back(r, pair):
            here = pl.ds(r * length, length)
            lanes = pl.ds(pair * LANES, LANES)
            query, keys, values = (mixed[j, here, lanes] for j in range(3))
            up = context_grad[here, lanes].astype(F32) * inverse[here, lanes].astype(F32)
            up = up.astype(BF16)
            inner = up.astype(F32) * context[here, lanes].astype(F32)
            sides = []
            for part in (0, 1):
                raised = probs[r * heads + 2 * pair + part]
                mine = first_head if part == 0 else jnp.logical_not(first_head)
                delta = jnp.sum(jnp.where(mine, inner, 0.0), axis=1, keepdims=True)
                dprobs = nt(up * masks[part], values)
                score = (raised.astype(F32) * (dprobs - delta)).astype(BF16)
                sides.append((nn(score, keys), tn(score, query), tn(raised, up)))
            for j, factor in enumerate((SCALE, SCALE, 1.0)):
                both = jnp.where(first_head, sides[0][j], sides[1][j])
                mixed[j, here, lanes] = (both * factor).astype(BF16)

        def tokens_back(r):
            here = pl.ds(r * length, length)
            grad = second[here]
            for j in range(3):
                grad = grad + nt(mixed[j, here], proj[j])
            low1[here] = grad.astype(BF16)

        def out_back():
            base = 2 * blocks * width
            grads[base : base + width] = tn(context[...], attended_low[...]).astype(BF16)
            done(2 * blocks)

        def mix_back(j):
            if j == 0:
                for copies in results:
                    for copy in copies:
                        copy.wait_send()
                        shown.append(copy)
                while kept:
                    kept.pop().wait()
            base = (2 * blocks + 1 + j) * width
            grads[base : base + width] = tn(x[...], mixed[j]).astype(BF16)
            done(2 * blocks + 1 + j)

        def sums_back():
            for row, j in ((V_QUERY, 0), (V_VALUE, 2)):
                sums[row : row + 1, :] = nn(ones, mixed[j])[0:1]
            begin(n_chunks)

        returned, shown = [], []

        def give_back(r):
            tokens_back(r)
            returned.append(deliver(low1, tgrad_in, r))

        for r in range(rows):
            arrive(incoming[r])
            mix(r)
            attend(r)
            first_half(r)
            expand(r)
        results = []
        for r in range(rows):
            arrive(cotangents[r])
            second_half(r)
            if r + 1 < rows:
                for c in range(blocks):
                    upper_back(c, r)
        for copy in sent:
            copy.wait_send()

        def show(r):
            results.append(deliver(grads.at[pl.ds(shown_at, own_tokens)], result_in, r))

        units = []
        for c in range(blocks):
            units += [lambda c=c: expand_back(c), lambda c=c: shrink_back(c)]
        units += [lambda r=r: first_half_back(r) for r in range(rows)]
        units.append(out_back)
        for r in range(rows):
            units += [lambda r=r, pair=pair: attend_back(r, pair) for pair in range(pairs)]
        units += [lambda j=j: mix_back(j) for j in range(3)]
        units.append(sums_back)
        units += [lambda r=r: give_back(r) for r in range(rows)]
        late = {SHOW: lambda: [show(r) for r in range(rows)]}
        for index in PLAN:
            if index == UNIT:
                if units:
                    units.pop(0)()
            elif index in late:
                late.pop(index)()
            else:
                advance(index)
        for unit in list(late.values()) + units:
            unit()
        while running:
            for index in list(running):
                advance(index)
        for copies in results + returned:
            arrive(copies)
        for copy in started[len(sent) :]:
            if all(copy is not other for other in shown):
                copy.wait_send()
        for copy in kept:
            copy.wait()

    hbm = pl.BlockSpec(memory_space=pl.ANY)
    vmem = pl.BlockSpec(memory_space=pltpu.VMEM)
    big = (own_tokens, width)
    result, tokens_grad, low_grads, sums = pl.pallas_call(
        kernel,
        out_shape=(
            jax.ShapeDtypeStruct((group, span, width), BF16),
            jax.ShapeDtypeStruct((group, span, width), BF16),
            jax.ShapeDtypeStruct((grad_rows, width), BF16),
            jax.ShapeDtypeStruct((sum_rows, width), F32),
        ),
        in_specs=[hbm, hbm, vmem, hbm, hbm, hbm, hbm, *([vmem] * 8)],
        out_specs=(hbm, hbm, hbm, vmem),
        scratch_shapes=[
            pltpu.VMEM((span, group, width), BF16),
            pltpu.VMEM((sum_rows, width), F32),
            pltpu.VMEM(big, BF16),
            pltpu.VMEM(big, BF16),
            pltpu.VMEM((3, width, width), BF16),
            pltpu.VMEM((width, width), BF16),
            pltpu.VMEM((blocks, width, width), BF16),
            pltpu.VMEM((blocks, width, width), BF16),
            pltpu.VMEM((3, *big), BF16),
            pltpu.VMEM((rows * heads, length, length), BF16),
            pltpu.VMEM(big, BF16),
            pltpu.VMEM(big, BF16),
            pltpu.VMEM(big, F32),
            pltpu.VMEM((own_tokens, LANES), F32),
            pltpu.VMEM(big, BF16),
            pltpu.VMEM((blocks, *big), BF16),
            pltpu.VMEM((blocks, *big), BF16),
            pltpu.VMEM(big, F32),
            pltpu.VMEM(big, BF16),
            pltpu.VMEM((own_tokens, LANES), BF16),
            pltpu.VMEM((grad_rows, width), BF16),
            pltpu.VMEM((slot_rows, width), BF16),
            pltpu.VMEM((sum_rows, width), F32),
            pltpu.VMEM((sum(size for _, _, size in levels.values()), sum_rows, width), F32),
            pltpu.SemaphoreType.DMA((n_remote,)),
            pltpu.SemaphoreType.DMA((n_remote,)),
            pltpu.SemaphoreType.DMA((n_local,)),
        ],
        compiler_params=pltpu.CompilerParams(
            collective_id=0, has_side_effects=True, vmem_limit_bytes=63 * 2**20
        ),
    )(
        tokens,
        cotangent,
        jnp.transpose(segments),
        jnp.transpose(projections, (1, 0, 2)),
        outweight,
        expander.reshape(blocks, width, width),
        shrinker.reshape(blocks, width, width),
        projbias,
        outbias,
        normgain,
        normshift,
        expandbias,
        shrinkbias,
        finalgain,
        finalshift,
    )
    def finish(
        result_in,
        tgrad_in,
        low_grads,
        totals,
        result_out,
        tgrad_out,
        proj_out,
        bias_out,
        out_out,
        out_bias_out,
        gain1_out,
        shift1_out,
        exp_out,
        exp_bias_out,
        shr_out,
        shr_bias_out,
        gain2_out,
        shift2_out,
        rms_out,
        turned_in,
        turned,
        low,
        full,
        in_sem,
        out_sem,
    ):
        places = []
        for c in range(blocks):
            here = pl.ds(c * width, width)
            places += [exp_out.at[here], shr_out.at[here]]
        places.append(out_out)
        places += [proj_out.at[j] for j in range(3)]
        loads = []
        for i in range(n_blocks):
            src = low_grads.at[pl.ds(i * width, width)]
            loads.append(pltpu.make_async_copy(src, low.at[i], in_sem.at[i]))
        for i, src in enumerate((result_in, tgrad_in)):
            loads.append(pltpu.make_async_copy(src, turned_in.at[i], in_sem.at[n_blocks + i]))
        for load in loads:
            load.start()
        bias_out[...] = totals[V_QUERY : V_VALUE + 1]
        for row, out in (
            (V_OUT, out_bias_out),
            (V_GAIN1, gain1_out),
            (V_SHIFT1, shift1_out),
            (V_SHRINK, shr_bias_out),
            (V_GAIN2, gain2_out),
            (V_SHIFT2, shift2_out),
        ):
            out[...] = totals[row]
        exp_bias_out[...] = totals[V_EXPAND : V_EXPAND + blocks].reshape(hidden_units)
        squares = jnp.sum(totals[sums_at : sums_at + 4], axis=1, keepdims=True)
        count = totals[sums_at + S_COUNT : sums_at + S_COUNT + 1, 0:1] * width
        roots = jnp.sqrt(squares / count)
        lane = lax.broadcasted_iota(jnp.int32, (4, LANES), 1)
        row = lax.broadcasted_iota(jnp.int32, (4, LANES), 0)
        line = jnp.sum(jnp.where(lane == row, roots, 0.0), axis=0)
        rms_out[...] = line[0:3]
        stores = []
        for i, dst in enumerate(places):
            loads[i].wait()
            full[i] = low[i].astype(F32)
            stores.append(pltpu.make_async_copy(full.at[i], dst, out_sem.at[i]))
            stores[-1].start()
        for i, dst in enumerate((result_out, tgrad_out)):
            loads[n_blocks + i].wait()
            turned[i] = jnp.swapaxes(turned_in[i], 0, 1)
            stores.append(pltpu.make_async_copy(turned.at[i], dst, out_sem.at[n_blocks + i]))
            stores[-1].start()
        for store in stores:
            store.wait()

    vector = jax.ShapeDtypeStruct((width,), F32)
    square = (n_blocks, width, width)
    outs = pl.pallas_call(
        finish,
        out_shape=(
            jax.ShapeDtypeStruct((span, group, width), BF16),
            jax.ShapeDtypeStruct((span, group, width), BF16),
            jax.ShapeDtypeStruct((3, width, width), F32),
            jax.ShapeDtypeStruct((2, width), F32),
            jax.ShapeDtypeStruct((width, width), F32),
            vector,
            vector,
            vector,
            jax.ShapeDtypeStruct((hidden_units, width), F32),
            jax.ShapeDtypeStruct((hidden_units,), F32),
            jax.ShapeDtypeStruct((hidden_units, width), F32),
            vector,
            vector,
            vector,
            jax.ShapeDtypeStruct((3,), F32),
        ),
        in_specs=[hbm, hbm, hbm, vmem],
        out_specs=(hbm, hbm, hbm, vmem, hbm, vmem, vmem, vmem, hbm, vmem, hbm, *([vmem] * 4)),
        scratch_shapes=[
            pltpu.VMEM((2, group, span, width), BF16),
            pltpu.VMEM((2, span, group, width), BF16),
            pltpu.VMEM(square, BF16),
            pltpu.VMEM(square, F32),
            pltpu.SemaphoreType.DMA((n_blocks + 2,)),
            pltpu.SemaphoreType.DMA((n_blocks + 2,)),
        ],
        compiler_params=pltpu.CompilerParams(vmem_limit_bytes=62 * 2**20),
    )(result, tokens_grad, low_grads, sums)
    outs = list(outs)
    outs[2] = jnp.transpose(outs[2], (1, 0, 2))
    return tuple(outs)


def solution(mesh):
    split = P("seq", "dp", None)
    placed = (split, P(None, "dp"), *([P()] * 12), split)
    return jax.shard_map(
        local,
        mesh=mesh,
        in_specs=placed,
        out_specs=(split, split, *([P()] * 13)),
        check_vma=False,
    )
```

```python
import jax
import jax.numpy as jnp
from jax import lax
from jax.experimental import pallas as pl
from jax.experimental.pallas import tpu as pltpu
from jax.sharding import PartitionSpec as P

HEAD_DIM = 64
EPSILON = 1e-12
LANES = 128
F32 = jnp.float32
BF16 = jnp.bfloat16
SCALE = HEAD_DIM ** (-0.5)

(V_QUERY, V_VALUE, V_OUT, V_GAIN1, V_SHIFT1, V_SHRINK, V_GAIN2, V_SHIFT2, V_EXPAND) = range(9)
(S_INPUT, S_ATTENDED, S_SHRUNK, S_COUNT) = range(4)


ORDERS = (
    ("core", "side", "near", "far"),
    ("core", "near", "side", "far"),
    ("core", "far", "near", "side"),
    ("core", "near", "far", "side"),
)
CLASSES = (1, 1, 0, 2, 1, 0, 1, 1)
UNIT, SHOW = -1, -2
MERGED = (2, 2, 2, 2, 1, 1, 1, 1)
PLAN = (
    SHOW, UNIT, UNIT, UNIT, UNIT, UNIT, UNIT, 0, UNIT, UNIT, UNIT, 1, 2, 3, UNIT, UNIT, 0,
    UNIT, UNIT, UNIT, UNIT, 4, 1, UNIT, UNIT, 0, UNIT, UNIT, 1, 2, UNIT, UNIT, 4, 0, 3, UNIT,
    5, 6, 2, 3, 7, 0, 1, 4, 5, 6, 3, 2, 0, 7, 1, 6, 4, UNIT, 3, UNIT, 7, 8, 2, 5, 6, 4, 7, 1,
    5, 3, 6, 0, 7, 2, 5, 8, 6, 1, 4, 5, UNIT, 1, 7, 2, 4, 8, 6, 0, 5, 3, 7, 2, 8, 6, 4, 5, 3,
    7,
)


def nn(a, b):
    return lax.dot_general(a, b, (((1,), (0,)), ((), ())), preferred_element_type=F32)


def nt(a, b):
    return lax.dot_general(a, b, (((1,), (1,)), ((), ())), preferred_element_type=F32)


def tn(a, b):
    return lax.dot_general(a, b, (((0,), (0,)), ((), ())), preferred_element_type=F32)


def gelu_parts(u):
    phi = 0.5 + 0.5 * lax.erf(u * 0.5**0.5)
    density = jnp.exp2((u * (-0.5 * 1.4426950408889634)) * u)
    return u * phi, phi + (0.3989422804014327 * u) * density


def levels_of(n_seq, n_dp):
    low = 2 if n_seq % 2 == 0 else 1
    near = 1
    while 4 * near * near <= n_dp and n_dp % (2 * near) == 0:
        near *= 2
    return {
        "core": ("seq", 1, low),
        "side": ("seq", low, n_seq // low),
        "near": ("dp", 1, near),
        "far": ("dp", near, n_dp // near),
    }


def slots_of(levels, order, rows):
    total = 0
    for name in order:
        size = levels[name][2]
        if size == 1:
            continue
        if rows % (16 * size) == 0:
            rows //= size
            total += (size - 1) * rows
        else:
            total += size * rows
    return total


def local(
    tokens,
    segments,
    projections,
    projbias,
    outweight,
    outbias,
    normgain,
    normshift,
    expander,
    expandbias,
    shrinker,
    shrinkbias,
    finalgain,
    finalshift,
    cotangent,
):
    n_seq, n_dp = lax.axis_size("seq"), lax.axis_size("dp")
    span, group, width = tokens.shape
    length = segments.shape[0]
    rows = group // n_seq
    hidden_units = expander.shape[0]
    blocks = hidden_units // width
    heads = width // HEAD_DIM
    pairs = width // LANES
    own_tokens = rows * length
    levels = levels_of(n_seq, n_dp)
    n_blocks = 2 * blocks + 4
    chunks, taken = [], 0
    while taken < n_blocks:
        count = min(MERGED[len(chunks)] if len(chunks) < len(MERGED) else 1, n_blocks - taken)
        chunks.append((taken, count))
        taken += count
    n_chunks = len(chunks)
    chunk_orders = []
    for index, (_, count) in enumerate(chunks):
        choices = (ORDERS[CLASSES[index % len(CLASSES)]], ORDERS[0])
        chunk_orders.append(min(choices, key=lambda order: slots_of(levels, order, count * width)))
    slot_bases, slot_rows = [], 0
    for order, (_, count) in zip(chunk_orders, chunks):
        slot_bases.append(slot_rows)
        slot_rows += slots_of(levels, order, count * width)
    grad_rows = n_blocks * width
    vec_rows = V_EXPAND + blocks
    sum_rows = -(-(vec_rows + 4) // 8) * 8
    sums_at = vec_rows
    ring = sum(size - 1 for _, _, size in levels.values())
    n_remote = 4 * rows * (n_seq - 1) + n_chunks * 2 * ring + ring
    n_local = 8 + 4 * rows + n_chunks

    def kernel(
        tok_hbm,
        cot_hbm,
        labels,
        proj_hbm,
        out_hbm,
        exp_hbm,
        shr_hbm,
        bias,
        out_bias,
        gain1,
        shift1,
        exp_bias,
        shr_bias,
        gain2,
        shift2,
        result_in,
        tgrad_in,
        low_grads,
        sums_out,
        raw,
        vec,
        x,
        cot,
        proj,
        outw,
        expw,
        shrw,
        mixed,
        probs,
        context,
        inverse,
        vhat1,
        rstd1,
        low1,
        active,
        slope,
        second,
        shrunk_low,
        qfeat,
        grads,
        slots,
        sums,
        sum_slots,
        send_sem,
        recv_sem,
        local_sem,
    ):
        me = lax.axis_index("seq")
        attended_low, context_grad = shrunk_low, cot
        shown_at = (n_blocks - 3) * width
        started, counters = [], {"remote": 0, "local": 0}

        def remote(src, dst, where):
            i = counters["remote"]
            counters["remote"] += 1
            copy = pltpu.make_async_remote_copy(
                src_ref=src,
                dst_ref=dst,
                send_sem=send_sem.at[i],
                recv_sem=recv_sem.at[i],
                device_id=where,
                device_id_type=pl.DeviceIdType.MESH,
            )
            copy.start()
            started.append(copy)
            return copy

        def near_copy(src, dst):
            i = counters["local"]
            counters["local"] += 1
            copy = pltpu.make_async_copy(src, dst, local_sem.at[i])
            copy.start()
            return copy

        def place(name):
            axis, stride, size = levels[name]
            index = lax.axis_index(axis)
            mine = lax.rem(lax.div(index, stride), size)
            return axis, index, stride, size, mine

        arriving = [near_copy(tok_hbm, raw)]
        weights = [
            near_copy(proj_hbm, proj),
            near_copy(out_hbm, outw),
            near_copy(exp_hbm, expw),
            near_copy(shr_hbm, shrw),
        ]

        barrier = pltpu.get_barrier_semaphore()
        greeted = 0
        for j in range(1, n_seq):
            pl.semaphore_signal(
                barrier,
                inc=1,
                device_id={"seq": lax.rem(me + j, n_seq)},
                device_id_type=pl.DeviceIdType.MESH,
            )
            greeted += 1
        for name in ("near", "far"):
            axis, index, stride, size, mine = place(name)
            for j in range(1, size):
                k = lax.rem(mine + j, size)
                pl.semaphore_signal(
                    barrier,
                    inc=1,
                    device_id={axis: index + (k - mine) * stride},
                    device_id_type=pl.DeviceIdType.MESH,
                )
                greeted += 1

        def bring(base, dst, r):
            here = pl.ds(pl.multiple_of(r * length + me * span, 16), span)
            far = []
            for j in sorted(range(1, n_seq), key=lambda j: j % 2):
                k = lax.rem(me + j, n_seq)
                src = grads.at[pl.ds(pl.multiple_of(base + (k * rows + r) * span, 16), span)]
                far.append(remote(src, dst.at[here], {"seq": k}))
            own = pl.ds(pl.multiple_of(base + (me * rows + r) * span, 16), span)
            dst[here] = grads[own]
            return far

        def deliver(src, dst, r):
            far = []
            for j in sorted(range(1, n_seq), key=lambda j: j % 2):
                k = lax.rem(me + j, n_seq)
                piece = src.at[pl.ds(pl.multiple_of(r * length + k * span, 16), span)]
                far.append(remote(piece, dst.at[me * rows + r], {"seq": k}))
            own = pl.ds(pl.multiple_of(r * length + me * span, 16), span)
            kept.append(near_copy(src.at[own], dst.at[me * rows + r]))
            return far

        kept = []

        def arrive(copies):
            for copy in copies:
                copy.wait_recv()

        def spread(index, base):
            arriving[index].wait()
            turned = jnp.swapaxes(raw[...], 0, 1)
            grads[base : base + group * span] = turned.reshape(group * span, width)

        def reduce_chunk(index):
            base, count = chunks[index][0] * width, chunks[index][1] * width
            written = []
            at, slot, stack = base, slot_bases[index], []
            for name in chunk_orders[index]:
                axis, own, stride, size, mine = place(name)
                if size == 1:
                    continue
                copies = []
                if count % (16 * size) == 0:
                    piece = count // size
                    for j in range(1, size):
                        k = lax.rem(mine + j, size)
                        copies.append(
                            remote(
                                grads.at[pl.ds(pl.multiple_of(at + k * piece, 16), piece)],
                                slots.at[pl.ds(slot + (j - 1) * piece, piece)],
                                {axis: own + (k - mine) * stride},
                            )
                        )
                    yield
                    here = pl.multiple_of(at + mine * piece, 16)
                    for copy in copies:
                        copy.wait_recv()
                    total = grads[pl.ds(here, piece)].astype(F32)
                    for j in range(size - 1):
                        total = total + slots[pl.ds(slot + j * piece, piece)].astype(F32)
                    grads[pl.ds(here, piece)] = total.astype(BF16)
                    stack.append((name, at, piece))
                    slot += (size - 1) * piece
                    at, count = here, piece
                else:
                    mine_slot = pl.ds(pl.multiple_of(slot + mine * count, 16), count)
                    slots[mine_slot] = grads[pl.ds(at, count)]
                    for j in range(1, size):
                        k = lax.rem(mine + j, size)
                        copies.append(
                            remote(
                                slots.at[mine_slot],
                                slots.at[mine_slot],
                                {axis: own + (k - mine) * stride},
                            )
                        )
                    yield
                    for copy in copies:
                        copy.wait_recv()
                    total = jnp.zeros((count, width), F32)
                    for j in range(size):
                        total = total + slots[pl.ds(slot + j * count, count)].astype(F32)
                    grads[pl.ds(at, count)] = total.astype(BF16)
                    slot += size * count
            block, copies = grads.at[pl.ds(at, count)], []
            written.append(near_copy(block, low_grads.at[pl.ds(pl.multiple_of(at, 16), count)]))
            for name, before, piece in reversed(stack):
                axis, own, stride, size, mine = place(name)
                target = low_grads.at[pl.ds(pl.multiple_of(at, 16), piece)]
                copies = []
                for j in range(1, size):
                    k = lax.rem(mine + j, size)
                    copies.append(remote(block, target, {axis: own + (k - mine) * stride}))
                yield
                for copy in copies:
                    copy.wait_recv()
                if written:
                    written.pop().wait()
                count = piece * size
                at, block = before, low_grads.at[pl.ds(pl.multiple_of(before, 16), count)]
            if written:
                written.pop().wait()

        def reduce_sums():
            current = sums
            for step, name in enumerate(("core", "side", "near", "far")):
                axis, own, stride, size, mine = place(name)
                if size == 1:
                    continue
                first = sum(levels[n][2] for n in ("core", "side", "near", "far")[:step])
                sum_slots[first + mine] = current[...]
                copies = []
                for j in range(1, size):
                    k = lax.rem(mine + j, size)
                    block = sum_slots.at[first + mine]
                    copies.append(remote(block, block, {axis: own + (k - mine) * stride}))
                yield
                for copy in copies:
                    copy.wait_recv()
                total = sum_slots[first]
                for j in range(1, size):
                    total = total + sum_slots[first + j]
                current[...] = total
            sums_out[...] = current[...]

        running = {}

        def advance(index):
            if index in running and next(running[index], "end") == "end":
                del running[index]

        def begin(index):
            running[index] = reduce_chunk(index) if index < n_chunks else reduce_sums()
            next(running[index])

        def done(block):
            for index, (first, count) in enumerate(chunks):
                if first + count - 1 == block:
                    begin(index)

        def add(row, value):
            sums[row : row + 1, :] += jnp.sum(value, axis=0, keepdims=True)

        def vrow(i):
            return vec[i : i + 1, :]

        def features(r):
            here = pl.ds(r * length, length)
            label = labels[pl.ds(me * rows + r, 1), :]
            ids = lax.broadcasted_iota(jnp.int32, (LANES, length), 0)
            hot = jnp.where(ids == label, 1.0, 0.0)
            hot = jnp.transpose(hot)
            qfeat[here] = hot.astype(BF16)
            real = 1.0 - hot[:, 0:1]
            sums[sums_at + S_COUNT : sums_at + S_COUNT + 1, 0:LANES] += jnp.sum(
                jnp.broadcast_to(real, (length, LANES)), axis=0, keepdims=True
            )

        vec[0:2] = bias[...].astype(F32)
        for row, vector in enumerate((out_bias, gain1, shift1, shr_bias, gain2, shift2)):
            vec[2 + row : 3 + row] = vector[...].astype(F32).reshape(1, width)
        vec[V_EXPAND:vec_rows] = exp_bias[...].astype(F32).reshape(blocks, width)
        spread(0, 0)
        arriving.append(near_copy(cot_hbm, raw))
        pl.semaphore_wait(barrier, greeted)
        incoming = [bring(0, x, r) for r in range(rows)]
        spread(1, group * span)
        cotangents = [bring(group * span, cot, r) for r in range(rows)]
        sent = list(started)
        sums[...] = jnp.zeros_like(sums)
        for r in range(rows):
            features(r)
        for copy in weights:
            copy.wait()

        lane = lax.broadcasted_iota(jnp.int32, (length, LANES), 1)
        first_head = lane < HEAD_DIM
        lane_row = lax.broadcasted_iota(jnp.int32, (1, LANES), 1)
        masks = [
            jnp.where(lane_row // HEAD_DIM == part, 1.0, 0.0).astype(BF16) for part in (0, 1)
        ]
        scaled = [mask * BF16(SCALE) for mask in masks]

        def mix(r):
            here = pl.ds(r * length, length)
            block = x[here]
            mixed[0, here] = (nn(block, proj[0]) + vrow(V_QUERY)).astype(BF16)
            mixed[1, here] = nn(block, proj[1]).astype(BF16)
            mixed[2, here] = (nn(block, proj[2]) + vrow(V_VALUE)).astype(BF16)

        def attend(r):
            here = pl.ds(r * length, length)

            apart = ((qfeat[here].astype(F32) - 1.0) * 1e30).astype(BF16)
            for pair in range(pairs):
                lanes = pl.ds(pair * LANES, LANES)
                query = mixed[0, here, lanes]
                keys = jnp.concatenate([mixed[1, here, lanes], apart], axis=1)
                values = jnp.concatenate(
                    [mixed[2, here, lanes], jnp.ones((length, LANES), BF16)], axis=1
                )
                sides = []
                for part in (0, 1):
                    wide = jnp.concatenate([query * scaled[part], qfeat[here]], axis=1)
                    scores = nt(wide, keys)
                    raised = jnp.exp(scores - jnp.max(scores, axis=1, keepdims=True)).astype(BF16)
                    probs[r * heads + 2 * pair + part] = raised
                    sides.append(nn(raised, values))
                total = jnp.where(first_head, sides[0][:, LANES:], sides[1][:, LANES:])
                mean = jnp.where(first_head, sides[0][:, :LANES], sides[1][:, :LANES])
                inv = 1.0 / total
                context[here, lanes] = (mean * inv).astype(BF16)
                inverse[here, lanes] = inv.astype(BF16)

        def wide_valid(r):
            return 1.0 - qfeat[pl.ds(r * length, length)].astype(F32)[:, 0:1]

        def normalize(value):
            center = value - jnp.mean(value, axis=1, keepdims=True)
            spread = jnp.mean(center * center, axis=1, keepdims=True)
            scale = lax.rsqrt(spread + EPSILON)
            return center * scale, scale

        def normalize_back(up, gain, vhat, scale):
            a = up * gain
            return (
                a
                - jnp.mean(a, axis=1, keepdims=True)
                - vhat * jnp.mean(a * vhat, axis=1, keepdims=True)
            ) * scale

        def first_half(r):
            here = pl.ds(r * length, length)
            attended = nn(context[here], outw[...]) + vrow(V_OUT)
            inputs = x[here].astype(F32)
            real = wide_valid(r)
            add(sums_at + S_INPUT, real * inputs * inputs)
            add(sums_at + S_ATTENDED, real * attended * attended)
            vhat, scale = normalize(inputs + attended)
            vhat1[here] = vhat
            rstd1[here] = jnp.broadcast_to(scale, (length, LANES))
            low1[here] = (vhat * vrow(V_GAIN1) + vrow(V_SHIFT1)).astype(BF16)

        def expand(r):
            here = pl.ds(r * length, length)

            for c in range(blocks):
                upper = nt(low1[here], expw[c]) + vrow(V_EXPAND + c)
                value, derivative = gelu_parts(upper)
                active[c, here] = value.astype(BF16)
                slope[c, here] = derivative.astype(BF16)

        def second_half(r):
            here = pl.ds(r * length, length)
            shrunk = nn(active[0, here], shrw[0])
            for c in range(1, blocks):
                shrunk = shrunk + nn(active[c, here], shrw[c])
            shrunk = shrunk + vrow(V_SHRINK)
            add(sums_at + S_SHRUNK, wide_valid(r) * shrunk * shrunk)
            hidden = vhat1[here] * vrow(V_GAIN1) + vrow(V_SHIFT1)
            vhat, scale = normalize(hidden + shrunk)
            there = pl.ds(shown_at + r * length, length)
            grads[there] = (vhat * vrow(V_GAIN2) + vrow(V_SHIFT2)).astype(BF16)
            up = cot[here].astype(F32)
            add(V_GAIN2, up * vhat)
            add(V_SHIFT2, up)
            grad = normalize_back(up, vrow(V_GAIN2), vhat, scale)
            second[here] = grad
            low = grad.astype(BF16)
            shrunk_low[here] = low
            add(V_SHRINK, low.astype(F32))

        ones = jnp.ones((8, own_tokens), BF16)

        def upper_back(c, r):
            here = pl.ds(r * length, length)
            grad = nt(shrunk_low[here], shrw[c])
            slope[c, here] = (grad * slope[c, here].astype(F32)).astype(BF16)

        def expand_back(c):
            upper_back(c, rows - 1)
            base = 2 * width * c
            grads[base : base + width] = tn(slope[c], low1[...]).astype(BF16)
            done(2 * c)

        def shrink_back(c):
            base = 2 * width * c + width
            grads[base : base + width] = tn(active[c], shrunk_low[...]).astype(BF16)
            done(2 * c + 1)
            sums[V_EXPAND + c : V_EXPAND + c + 1, :] = nn(ones, slope[c])[0:1]

        def first_half_back(r):
            here = pl.ds(r * length, length)
            up = second[here]
            for c in range(blocks):
                up = up + nn(slope[c, here], expw[c])
            vhat = vhat1[here]
            add(V_GAIN1, up * vhat)
            add(V_SHIFT1, up)
            grad = normalize_back(up, vrow(V_GAIN1), vhat, rstd1[here][:, 0:1])
            second[here] = grad
            low = grad.astype(BF16)
            attended_low[here] = low
            add(V_OUT, low.astype(F32))
            context_grad[here] = nt(low, outw[...]).astype(BF16)

        def attend_back(r, pair):
            here = pl.ds(r * length, length)
            lanes = pl.ds(pair * LANES, LANES)
            query, keys, values = (mixed[j, here, lanes] for j in range(3))
            up = context_grad[here, lanes].astype(F32) * inverse[here, lanes].astype(F32)
            up = up.astype(BF16)
            inner = up.astype(F32) * context[here, lanes].astype(F32)
            sides = []
            for part in (0, 1):
                raised = probs[r * heads + 2 * pair + part]
                mine = first_head if part == 0 else jnp.logical_not(first_head)
                delta = jnp.sum(jnp.where(mine, inner, 0.0), axis=1, keepdims=True)
                dprobs = nt(up * masks[part], values)
                score = (raised.astype(F32) * (dprobs - delta)).astype(BF16)
                sides.append((nn(score, keys), tn(score, query), tn(raised, up)))
            for j, factor in enumerate((SCALE, SCALE, 1.0)):
                both = jnp.where(first_head, sides[0][j], sides[1][j])
                mixed[j, here, lanes] = (both * factor).astype(BF16)

        def tokens_back(r):
            here = pl.ds(r * length, length)
            grad = second[here]
            for j in range(3):
                grad = grad + nt(mixed[j, here], proj[j])
            low1[here] = grad.astype(BF16)

        def out_back():
            base = 2 * blocks * width
            grads[base : base + width] = tn(context[...], attended_low[...]).astype(BF16)
            done(2 * blocks)

        def mix_back(j):
            if j == 0:
                for copies in results:
                    for copy in copies:
                        copy.wait_send()
                        shown.append(copy)
                while kept:
                    kept.pop().wait()
            base = (2 * blocks + 1 + j) * width
            grads[base : base + width] = tn(x[...], mixed[j]).astype(BF16)
            done(2 * blocks + 1 + j)

        def sums_back():
            for row, j in ((V_QUERY, 0), (V_VALUE, 2)):
                sums[row : row + 1, :] = nn(ones, mixed[j])[0:1]
            begin(n_chunks)

        returned, shown = [], []

        def give_back(r):
            tokens_back(r)
            returned.append(deliver(low1, tgrad_in, r))

        for r in range(rows):
            arrive(incoming[r])
            mix(r)
            attend(r)
            first_half(r)
            expand(r)
        results = []
        for r in range(rows):
            arrive(cotangents[r])
            second_half(r)
            if r + 1 < rows:
                for c in range(blocks):
                    upper_back(c, r)
        for copy in sent:
            copy.wait_send()

        def show(r):
            results.append(deliver(grads.at[pl.ds(shown_at, own_tokens)], result_in, r))

        units = []
        for c in range(blocks):
            units += [lambda c=c: expand_back(c), lambda c=c: shrink_back(c)]
        units += [lambda r=r: first_half_back(r) for r in range(rows)]
        units.append(out_back)
        for r in range(rows):
            units += [lambda r=r, pair=pair: attend_back(r, pair) for pair in range(pairs)]
        units += [lambda j=j: mix_back(j) for j in range(3)]
        units.append(sums_back)
        units += [lambda r=r: give_back(r) for r in range(rows)]
        late = {SHOW: lambda: [show(r) for r in range(rows)]}
        for index in PLAN:
            if index == UNIT:
                if units:
                    units.pop(0)()
            elif index in late:
                late.pop(index)()
            else:
                advance(index)
        for unit in list(late.values()) + units:
            unit()
        while running:
            for index in list(running):
                advance(index)
        for copies in results + returned:
            arrive(copies)
        for copy in started[len(sent) :]:
            if all(copy is not other for other in shown):
                copy.wait_send()
        for copy in kept:
            copy.wait()

    hbm = pl.BlockSpec(memory_space=pl.ANY)
    vmem = pl.BlockSpec(memory_space=pltpu.VMEM)
    big = (own_tokens, width)
    result, tokens_grad, low_grads, sums = pl.pallas_call(
        kernel,
        out_shape=(
            jax.ShapeDtypeStruct((group, span, width), BF16),
            jax.ShapeDtypeStruct((group, span, width), BF16),
            jax.ShapeDtypeStruct((grad_rows, width), BF16),
            jax.ShapeDtypeStruct((sum_rows, width), F32),
        ),
        in_specs=[hbm, hbm, vmem, hbm, hbm, hbm, hbm, *([vmem] * 8)],
        out_specs=(hbm, hbm, hbm, vmem),
        scratch_shapes=[
            pltpu.VMEM((span, group, width), BF16),
            pltpu.VMEM((sum_rows, width), F32),
            pltpu.VMEM(big, BF16),
            pltpu.VMEM(big, BF16),
            pltpu.VMEM((3, width, width), BF16),
            pltpu.VMEM((width, width), BF16),
            pltpu.VMEM((blocks, width, width), BF16),
            pltpu.VMEM((blocks, width, width), BF16),
            pltpu.VMEM((3, *big), BF16),
            pltpu.VMEM((rows * heads, length, length), BF16),
            pltpu.VMEM(big, BF16),
            pltpu.VMEM(big, BF16),
            pltpu.VMEM(big, F32),
            pltpu.VMEM((own_tokens, LANES), F32),
            pltpu.VMEM(big, BF16),
            pltpu.VMEM((blocks, *big), BF16),
            pltpu.VMEM((blocks, *big), BF16),
            pltpu.VMEM(big, F32),
            pltpu.VMEM(big, BF16),
            pltpu.VMEM((own_tokens, LANES), BF16),
            pltpu.VMEM((grad_rows, width), BF16),
            pltpu.VMEM((slot_rows, width), BF16),
            pltpu.VMEM((sum_rows, width), F32),
            pltpu.VMEM((sum(size for _, _, size in levels.values()), sum_rows, width), F32),
            pltpu.SemaphoreType.DMA((n_remote,)),
            pltpu.SemaphoreType.DMA((n_remote,)),
            pltpu.SemaphoreType.DMA((n_local,)),
        ],
        compiler_params=pltpu.CompilerParams(
            collective_id=0, has_side_effects=True, vmem_limit_bytes=63 * 2**20
        ),
    )(
        tokens,
        cotangent,
        jnp.transpose(segments),
        jnp.transpose(projections, (1, 0, 2)),
        outweight,
        expander.reshape(blocks, width, width),
        shrinker.reshape(blocks, width, width),
        projbias,
        outbias,
        normgain,
        normshift,
        expandbias,
        shrinkbias,
        finalgain,
        finalshift,
    )
    def finish(
        result_in,
        tgrad_in,
        low_grads,
        totals,
        result_out,
        tgrad_out,
        proj_out,
        bias_out,
        out_out,
        out_bias_out,
        gain1_out,
        shift1_out,
        exp_out,
        exp_bias_out,
        shr_out,
        shr_bias_out,
        gain2_out,
        shift2_out,
        rms_out,
        turned_in,
        turned,
        low,
        full,
        in_sem,
        out_sem,
    ):
        places = []
        for c in range(blocks):
            here = pl.ds(c * width, width)
            places += [exp_out.at[here], shr_out.at[here]]
        places.append(out_out)
        places += [proj_out.at[j] for j in range(3)]
        loads = []
        for i in range(n_blocks):
            src = low_grads.at[pl.ds(i * width, width)]
            loads.append(pltpu.make_async_copy(src, low.at[i], in_sem.at[i]))
        for i, src in enumerate((result_in, tgrad_in)):
            loads.append(pltpu.make_async_copy(src, turned_in.at[i], in_sem.at[n_blocks + i]))
        for load in loads:
            load.start()
        bias_out[...] = totals[V_QUERY : V_VALUE + 1]
        for row, out in (
            (V_OUT, out_bias_out),
            (V_GAIN1, gain1_out),
            (V_SHIFT1, shift1_out),
            (V_SHRINK, shr_bias_out),
            (V_GAIN2, gain2_out),
            (V_SHIFT2, shift2_out),
        ):
            out[...] = totals[row]
        exp_bias_out[...] = totals[V_EXPAND : V_EXPAND + blocks].reshape(hidden_units)
        squares = jnp.sum(totals[sums_at : sums_at + 4], axis=1, keepdims=True)
        count = totals[sums_at + S_COUNT : sums_at + S_COUNT + 1, 0:1] * width
        roots = jnp.sqrt(squares / count)
        lane = lax.broadcasted_iota(jnp.int32, (4, LANES), 1)
        row = lax.broadcasted_iota(jnp.int32, (4, LANES), 0)
        line = jnp.sum(jnp.where(lane == row, roots, 0.0), axis=0)
        rms_out[...] = line[0:3]
        stores = []
        for i, dst in enumerate(places):
            loads[i].wait()
            full[i] = low[i].astype(F32)
            stores.append(pltpu.make_async_copy(full.at[i], dst, out_sem.at[i]))
            stores[-1].start()
        for i, dst in enumerate((result_out, tgrad_out)):
            loads[n_blocks + i].wait()
            turned[i] = jnp.swapaxes(turned_in[i], 0, 1)
            stores.append(pltpu.make_async_copy(turned.at[i], dst, out_sem.at[n_blocks + i]))
            stores[-1].start()
        for store in stores:
            store.wait()

    vector = jax.ShapeDtypeStruct((width,), F32)
    square = (n_blocks, width, width)
    outs = pl.pallas_call(
        finish,
        out_shape=(
            jax.ShapeDtypeStruct((span, group, width), BF16),
            jax.ShapeDtypeStruct((span, group, width), BF16),
            jax.ShapeDtypeStruct((3, width, width), F32),
            jax.ShapeDtypeStruct((2, width), F32),
            jax.ShapeDtypeStruct((width, width), F32),
            vector,
            vector,
            vector,
            jax.ShapeDtypeStruct((hidden_units, width), F32),
            jax.ShapeDtypeStruct((hidden_units,), F32),
            jax.ShapeDtypeStruct((hidden_units, width), F32),
            vector,
            vector,
            vector,
            jax.ShapeDtypeStruct((3,), F32),
        ),
        in_specs=[hbm, hbm, hbm, vmem],
        out_specs=(hbm, hbm, hbm, vmem, hbm, vmem, vmem, vmem, hbm, vmem, hbm, *([vmem] * 4)),
        scratch_shapes=[
            pltpu.VMEM((2, group, span, width), BF16),
            pltpu.VMEM((2, span, group, width), BF16),
            pltpu.VMEM(square, BF16),
            pltpu.VMEM(square, F32),
            pltpu.SemaphoreType.DMA((n_blocks + 2,)),
            pltpu.SemaphoreType.DMA((n_blocks + 2,)),
        ],
        compiler_params=pltpu.CompilerParams(vmem_limit_bytes=62 * 2**20),
    )(result, tokens_grad, low_grads, sums)
    outs = list(outs)
    outs[2] = jnp.transpose(outs[2], (1, 0, 2))
    return tuple(outs)


def solution(mesh):
    split = P("seq", "dp", None)
    placed = (split, P(None, "dp"), *([P()] * 12), split)
    return jax.shard_map(
        local,
        mesh=mesh,
        in_specs=placed,
        out_specs=(split, split, *([P()] * 13)),
        check_vma=False,
    )
```

```python
import jax
import jax.numpy as jnp
from jax import lax
from jax.experimental import pallas as pl
from jax.experimental.pallas import tpu as pltpu
from jax.sharding import PartitionSpec as P

HEAD_DIM = 64
EPSILON = 1e-12
LANES = 128
F32 = jnp.float32
BF16 = jnp.bfloat16
SCALE = HEAD_DIM ** (-0.5)

(V_QUERY, V_VALUE, V_OUT, V_GAIN1, V_SHIFT1, V_SHRINK, V_GAIN2, V_SHIFT2, V_EXPAND) = range(9)
(S_INPUT, S_ATTENDED, S_SHRUNK, S_COUNT) = range(4)


ORDERS = (
    ("core", "side", "near", "far"),
    ("core", "near", "side", "far"),
    ("core", "far", "near", "side"),
    ("core", "near", "far", "side"),
)
CLASSES = (1, 2, 1, 0, 3, 0, 1, 1)
UNIT, SHOW = -1, -2
MERGED = (2, 2, 2, 2, 1, 1, 1, 1)
PLAN = (
    SHOW, UNIT, UNIT, UNIT, UNIT, UNIT, UNIT, 0, UNIT, 1, UNIT, UNIT, 2, UNIT, UNIT, UNIT, 0,
    3, UNIT, 4, UNIT, UNIT, 0, UNIT, UNIT, 4, 2, UNIT, 3, 0, UNIT, UNIT, UNIT, 2, UNIT, 1, 5,
    3, 6, 4, 0, 2, 7, UNIT, 1, 5, 4, 3, 6, 0, 2, 8, 4, 7, 1, 5, 6, UNIT, 3, 7, 1, 5, 6, 4, 3,
    7, 5, 1, 2, 6, 7, 5, 8, 4, 3, 6, UNIT, 8, 0, 7, 2, 5, 0, 4, 6, 8, 1, 7, 5, 3, 2, 6, 1, 7,
)


def nn(a, b):
    return lax.dot_general(a, b, (((1,), (0,)), ((), ())), preferred_element_type=F32)


def nt(a, b):
    return lax.dot_general(a, b, (((1,), (1,)), ((), ())), preferred_element_type=F32)


def tn(a, b):
    return lax.dot_general(a, b, (((0,), (0,)), ((), ())), preferred_element_type=F32)


def gelu_parts(u):
    phi = 0.5 + 0.5 * lax.erf(u * 0.5**0.5)
    density = jnp.exp2((u * (-0.5 * 1.4426950408889634)) * u)
    return u * phi, phi + (0.3989422804014327 * u) * density


def levels_of(n_seq, n_dp):
    low = 2 if n_seq % 2 == 0 else 1
    near = 1
    while 4 * near * near <= n_dp and n_dp % (2 * near) == 0:
        near *= 2
    return {
        "core": ("seq", 1, low),
        "side": ("seq", low, n_seq // low),
        "near": ("dp", 1, near),
        "far": ("dp", near, n_dp // near),
    }


def slots_of(levels, order, rows):
    total = 0
    for name in order:
        size = levels[name][2]
        if size == 1:
            continue
        if rows % (16 * size) == 0:
            rows //= size
            total += (size - 1) * rows
        else:
            total += size * rows
    return total


def local(
    tokens,
    segments,
    projections,
    projbias,
    outweight,
    outbias,
    normgain,
    normshift,
    expander,
    expandbias,
    shrinker,
    shrinkbias,
    finalgain,
    finalshift,
    cotangent,
):
    n_seq, n_dp = lax.axis_size("seq"), lax.axis_size("dp")
    span, group, width = tokens.shape
    length = segments.shape[0]
    rows = group // n_seq
    hidden_units = expander.shape[0]
    blocks = hidden_units // width
    heads = width // HEAD_DIM
    pairs = width // LANES
    own_tokens = rows * length
    levels = levels_of(n_seq, n_dp)
    n_blocks = 2 * blocks + 4
    chunks, taken = [], 0
    while taken < n_blocks:
        count = min(MERGED[len(chunks)] if len(chunks) < len(MERGED) else 1, n_blocks - taken)
        chunks.append((taken, count))
        taken += count
    n_chunks = len(chunks)
    chunk_orders = []
    for index, (_, count) in enumerate(chunks):
        choices = (ORDERS[CLASSES[index % len(CLASSES)]], ORDERS[0])
        chunk_orders.append(min(choices, key=lambda order: slots_of(levels, order, count * width)))
    slot_bases, slot_rows = [], 0
    for order, (_, count) in zip(chunk_orders, chunks):
        slot_bases.append(slot_rows)
        slot_rows += slots_of(levels, order, count * width)
    grad_rows = n_blocks * width
    vec_rows = V_EXPAND + blocks
    sum_rows = -(-(vec_rows + 4) // 8) * 8
    sums_at = vec_rows
    ring = sum(size - 1 for _, _, size in levels.values())
    n_remote = 4 * rows * (n_seq - 1) + n_chunks * 2 * ring + ring
    n_local = 8 + 4 * rows + n_chunks

    def kernel(
        tok_hbm,
        cot_hbm,
        labels,
        proj_hbm,
        out_hbm,
        exp_hbm,
        shr_hbm,
        bias,
        out_bias,
        gain1,
        shift1,
        exp_bias,
        shr_bias,
        gain2,
        shift2,
        result_in,
        tgrad_in,
        low_grads,
        sums_out,
        raw,
        vec,
        x,
        cot,
        proj,
        outw,
        expw,
        shrw,
        mixed,
        probs,
        context,
        inverse,
        vhat1,
        rstd1,
        low1,
        active,
        slope,
        second,
        shrunk_low,
        qfeat,
        grads,
        slots,
        sums,
        sum_slots,
        send_sem,
        recv_sem,
        local_sem,
    ):
        me = lax.axis_index("seq")
        attended_low, context_grad = shrunk_low, cot
        shown_at = (n_blocks - 3) * width
        started, counters = [], {"remote": 0, "local": 0}

        def remote(src, dst, where):
            i = counters["remote"]
            counters["remote"] += 1
            copy = pltpu.make_async_remote_copy(
                src_ref=src,
                dst_ref=dst,
                send_sem=send_sem.at[i],
                recv_sem=recv_sem.at[i],
                device_id=where,
                device_id_type=pl.DeviceIdType.MESH,
            )
            copy.start()
            started.append(copy)
            return copy

        def near_copy(src, dst):
            i = counters["local"]
            counters["local"] += 1
            copy = pltpu.make_async_copy(src, dst, local_sem.at[i])
            copy.start()
            return copy

        def place(name):
            axis, stride, size = levels[name]
            index = lax.axis_index(axis)
            mine = lax.rem(lax.div(index, stride), size)
            return axis, index, stride, size, mine

        arriving = [near_copy(tok_hbm, raw)]

        barrier = pltpu.get_barrier_semaphore()
        greeted = 0
        for j in range(1, n_seq):
            pl.semaphore_signal(
                barrier,
                inc=1,
                device_id={"seq": lax.rem(me + j, n_seq)},
                device_id_type=pl.DeviceIdType.MESH,
            )
            greeted += 1
        for name in ("near", "far"):
            axis, index, stride, size, mine = place(name)
            for j in range(1, size):
                k = lax.rem(mine + j, size)
                pl.semaphore_signal(
                    barrier,
                    inc=1,
                    device_id={axis: index + (k - mine) * stride},
                    device_id_type=pl.DeviceIdType.MESH,
                )
                greeted += 1

        def bring(base, dst, r):
            here = pl.ds(pl.multiple_of(r * length + me * span, 16), span)
            far = []
            for j in sorted(range(1, n_seq), key=lambda j: j % 2):
                k = lax.rem(me + j, n_seq)
                src = grads.at[pl.ds(pl.multiple_of(base + (k * rows + r) * span, 16), span)]
                far.append(remote(src, dst.at[here], {"seq": k}))
            own = pl.ds(pl.multiple_of(base + (me * rows + r) * span, 16), span)
            dst[here] = grads[own]
            return far

        def deliver(src, dst, r):
            far = []
            for j in sorted(range(1, n_seq), key=lambda j: j % 2):
                k = lax.rem(me + j, n_seq)
                piece = src.at[pl.ds(pl.multiple_of(r * length + k * span, 16), span)]
                far.append(remote(piece, dst.at[me * rows + r], {"seq": k}))
            own = pl.ds(pl.multiple_of(r * length + me * span, 16), span)
            kept.append(near_copy(src.at[own], dst.at[me * rows + r]))
            return far

        kept = []

        def arrive(copies):
            for copy in copies:
                copy.wait_recv()

        def spread(index, base):
            arriving[index].wait()
            turned = jnp.swapaxes(raw[...], 0, 1)
            grads[base : base + group * span] = turned.reshape(group * span, width)

        def reduce_chunk(index):
            base, count = chunks[index][0] * width, chunks[index][1] * width
            written = []
            at, slot, stack = base, slot_bases[index], []
            for name in chunk_orders[index]:
                axis, own, stride, size, mine = place(name)
                if size == 1:
                    continue
                copies = []
                if count % (16 * size) == 0:
                    piece = count // size
                    for j in range(1, size):
                        k = lax.rem(mine + j, size)
                        copies.append(
                            remote(
                                grads.at[pl.ds(pl.multiple_of(at + k * piece, 16), piece)],
                                slots.at[pl.ds(slot + (j - 1) * piece, piece)],
                                {axis: own + (k - mine) * stride},
                            )
                        )
                    yield
                    here = pl.multiple_of(at + mine * piece, 16)
                    for copy in copies:
                        copy.wait_recv()
                    total = grads[pl.ds(here, piece)].astype(F32)
                    for j in range(size - 1):
                        total = total + slots[pl.ds(slot + j * piece, piece)].astype(F32)
                    grads[pl.ds(here, piece)] = total.astype(BF16)
                    stack.append((name, at, piece))
                    slot += (size - 1) * piece
                    at, count = here, piece
                else:
                    mine_slot = pl.ds(pl.multiple_of(slot + mine * count, 16), count)
                    slots[mine_slot] = grads[pl.ds(at, count)]
                    for j in range(1, size):
                        k = lax.rem(mine + j, size)
                        copies.append(
                            remote(
                                slots.at[mine_slot],
                                slots.at[mine_slot],
                                {axis: own + (k - mine) * stride},
                            )
                        )
                    yield
                    for copy in copies:
                        copy.wait_recv()
                    total = jnp.zeros((count, width), F32)
                    for j in range(size):
                        total = total + slots[pl.ds(slot + j * count, count)].astype(F32)
                    grads[pl.ds(at, count)] = total.astype(BF16)
                    slot += size * count
            block, copies = grads.at[pl.ds(at, count)], []
            written.append(near_copy(block, low_grads.at[pl.ds(pl.multiple_of(at, 16), count)]))
            for name, before, piece in reversed(stack):
                axis, own, stride, size, mine = place(name)
                target = low_grads.at[pl.ds(pl.multiple_of(at, 16), piece)]
                copies = []
                for j in range(1, size):
                    k = lax.rem(mine + j, size)
                    copies.append(remote(block, target, {axis: own + (k - mine) * stride}))
                yield
                for copy in copies:
                    copy.wait_recv()
                if written:
                    written.pop().wait()
                count = piece * size
                at, block = before, low_grads.at[pl.ds(pl.multiple_of(before, 16), count)]
            if written:
                written.pop().wait()

        def reduce_sums():
            current = sums
            for step, name in enumerate(("core", "side", "near", "far")):
                axis, own, stride, size, mine = place(name)
                if size == 1:
                    continue
                first = sum(levels[n][2] for n in ("core", "side", "near", "far")[:step])
                sum_slots[first + mine] = current[...]
                copies = []
                for j in range(1, size):
                    k = lax.rem(mine + j, size)
                    block = sum_slots.at[first + mine]
                    copies.append(remote(block, block, {axis: own + (k - mine) * stride}))
                yield
                for copy in copies:
                    copy.wait_recv()
                total = sum_slots[first]
                for j in range(1, size):
                    total = total + sum_slots[first + j]
                current[...] = total
            sums_out[...] = current[...]

        running = {}

        def advance(index):
            if index in running and next(running[index], "end") == "end":
                del running[index]

        def begin(index):
            running[index] = reduce_chunk(index) if index < n_chunks else reduce_sums()
            next(running[index])

        def done(block):
            for index, (first, count) in enumerate(chunks):
                if first + count - 1 == block:
                    begin(index)

        def add(row, value):
            sums[row : row + 1, :] += jnp.sum(value, axis=0, keepdims=True)

        def vrow(i):
            return vec[i : i + 1, :]

        def features(r):
            here = pl.ds(r * length, length)
            label = labels[pl.ds(me * rows + r, 1), :]
            ids = lax.broadcasted_iota(jnp.int32, (LANES, length), 0)
            hot = jnp.where(ids == label, 1.0, 0.0)
            hot = jnp.transpose(hot)
            qfeat[here] = hot.astype(BF16)
            real = 1.0 - hot[:, 0:1]
            sums[sums_at + S_COUNT : sums_at + S_COUNT + 1, 0:LANES] += jnp.sum(
                jnp.broadcast_to(real, (length, LANES)), axis=0, keepdims=True
            )

        vec[0:2] = bias[...].astype(F32)
        for row, vector in enumerate((out_bias, gain1, shift1, shr_bias, gain2, shift2)):
            vec[2 + row : 3 + row] = vector[...].astype(F32).reshape(1, width)
        vec[V_EXPAND:vec_rows] = exp_bias[...].astype(F32).reshape(blocks, width)
        spread(0, 0)
        arriving.append(near_copy(cot_hbm, raw))
        weights = [
            near_copy(proj_hbm, proj),
            near_copy(out_hbm, outw),
            near_copy(exp_hbm, expw),
            near_copy(shr_hbm, shrw),
        ]
        pl.semaphore_wait(barrier, greeted)
        incoming = [bring(0, x, r) for r in range(rows)]
        spread(1, group * span)
        cotangents = [bring(group * span, cot, r) for r in range(rows)]
        sent = list(started)
        sums[...] = jnp.zeros_like(sums)
        for r in range(rows):
            features(r)
        for copy in weights:
            copy.wait()

        lane = lax.broadcasted_iota(jnp.int32, (length, LANES), 1)
        first_head = lane < HEAD_DIM
        lane_row = lax.broadcasted_iota(jnp.int32, (1, LANES), 1)
        masks = [
            jnp.where(lane_row // HEAD_DIM == part, 1.0, 0.0).astype(BF16) for part in (0, 1)
        ]
        scaled = [mask * BF16(SCALE) for mask in masks]

        def mix(r):
            here = pl.ds(r * length, length)
            block = x[here]
            mixed[0, here] = (nn(block, proj[0]) + vrow(V_QUERY)).astype(BF16)
            mixed[1, here] = nn(block, proj[1]).astype(BF16)
            mixed[2, here] = (nn(block, proj[2]) + vrow(V_VALUE)).astype(BF16)

        def attend(r):
            here = pl.ds(r * length, length)

            apart = ((qfeat[here].astype(F32) - 1.0) * 1e30).astype(BF16)
            for pair in range(pairs):
                lanes = pl.ds(pair * LANES, LANES)
                query = mixed[0, here, lanes]
                keys = jnp.concatenate([mixed[1, here, lanes], apart], axis=1)
                values = jnp.concatenate(
                    [mixed[2, here, lanes], jnp.ones((length, LANES), BF16)], axis=1
                )
                sides = []
                for part in (0, 1):
                    wide = jnp.concatenate([query * scaled[part], qfeat[here]], axis=1)
                    scores = nt(wide, keys)
                    raised = jnp.exp(scores - jnp.max(scores, axis=1, keepdims=True)).astype(BF16)
                    probs[r * heads + 2 * pair + part] = raised
                    sides.append(nn(raised, values))
                total = jnp.where(first_head, sides[0][:, LANES:], sides[1][:, LANES:])
                mean = jnp.where(first_head, sides[0][:, :LANES], sides[1][:, :LANES])
                inv = 1.0 / total
                context[here, lanes] = (mean * inv).astype(BF16)
                inverse[here, lanes] = inv.astype(BF16)

        def wide_valid(r):
            return 1.0 - qfeat[pl.ds(r * length, length)].astype(F32)[:, 0:1]

        def normalize(value):
            center = value - jnp.mean(value, axis=1, keepdims=True)
            spread = jnp.mean(center * center, axis=1, keepdims=True)
            scale = lax.rsqrt(spread + EPSILON)
            return center * scale, scale

        def normalize_back(up, gain, vhat, scale):
            a = up * gain
            return (
                a
                - jnp.mean(a, axis=1, keepdims=True)
                - vhat * jnp.mean(a * vhat, axis=1, keepdims=True)
            ) * scale

        def first_half(r):
            here = pl.ds(r * length, length)
            attended = nn(context[here], outw[...]) + vrow(V_OUT)
            inputs = x[here].astype(F32)
            real = wide_valid(r)
            add(sums_at + S_INPUT, real * inputs * inputs)
            add(sums_at + S_ATTENDED, real * attended * attended)
            vhat, scale = normalize(inputs + attended)
            vhat1[here] = vhat
            rstd1[here] = jnp.broadcast_to(scale, (length, LANES))
            low1[here] = (vhat * vrow(V_GAIN1) + vrow(V_SHIFT1)).astype(BF16)

        def expand(r):
            here = pl.ds(r * length, length)

            for c in range(blocks):
                upper = nt(low1[here], expw[c]) + vrow(V_EXPAND + c)
                value, derivative = gelu_parts(upper)
                active[c, here] = value.astype(BF16)
                slope[c, here] = derivative.astype(BF16)

        def second_half(r):
            here = pl.ds(r * length, length)
            shrunk = nn(active[0, here], shrw[0])
            for c in range(1, blocks):
                shrunk = shrunk + nn(active[c, here], shrw[c])
            shrunk = shrunk + vrow(V_SHRINK)
            add(sums_at + S_SHRUNK, wide_valid(r) * shrunk * shrunk)
            hidden = vhat1[here] * vrow(V_GAIN1) + vrow(V_SHIFT1)
            vhat, scale = normalize(hidden + shrunk)
            there = pl.ds(shown_at + r * length, length)
            grads[there] = (vhat * vrow(V_GAIN2) + vrow(V_SHIFT2)).astype(BF16)
            up = cot[here].astype(F32)
            add(V_GAIN2, up * vhat)
            add(V_SHIFT2, up)
            grad = normalize_back(up, vrow(V_GAIN2), vhat, scale)
            second[here] = grad
            low = grad.astype(BF16)
            shrunk_low[here] = low
            add(V_SHRINK, low.astype(F32))

        ones = jnp.ones((8, own_tokens), BF16)

        def upper_back(c, r):
            here = pl.ds(r * length, length)
            grad = nt(shrunk_low[here], shrw[c])
            slope[c, here] = (grad * slope[c, here].astype(F32)).astype(BF16)

        def expand_back(c):
            upper_back(c, rows - 1)
            base = 2 * width * c
            grads[base : base + width] = tn(slope[c], low1[...]).astype(BF16)
            done(2 * c)

        def shrink_back(c):
            base = 2 * width * c + width
            grads[base : base + width] = tn(active[c], shrunk_low[...]).astype(BF16)
            done(2 * c + 1)
            sums[V_EXPAND + c : V_EXPAND + c + 1, :] = nn(ones, slope[c])[0:1]

        def first_half_back(r):
            here = pl.ds(r * length, length)
            up = second[here]
            for c in range(blocks):
                up = up + nn(slope[c, here], expw[c])
            vhat = vhat1[here]
            add(V_GAIN1, up * vhat)
            add(V_SHIFT1, up)
            grad = normalize_back(up, vrow(V_GAIN1), vhat, rstd1[here][:, 0:1])
            second[here] = grad
            low = grad.astype(BF16)
            attended_low[here] = low
            add(V_OUT, low.astype(F32))
            context_grad[here] = nt(low, outw[...]).astype(BF16)

        def attend_back(r, pair):
            here = pl.ds(r * length, length)
            lanes = pl.ds(pair * LANES, LANES)
            query, keys, values = (mixed[j, here, lanes] for j in range(3))
            up = context_grad[here, lanes].astype(F32) * inverse[here, lanes].astype(F32)
            up = up.astype(BF16)
            inner = up.astype(F32) * context[here, lanes].astype(F32)
            sides = []
            for part in (0, 1):
                raised = probs[r * heads + 2 * pair + part]
                mine = first_head if part == 0 else jnp.logical_not(first_head)
                delta = jnp.sum(jnp.where(mine, inner, 0.0), axis=1, keepdims=True)
                dprobs = nt(up * masks[part], values)
                score = (raised.astype(F32) * (dprobs - delta)).astype(BF16)
                sides.append((nn(score, keys), tn(score, query), tn(raised, up)))
            for j, factor in enumerate((SCALE, SCALE, 1.0)):
                both = jnp.where(first_head, sides[0][j], sides[1][j])
                mixed[j, here, lanes] = (both * factor).astype(BF16)

        def tokens_back(r):
            here = pl.ds(r * length, length)
            grad = second[here]
            for j in range(3):
                grad = grad + nt(mixed[j, here], proj[j])
            low1[here] = grad.astype(BF16)

        def out_back():
            base = 2 * blocks * width
            grads[base : base + width] = tn(context[...], attended_low[...]).astype(BF16)
            done(2 * blocks)

        def mix_back(j):
            if j == 0:
                for copies in results:
                    for copy in copies:
                        copy.wait_send()
                        shown.append(copy)
                while kept:
                    kept.pop().wait()
            base = (2 * blocks + 1 + j) * width
            grads[base : base + width] = tn(x[...], mixed[j]).astype(BF16)
            done(2 * blocks + 1 + j)

        def sums_back():
            for row, j in ((V_QUERY, 0), (V_VALUE, 2)):
                sums[row : row + 1, :] = nn(ones, mixed[j])[0:1]
            begin(n_chunks)

        returned, shown = [], []

        def give_back(r):
            tokens_back(r)
            returned.append(deliver(low1, tgrad_in, r))

        for r in range(rows):
            arrive(incoming[r])
            mix(r)
            attend(r)
            first_half(r)
            expand(r)
        results = []
        for r in range(rows):
            arrive(cotangents[r])
            second_half(r)
            if r + 1 < rows:
                for c in range(blocks):
                    upper_back(c, r)
        for copy in sent:
            copy.wait_send()

        def show(r):
            results.append(deliver(grads.at[pl.ds(shown_at, own_tokens)], result_in, r))

        units = []
        for c in range(blocks):
            units += [lambda c=c: expand_back(c), lambda c=c: shrink_back(c)]
        units += [lambda r=r: first_half_back(r) for r in range(rows)]
        units.append(out_back)
        for r in range(rows):
            units += [lambda r=r, pair=pair: attend_back(r, pair) for pair in range(pairs)]
        units += [lambda j=j: mix_back(j) for j in range(3)]
        units.append(sums_back)
        units += [lambda r=r: give_back(r) for r in range(rows)]
        late = {SHOW: lambda: [show(r) for r in range(rows)]}
        for index in PLAN:
            if index == UNIT:
                if units:
                    units.pop(0)()
            elif index in late:
                late.pop(index)()
            else:
                advance(index)
        for unit in list(late.values()) + units:
            unit()
        while running:
            for index in list(running):
                advance(index)
        for copies in results + returned:
            arrive(copies)
        for copy in started[len(sent) :]:
            if all(copy is not other for other in shown):
                copy.wait_send()
        for copy in kept:
            copy.wait()

    hbm = pl.BlockSpec(memory_space=pl.ANY)
    vmem = pl.BlockSpec(memory_space=pltpu.VMEM)
    big = (own_tokens, width)
    result, tokens_grad, low_grads, sums = pl.pallas_call(
        kernel,
        out_shape=(
            jax.ShapeDtypeStruct((group, span, width), BF16),
            jax.ShapeDtypeStruct((group, span, width), BF16),
            jax.ShapeDtypeStruct((grad_rows, width), BF16),
            jax.ShapeDtypeStruct((sum_rows, width), F32),
        ),
        in_specs=[hbm, hbm, vmem, hbm, hbm, hbm, hbm, *([vmem] * 8)],
        out_specs=(hbm, hbm, hbm, vmem),
        scratch_shapes=[
            pltpu.VMEM((span, group, width), BF16),
            pltpu.VMEM((sum_rows, width), F32),
            pltpu.VMEM(big, BF16),
            pltpu.VMEM(big, BF16),
            pltpu.VMEM((3, width, width), BF16),
            pltpu.VMEM((width, width), BF16),
            pltpu.VMEM((blocks, width, width), BF16),
            pltpu.VMEM((blocks, width, width), BF16),
            pltpu.VMEM((3, *big), BF16),
            pltpu.VMEM((rows * heads, length, length), BF16),
            pltpu.VMEM(big, BF16),
            pltpu.VMEM(big, BF16),
            pltpu.VMEM(big, F32),
            pltpu.VMEM((own_tokens, LANES), F32),
            pltpu.VMEM(big, BF16),
            pltpu.VMEM((blocks, *big), BF16),
            pltpu.VMEM((blocks, *big), BF16),
            pltpu.VMEM(big, F32),
            pltpu.VMEM(big, BF16),
            pltpu.VMEM((own_tokens, LANES), BF16),
            pltpu.VMEM((grad_rows, width), BF16),
            pltpu.VMEM((slot_rows, width), BF16),
            pltpu.VMEM((sum_rows, width), F32),
            pltpu.VMEM((sum(size for _, _, size in levels.values()), sum_rows, width), F32),
            pltpu.SemaphoreType.DMA((n_remote,)),
            pltpu.SemaphoreType.DMA((n_remote,)),
            pltpu.SemaphoreType.DMA((n_local,)),
        ],
        compiler_params=pltpu.CompilerParams(
            collective_id=0, has_side_effects=True, vmem_limit_bytes=63 * 2**20
        ),
    )(
        tokens,
        cotangent,
        jnp.transpose(segments),
        jnp.transpose(projections, (1, 0, 2)),
        outweight,
        expander.reshape(blocks, width, width),
        shrinker.reshape(blocks, width, width),
        projbias,
        outbias,
        normgain,
        normshift,
        expandbias,
        shrinkbias,
        finalgain,
        finalshift,
    )
    def finish(
        result_in,
        tgrad_in,
        low_grads,
        totals,
        result_out,
        tgrad_out,
        proj_out,
        bias_out,
        out_out,
        out_bias_out,
        gain1_out,
        shift1_out,
        exp_out,
        exp_bias_out,
        shr_out,
        shr_bias_out,
        gain2_out,
        shift2_out,
        rms_out,
        turned_in,
        turned,
        low,
        full,
        in_sem,
        out_sem,
    ):
        places = []
        for c in range(blocks):
            here = pl.ds(c * width, width)
            places += [exp_out.at[here], shr_out.at[here]]
        places.append(out_out)
        places += [proj_out.at[j] for j in range(3)]
        loads = []
        for i in range(n_blocks):
            src = low_grads.at[pl.ds(i * width, width)]
            loads.append(pltpu.make_async_copy(src, low.at[i], in_sem.at[i]))
        for i, src in enumerate((result_in, tgrad_in)):
            loads.append(pltpu.make_async_copy(src, turned_in.at[i], in_sem.at[n_blocks + i]))
        for load in loads:
            load.start()
        bias_out[...] = totals[V_QUERY : V_VALUE + 1]
        for row, out in (
            (V_OUT, out_bias_out),
            (V_GAIN1, gain1_out),
            (V_SHIFT1, shift1_out),
            (V_SHRINK, shr_bias_out),
            (V_GAIN2, gain2_out),
            (V_SHIFT2, shift2_out),
        ):
            out[...] = totals[row]
        exp_bias_out[...] = totals[V_EXPAND : V_EXPAND + blocks].reshape(hidden_units)
        squares = jnp.sum(totals[sums_at : sums_at + 4], axis=1, keepdims=True)
        count = totals[sums_at + S_COUNT : sums_at + S_COUNT + 1, 0:1] * width
        roots = jnp.sqrt(squares / count)
        lane = lax.broadcasted_iota(jnp.int32, (4, LANES), 1)
        row = lax.broadcasted_iota(jnp.int32, (4, LANES), 0)
        line = jnp.sum(jnp.where(lane == row, roots, 0.0), axis=0)
        rms_out[...] = line[0:3]
        stores = []
        for i, dst in enumerate(places):
            loads[i].wait()
            full[i] = low[i].astype(F32)
            stores.append(pltpu.make_async_copy(full.at[i], dst, out_sem.at[i]))
            stores[-1].start()
        for i, dst in enumerate((result_out, tgrad_out)):
            loads[n_blocks + i].wait()
            turned[i] = jnp.swapaxes(turned_in[i], 0, 1)
            stores.append(pltpu.make_async_copy(turned.at[i], dst, out_sem.at[n_blocks + i]))
            stores[-1].start()
        for store in stores:
            store.wait()

    vector = jax.ShapeDtypeStruct((width,), F32)
    square = (n_blocks, width, width)
    outs = pl.pallas_call(
        finish,
        out_shape=(
            jax.ShapeDtypeStruct((span, group, width), BF16),
            jax.ShapeDtypeStruct((span, group, width), BF16),
            jax.ShapeDtypeStruct((3, width, width), F32),
            jax.ShapeDtypeStruct((2, width), F32),
            jax.ShapeDtypeStruct((width, width), F32),
            vector,
            vector,
            vector,
            jax.ShapeDtypeStruct((hidden_units, width), F32),
            jax.ShapeDtypeStruct((hidden_units,), F32),
            jax.ShapeDtypeStruct((hidden_units, width), F32),
            vector,
            vector,
            vector,
            jax.ShapeDtypeStruct((3,), F32),
        ),
        in_specs=[hbm, hbm, hbm, vmem],
        out_specs=(hbm, hbm, hbm, vmem, hbm, vmem, vmem, vmem, hbm, vmem, hbm, *([vmem] * 4)),
        scratch_shapes=[
            pltpu.VMEM((2, group, span, width), BF16),
            pltpu.VMEM((2, span, group, width), BF16),
            pltpu.VMEM(square, BF16),
            pltpu.VMEM(square, F32),
            pltpu.SemaphoreType.DMA((n_blocks + 2,)),
            pltpu.SemaphoreType.DMA((n_blocks + 2,)),
        ],
        compiler_params=pltpu.CompilerParams(vmem_limit_bytes=62 * 2**20),
    )(result, tokens_grad, low_grads, sums)
    outs = list(outs)
    outs[2] = jnp.transpose(outs[2], (1, 0, 2))
    return tuple(outs)


def solution(mesh):
    split = P("seq", "dp", None)
    placed = (split, P(None, "dp"), *([P()] * 12), split)
    return jax.shard_map(
        local,
        mesh=mesh,
        in_specs=placed,
        out_specs=(split, split, *([P()] * 13)),
        check_vma=False,
    )
```
